32 devices in a mesh: lon: 8 (over z, x), lat: 4 (over y, core).
Axes of the slice: x: 2, y: 2, z: 4, core: 2. Of those that a mesh axis runs over, the one named last changes fastest.
Arguments:
- features: bfloat16 [180, 360, 192], P('lat', 'lon'), may hold values from -6 to 6
- params: float32 [306176], P(('lon', 'lat')), may hold values from -1.5 to 1.5
- langevin_noise: float32 [306176], P(('lon', 'lat')), may hold values from -6 to 6
- upstream: bfloat16 [180, 360, 192], P('lat', 'lon'), may hold values from -6 to 6
Outputs:
- output: bfloat16 [180, 360, 192], P('lat', 'lon')
- field_grad: bfloat16 [180, 360, 192], P('lat', 'lon')
- new_params: float32 [306176], P(('lon', 'lat'))
The draws below stay inside these ranges and needn't reach their ends.
All inputs are finite; a program needn't handle non-finite values.
Results may differ from the reference program's by a relative error of at most 0.0085.
Values may be sent and summed in bfloat16 or wider, within the bound.
No kernel may reach another device: no remote copies, remote signals or barrier semaphores. Data moves between devices by JAX's collectives and lax.ppermute only.
A program may use at most 64 MiB of HBM per device.

```python
import math
import jax
import jax.numpy as jnp
from jax import lax

C = 192
H = 768
KS = 7
LAT_DEV = 45
LON = 360
LAT = 180
NPAR = 306048
PTOT = 306176


def draw_params(key, part):
    subkeys = jax.random.split(key, 3)
    position = jnp.arange(PTOT, dtype=jnp.int32)
    normal_base = jax.random.truncated_normal(subkeys[0], -3.0, 3.0, (PTOT,), jnp.float32)
    uniform_base = jax.random.uniform(subkeys[1], (PTOT,), jnp.float32, -1.0, 1.0)
    chan_scale = jnp.exp(jax.random.uniform(subkeys[2], (C,), jnp.float32, math.log(0.3), math.log(3.0)))
    end_in = C * H
    end_out = 2 * C * H
    end_kernel = end_out + KS * KS * C
    end_cbias = end_kernel + C
    end_gain = end_cbias + C
    end_shift = end_gain + C
    end_bias_in = end_shift + H
    end_bias_out = end_bias_in + C
    end_scale = end_bias_out + C
    channel = jnp.clip(position - end_out, 0, PTOT) % C
    kernel_vals = normal_base * chan_scale[channel] / KS
    values = jnp.where(position < end_scale, 1.0 + 0.5 * uniform_base, 0.02 * normal_base)
    values = jnp.where(position < end_bias_out, 0.5 * uniform_base, values)
    values = jnp.where(position < end_bias_in, 0.5 * uniform_base, values)
    values = jnp.where(position < end_shift, 0.5 * uniform_base, values)
    values = jnp.where(position < end_gain, 1.0 + 0.5 * uniform_base, values)
    values = jnp.where(position < end_cbias, uniform_base, values)
    values = jnp.where(position < end_kernel, kernel_vals, values)
    values = jnp.where(position < end_out, normal_base * H ** (-0.5), values)
    values = jnp.where(position < end_in, normal_base * C ** (-0.5), values)
    return values.astype(jnp.float32)


def block_levels(key, shape, cuts, low, top_value):
    def one(dim, parts):
        draws = jax.random.uniform(jax.random.fold_in(jax.random.fold_in(key, 6), dim), (parts,), jnp.float32, low / len(cuts), top_value / len(cuts))
        return jnp.repeat(jnp.exp(draws), shape[dim] // parts).reshape((-1,) + (1,) * (len(shape) - dim - 1))

    gain = one(*cuts[0])
    for cut in cuts[1:]:
        gain = gain * one(*cut)
    return gain


def normal_values(rng, dims, scale, limit, shards=(), kind=jnp.bfloat16):
    array = jax.random.normal(rng, dims, jnp.float32) * scale
    if len(shards) > 0:
        array = block_levels(rng, dims, shards, -0.22, 0.18) * array
    return jnp.clip(array, min=-limit, max=limit).astype(kind)


def setup_inputs(seed: int = 0) -> dict:
    key_of = jax.random.split(jax.random.key(seed), 5)
    features = normal_values(key_of[0], (LAT, LON, C), 1.0, 6.0, ((0, 4), (1, 8)))
    params = draw_params(jax.random.fold_in(key_of[4], 71), 0)
    langevin_noise = normal_values(key_of[2], (PTOT,), 1.0, 6.0, ((0, 32),), jnp.float32)
    upstream = normal_values(key_of[3], (LAT, LON, C), 1.0, 6.0, ((0, 4), (1, 8)))
    return dict(features=features, params=params, langevin_noise=langevin_noise, upstream=upstream)


EPSILON = 1e-06
STEP_SIZE = 0.003
NOISE_COEF = 0.08

def unpack(weights):
    layouts = [(C, H), (H, C), (KS, KS, C), (C,), (C,), (C,), (H,), (C,), (C,)]
    pieces = []
    offset = 0
    for layout in layouts:
        length = math.prod(layout)
        pieces.append(weights[offset:offset + length].reshape(layout))
        offset = offset + length
    return pieces

def gelu_tanh(values):
    return jax.nn.gelu(values, approximate=True)

def depthwise(padded, kernel, conv_bias, lat_rows, lon_cols):
    summed = jnp.zeros((lat_rows, lon_cols, padded.shape[2]), jnp.float32) + conv_bias
    for row_off in range(KS):
        for col_off in range(KS):
            window = padded[row_off:row_off + lat_rows, col_off:col_off + lon_cols]
            summed = summed + kernel[row_off, col_off] * window.astype(jnp.float32)
    return summed

def transposed(grad_padded, kernel, lat_rows, lon_cols):
    span = KS - 1
    summed = jnp.zeros((lat_rows, lon_cols, grad_padded.shape[2]), jnp.float32)
    for row_off in range(KS):
        for col_off in range(KS):
            window = grad_padded[span - row_off:span - row_off + lat_rows, span - col_off:span - col_off + lon_cols]
            summed = summed + kernel[row_off, col_off] * window.astype(jnp.float32)
    return summed

def kernel_grad(grad_conv, padded, lat_rows, lon_cols):
    sums = []
    for row_off in range(KS):
        for col_off in range(KS):
            window = padded[row_off:row_off + lat_rows, col_off:col_off + lon_cols]
            sums.append(lax.optimization_barrier(jnp.sum(grad_conv.astype(jnp.float32) * window.astype(jnp.float32), axis=(0, 1))))
    return jnp.stack(sums).reshape(KS, KS, -1)

def ref_layer(convolved, features, upstream, unpacked):
    w_in, w_out, kernel, conv_bias, ln_gain, ln_bias, bias_in, bias_out, layer_scale = unpacked
    lat_rows, lon_cols, channels = convolved.shape
    flat_conv = convolved.reshape(-1, channels)
    mean_val = lax.optimization_barrier(jnp.mean(flat_conv, axis=-1, keepdims=True))
    centred = flat_conv - mean_val
    inv_std = lax.rsqrt(lax.optimization_barrier(jnp.mean(centred * centred, axis=-1, keepdims=True)) + EPSILON)
    standard = centred * inv_std
    normed = (standard * ln_gain + ln_bias).astype(jnp.bfloat16)
    pre_act = jnp.dot(normed, w_in, preferred_element_type=jnp.float32) + bias_in
    activated, pullback = jax.vjp(gelu_tanh, pre_act)
    act_rounded = activated.astype(jnp.bfloat16)
    branch = jnp.dot(act_rounded, w_out, preferred_element_type=jnp.float32) + bias_out
    features_f32 = features.reshape(-1, channels).astype(jnp.float32)
    output = (features_f32 + layer_scale * branch).astype(jnp.bfloat16).reshape(lat_rows, lon_cols, channels)
    upstream_f32 = upstream.reshape(-1, channels).astype(jnp.float32)
    grad_branch = (layer_scale * upstream_f32).astype(jnp.bfloat16)
    grad_act = jnp.dot(grad_branch, w_out.T, preferred_element_type=jnp.float32)
    grad_pre = pullback(grad_act)[0].astype(jnp.bfloat16)
    grad_normed = jnp.dot(grad_pre, w_in.T, preferred_element_type=jnp.float32)
    scaled = grad_normed * ln_gain
    grad_conv = ((scaled - lax.optimization_barrier(jnp.mean(scaled, axis=-1, keepdims=True)) - standard * lax.optimization_barrier(jnp.mean(scaled * standard, axis=-1, keepdims=True))) * inv_std).astype(jnp.bfloat16)
    grad_in_proj = jnp.dot(normed.T, grad_pre, preferred_element_type=jnp.float32)
    grad_out_proj = jnp.dot(act_rounded.T, grad_branch, preferred_element_type=jnp.float32)
    grad_gain = lax.optimization_barrier(jnp.sum(grad_normed * standard, axis=0))
    grad_shift = lax.optimization_barrier(jnp.sum(grad_normed, axis=0))
    grad_bias_in = lax.optimization_barrier(jnp.sum(grad_pre.astype(jnp.float32), axis=0))
    grad_bias_out = lax.optimization_barrier(jnp.sum(grad_branch.astype(jnp.float32), axis=0))
    grad_scale = lax.optimization_barrier(jnp.sum(branch * upstream_f32, axis=0))
    layer_grads = (grad_in_proj, grad_out_proj, grad_gain, grad_shift, grad_bias_in, grad_bias_out, grad_scale)
    return (output, grad_conv.reshape(lat_rows, lon_cols, channels), layer_grads)

def reference(features, params, langevin_noise, upstream):
    weights = params.astype(jnp.bfloat16)
    segments = unpack(weights)
    unpacked = [segments[0], segments[1]] + [segment.astype(jnp.float32) for segment in segments[2:]]
    kernel = unpacked[2]
    conv_bias = unpacked[3]
    half_side = KS // 2

    def pad_field(values):
        wrapped = jnp.concatenate([values[:, LON - half_side:], values, values[:, :half_side]], axis=1)
        return jnp.pad(wrapped, ((half_side, half_side), (0, 0), (0, 0)))
    padded = pad_field(features)
    block_count = LAT // LAT_DEV

    def block_step(running, block_index):
        offset = block_index * LAT_DEV
        rows_pad = lax.dynamic_slice_in_dim(padded, offset, LAT_DEV + KS - 1, 0)
        rows_feat = lax.dynamic_slice_in_dim(features, offset, LAT_DEV, 0)
        rows_up = lax.dynamic_slice_in_dim(upstream, offset, LAT_DEV, 0)
        convolved = depthwise(rows_pad, kernel, conv_bias, LAT_DEV, LON)
        output, grad_conv, layer_grads = ref_layer(convolved, rows_feat, rows_up, unpacked)
        grad_kernel = kernel_grad(grad_conv, rows_pad, LAT_DEV, LON)
        grad_conv_bias = lax.optimization_barrier(jnp.sum(grad_conv.astype(jnp.float32), axis=(0, 1)))
        fresh = layer_grads + (grad_kernel, grad_conv_bias)
        updated = tuple((before_sum + block_sum for before_sum, block_sum in zip(running, fresh)))
        return (updated, (output, grad_conv))
    zeros_init = (jnp.zeros((C, H), jnp.float32), jnp.zeros((H, C), jnp.float32), jnp.zeros((C,), jnp.float32), jnp.zeros((C,), jnp.float32), jnp.zeros((H,), jnp.float32), jnp.zeros((C,), jnp.float32), jnp.zeros((C,), jnp.float32), jnp.zeros((KS, KS, C), jnp.float32), jnp.zeros((C,), jnp.float32))
    running, (out_blocks, grad_blocks) = lax.scan(block_step, zeros_init, jnp.arange(block_count, dtype=jnp.int32))
    output = out_blocks.reshape(LAT, LON, C)
    grad_conv_all = grad_blocks.reshape(LAT, LON, C)
    grad_padded = pad_field(grad_conv_all)

    def input_grad_block(block_index):
        offset = block_index * LAT_DEV
        rows_pad = lax.dynamic_slice_in_dim(grad_padded, offset, LAT_DEV + KS - 1, 0)
        rows_up = lax.dynamic_slice_in_dim(upstream, offset, LAT_DEV, 0)
        return (rows_up.astype(jnp.float32) + transposed(rows_pad, kernel, LAT_DEV, LON)).astype(jnp.bfloat16)
    field_grad = lax.map(input_grad_block, jnp.arange(block_count, dtype=jnp.int32)).reshape(LAT, LON, C)
    grad_in_proj, grad_out_proj, grad_gain, grad_shift, grad_bias_in, grad_bias_out, grad_scale, grad_kernel, grad_conv_bias = running
    flat_grads = jnp.concatenate([grad_in_proj.reshape(-1), grad_out_proj.reshape(-1), grad_kernel.reshape(-1), grad_conv_bias, grad_gain, grad_shift, grad_bias_in, grad_bias_out, grad_scale])
    flat_grads = jnp.pad(flat_grads, (0, PTOT - NPAR))
    new_params = params - STEP_SIZE * flat_grads + NOISE_COEF * langevin_noise
    return (output, field_grad, new_params)
```

```python
import math

import jax
import jax.numpy as jnp
from jax import lax
from jax.sharding import PartitionSpec as P

C = 192
H = 768
KS = 7


EPSILON = 1e-06
STEP_SIZE = 0.003
NOISE_COEF = 0.08


def padded_2(block, sides, width, periodic):
    for axis, dim in sides:
        count = lax.axis_size(axis)
        forward = [(i, i + 1) for i in range(count - 1)]
        if periodic:
            forward.append((count - 1, 0))
        backward = [(target, source) for source, target in forward]
        low = lax.ppermute(
            lax.slice_in_dim(block, block.shape[dim] - width, None, axis=dim), axis, forward
        )
        high = lax.ppermute(lax.slice_in_dim(block, 0, width, axis=dim), axis, backward)
        block = jnp.concatenate([low, block, high], axis=dim)
    return block


def exchange_bits(axes):
    steps = []
    for axis in axes:
        bit = lax.axis_size(axis) // 2
        while bit:
            steps.append((axis, bit))
            bit //= 2
    return steps


def swap(values, axis, bit):
    return lax.ppermute(values, axis, [(i, i ^ bit) for i in range(lax.axis_size(axis))])


def gather_flat(share, axes):
    steps = exchange_bits(axes)
    length = share.shape[0]
    for axis, bit in steps:
        other = swap(share, axis, bit)
        upper = (lax.axis_index(axis) & bit) != 0
        share = jnp.concatenate([jnp.where(upper, other, share), jnp.where(upper, share, other)])
    return reverse_bits(share, len(steps), length)


def reverse_bits(values, count, length):
    blocks = values.reshape((2,) * count + (length,))
    return blocks.transpose(tuple(range(count))[::-1] + (count,)).reshape(-1)


def scatter_sum(values, axes):
    steps = exchange_bits(axes)
    values = reverse_bits(values, len(steps), values.shape[0] >> len(steps))
    for axis, bit in steps[::-1]:
        half = values.shape[0] // 2
        upper = (lax.axis_index(axis) & bit) != 0
        low, high = values[:half], values[half:]
        sent = jnp.where(upper, low, high).astype(jnp.bfloat16)
        kept = jnp.where(upper, high, low)
        values = kept + swap(sent, axis, bit).astype(jnp.float32)
    return values


def unpack(weights):
    layouts = [(C, H), (H, C), (KS, KS, C), (C,), (C,), (C,), (H,), (C,), (C,)]
    pieces = []
    offset = 0
    for layout in layouts:
        length = math.prod(layout)
        pieces.append(weights[offset : offset + length].reshape(layout))
        offset = offset + length
    return pieces


def gelu_tanh(values):
    return jax.nn.gelu(values, approximate=True)


def depthwise(padded, kernel, conv_bias, lat_rows, lon_cols):
    summed = jnp.zeros((lat_rows, lon_cols, padded.shape[2]), jnp.float32) + conv_bias
    for row_off in range(KS):
        for col_off in range(KS):
            window = padded[row_off : row_off + lat_rows, col_off : col_off + lon_cols]
            summed = summed + kernel[row_off, col_off] * window.astype(jnp.float32)
    return summed


def transposed(grad_padded, kernel, lat_rows, lon_cols):
    span = KS - 1
    summed = jnp.zeros((lat_rows, lon_cols, grad_padded.shape[2]), jnp.float32)
    for row_off in range(KS):
        for col_off in range(KS):
            window = grad_padded[
                span - row_off : span - row_off + lat_rows,
                span - col_off : span - col_off + lon_cols,
            ]
            summed = summed + kernel[row_off, col_off] * window.astype(jnp.float32)
    return summed


def kernel_grad(grad_conv, padded, lat_rows, lon_cols):
    sums = []
    for row_off in range(KS):
        for col_off in range(KS):
            window = padded[row_off : row_off + lat_rows, col_off : col_off + lon_cols]
            sums.append(
                jnp.sum(grad_conv.astype(jnp.float32) * window.astype(jnp.float32), axis=(0, 1))
            )
    return jnp.stack(sums).reshape(KS, KS, -1)


def layer_pass(convolved, features, upstream, unpacked):
    w_in, w_out, kernel, conv_bias, ln_gain, ln_bias, bias_in, bias_out, layer_scale = unpacked
    mean_val = jnp.mean(convolved, axis=-1, keepdims=True)
    centred = convolved - mean_val
    inv_std = lax.rsqrt(jnp.mean(centred * centred, axis=-1, keepdims=True) + EPSILON)
    standard = centred * inv_std
    normed = (standard * ln_gain + ln_bias).astype(jnp.bfloat16)
    pre_act = jnp.einsum("ijc,ch->ijh", normed, w_in, preferred_element_type=jnp.float32) + bias_in
    activated, pullback = jax.vjp(gelu_tanh, pre_act)
    act_rounded = activated.astype(jnp.bfloat16)
    branch = (
        jnp.einsum("ijh,hc->ijc", act_rounded, w_out, preferred_element_type=jnp.float32) + bias_out
    )
    output = (features.astype(jnp.float32) + layer_scale * branch).astype(jnp.bfloat16)
    upstream_f32 = upstream.astype(jnp.float32)
    grad_branch = (layer_scale * upstream_f32).astype(jnp.bfloat16)
    grad_act = jnp.einsum("ijc,hc->ijh", grad_branch, w_out, preferred_element_type=jnp.float32)
    grad_pre = pullback(grad_act)[0].astype(jnp.bfloat16)
    grad_normed = jnp.einsum("ijh,ch->ijc", grad_pre, w_in, preferred_element_type=jnp.float32)
    scaled = grad_normed * ln_gain
    grad_conv = (
        (
            scaled
            - jnp.mean(scaled, axis=-1, keepdims=True)
            - standard * jnp.mean(scaled * standard, axis=-1, keepdims=True)
        )
        * inv_std
    ).astype(jnp.bfloat16)
    grad_in_proj = jnp.einsum("ijc,ijh->ch", normed, grad_pre, preferred_element_type=jnp.float32)
    grad_out_proj = jnp.einsum(
        "ijh,ijc->hc", act_rounded, grad_branch, preferred_element_type=jnp.float32
    )
    grad_gain = jnp.sum(grad_normed * standard, axis=(0, 1))
    grad_shift = jnp.sum(grad_normed, axis=(0, 1))
    grad_bias_in = jnp.sum(grad_pre.astype(jnp.float32), axis=(0, 1))
    grad_bias_out = jnp.sum(grad_branch.astype(jnp.float32), axis=(0, 1))
    grad_scale = jnp.sum(branch * upstream_f32, axis=(0, 1))
    layer_grads = (
        grad_in_proj,
        grad_out_proj,
        grad_gain,
        grad_shift,
        grad_bias_in,
        grad_bias_out,
        grad_scale,
    )
    return (output, grad_conv, layer_grads)


def body(features, params, langevin_noise, upstream):
    lat_rows = features.shape[0]
    lon_cols = features.shape[1]
    half_side = KS // 2
    rounded = params.astype(jnp.bfloat16)
    weights = gather_flat(rounded, ("lon", "lat"))
    segments = unpack(weights)
    unpacked = [segments[0], segments[1]] + [
        segment.astype(jnp.float32) for segment in segments[2:]
    ]
    kernel = unpacked[2]
    conv_bias = unpacked[3]
    lon_padded = padded_2(features, (("lon", 1),), half_side, True)
    padded = padded_2(lon_padded, (("lat", 0),), half_side, False)
    convolved = depthwise(padded, kernel, conv_bias, lat_rows, lon_cols)
    output, grad_conv, layer_grads = layer_pass(convolved, features, upstream, unpacked)
    grad_kernel = kernel_grad(grad_conv, padded, lat_rows, lon_cols)
    grad_conv_bias = jnp.sum(grad_conv.astype(jnp.float32), axis=(0, 1))
    grad_lon = padded_2(grad_conv, (("lon", 1),), half_side, True)
    grad_padded = padded_2(grad_lon, (("lat", 0),), half_side, False)
    field_grad = (
        upstream.astype(jnp.float32) + transposed(grad_padded, kernel, lat_rows, lon_cols)
    ).astype(jnp.bfloat16)
    grad_in_proj, grad_out_proj, grad_gain, grad_shift, grad_bias_in, grad_bias_out, grad_scale = (
        layer_grads
    )
    flat_grads = jnp.concatenate(
        [
            grad_in_proj.reshape(-1),
            grad_out_proj.reshape(-1),
            grad_kernel.reshape(-1),
            grad_conv_bias,
            grad_gain,
            grad_shift,
            grad_bias_in,
            grad_bias_out,
            grad_scale,
        ]
    )
    full_length = params.shape[0] * lax.axis_size("lon") * lax.axis_size("lat")
    flat_grads = jnp.pad(flat_grads, (0, full_length - flat_grads.shape[0]))
    summed = scatter_sum(flat_grads, ("lon", "lat"))
    new_params = params - STEP_SIZE * summed + NOISE_COEF * langevin_noise
    return (output, field_grad, new_params)


def solution(mesh):
    return jax.shard_map(
        body,
        mesh=mesh,
        in_specs=(
            P("lat", "lon", None),
            P(("lon", "lat")),
            P(("lon", "lat")),
            P("lat", "lon", None),
        ),
        out_specs=(P("lat", "lon", None), P("lat", "lon", None), P(("lon", "lat"))),
        check_vma=False,
    )
```

```python
import math

import jax
import jax.numpy as jnp
from jax import lax
from jax.experimental import pallas as pl
from jax.experimental.pallas import tpu as pltpu
from jax.sharding import PartitionSpec as P

C = 192
H = 768
KS = 7
RAD = KS // 2
LANES = 128
CP = 256
TAPS = KS * KS
EPSILON = 1e-06
STEP_SIZE = 0.003
NOISE_COEF = 0.08
GELU_A = math.sqrt(2.0 / math.pi)
GELU_B = GELU_A * 0.044715
F32 = jnp.float32
BF16 = jnp.bfloat16
ROW_OUT = C
ROW_TAPS = 2 * C
ROW_NORM = ROW_TAPS + TAPS // 4
ROW_BIAS_IN = ROW_NORM + 1
ROW_LAST = ROW_NORM + 2
ROWS = ROW_LAST + 1
TILES = H // LANES
WINDOW = 16
VMEM = 56 << 20


def exchange_bits(axes):
    steps = []
    for axis in axes:
        bit = lax.axis_size(axis) // 2
        while bit:
            steps.append((axis, bit))
            bit //= 2
    return steps


def swap(values, axis, bit):
    return lax.ppermute(values, axis, [(i, i ^ bit) for i in range(lax.axis_size(axis))])


def shift_both(low_edge, high_edge, axis, periodic):
    count = lax.axis_size(axis)
    forward = [(i, i + 1) for i in range(count - 1)]
    if periodic:
        forward.append((count - 1, 0))
    backward = [(target, source) for source, target in forward]
    return lax.ppermute(high_edge, axis, forward), lax.ppermute(low_edge, axis, backward)


def reversed_bits(number, count):
    result = 0
    for k in range(count):
        result |= ((number >> k) & 1) << (count - 1 - k)
    return result


def padded_field(block):
    west, east = shift_both(block[:, :RAD], block[:, -RAD:], "lon", True)
    wide = jnp.concatenate([west, block, east], axis=1)
    south, north = shift_both(wide[:RAD], wide[-RAD:], "lat", False)
    return jnp.concatenate([south, wide, north], axis=0)


def up(value, multiple):
    return -(-value // multiple) * multiple


def split_quarter(tiles, quarter):
    lane = lax.broadcasted_iota(jnp.int32, tiles[0].shape, 1)
    low = lane < LANES // 2
    first = 3 * quarter // 2
    if quarter % 2 == 0:
        return tiles[first], jnp.where(low, tiles[first + 1], 0.0)
    left = pltpu.roll(tiles[first], LANES // 2, 1)
    right = pltpu.roll(tiles[first + 1], LANES // 2, 1)
    return jnp.where(low, left, right), jnp.where(low, right, 0.0)


def join_quarters(quarters):
    lane = lax.broadcasted_iota(jnp.int32, quarters[0][0].shape, 1)
    low = lane < LANES // 2
    tiles = []
    for even in (0, 2):
        first, second = quarters[even]
        turned = pltpu.roll(quarters[even + 1][0], LANES // 2, 1)
        last = pltpu.roll(quarters[even + 1][1], LANES // 2, 1)
        tiles += [first, jnp.where(low, second, turned), jnp.where(low, turned, last)]
    return tiles


def depthwise_block(x_ref, k_ref, row, out_rows, lon_regs, store, flip):
    steps = lon_regs // 2

    def body(step, carry):
        tile = step // steps
        lon = pl.multiple_of(step % steps * 16, 16)
        sums = [None] * out_rows
        for offset in range(out_rows + KS - 1):
            for b in range(KS):
                window = x_ref[tile, row + offset, pl.ds(lon + b, 16), :]
                for r in range(out_rows):
                    a = offset - r
                    if 0 <= a < KS:
                        tap = a * KS + b
                        if flip:
                            tap = TAPS - 1 - tap
                        term = window * k_ref[tile, pl.ds(tap, 1), :]
                        sums[r] = term if sums[r] is None else sums[r] + term
        store(tile, lon, sums)
        return carry

    lax.fori_loop(0, 2 * steps, body, 0)


def layer_kernel(order, starts, rows, lon_pad, block_rows,
                 me_ref, gathered_ref, x_ref, feat_ref, up_ref,
                 out_ref, gconv_ref, gin_ref, gout_ref, sums_ref, taps_ref,
                 w_ref, win_ref, wint_ref, wout_ref, woutt_ref, wo32_ref, conv_ref):
    me = me_ref[0]
    w_ref[...] = jnp.zeros_like(w_ref)
    for position, start in zip(order, starts):
        share = gathered_ref[position ^ me].astype(F32)
        for j in range(TILES):
            w_ref[j, pl.ds(start, WINDOW), :] += share[:, j * LANES : (j + 1) * LANES]
    rest = lax.broadcasted_iota(jnp.int32, (CP - C, LANES), 0)
    for j in range(TILES):
        lanes = slice(j * LANES, (j + 1) * LANES)
        main = w_ref[j, pl.ds(0, C), :]
        bias = jnp.where(rest == 0, w_ref[j, pl.ds(ROW_BIAS_IN, 1), :], 0.0)
        whole = jnp.concatenate([main, bias], axis=0)
        win_ref[:, lanes] = whole.astype(BF16)
        wint_ref[lanes, :] = whole.T.astype(BF16)
    for quarter in range(4):
        tiles = [w_ref[j, pl.ds(ROW_OUT, C), :] for j in range(TILES)]
        pair = split_quarter(tiles, quarter)
        tail = split_quarter([w_ref[j, pl.ds(ROW_TAPS, 16), :] for j in range(TILES)], quarter)
        for t in range(2):
            wo32_ref[t, pl.ds(quarter, C, stride=4), :] = pair[t]
            taps_ref[t, pl.ds(quarter, 16, stride=4), :] = tail[t]
    for t in range(2):
        lanes = slice(t * LANES, (t + 1) * LANES)
        whole = wo32_ref[t]
        wout_ref[:, lanes] = whole.astype(BF16)
        woutt_ref[lanes, :] = whole.T.astype(BF16)

    def vector(row, quarter):
        at = (row - ROW_TAPS) * 4 + quarter
        return [taps_ref[t, pl.ds(at, 1), :] for t in range(2)]

    cbias = vector(ROW_NORM, 1)
    gain = vector(ROW_NORM, 2)
    shift = vector(ROW_NORM, 3)
    bias_out = vector(ROW_LAST, 0)
    scale = vector(ROW_LAST, 1)
    lane = lax.broadcasted_iota(jnp.int32, (1, LANES), 1)
    inside = (lane < C - LANES).astype(F32)
    shift[1] = shift[1] + (lane == C - LANES).astype(F32)

    gin_ref[...] = jnp.zeros_like(gin_ref)
    gout_ref[...] = jnp.zeros_like(gout_ref)
    sums_ref[...] = jnp.zeros_like(sums_ref)
    cells = block_rows * lon_pad

    def partial(values):
        return values.reshape(cells // 8, 8, LANES).sum(axis=0)

    def body(block, carry):
        row = block * block_rows

        def store(tile, lon, sums):
            for r in range(block_rows):
                conv_ref[tile, r, pl.ds(lon, 16), :] = sums[r]

        depthwise_block(x_ref, taps_ref, row, block_rows, lon_pad // 8, store, False)
        conv = [conv_ref[t].reshape(cells, LANES) + cbias[t] for t in range(2)]
        mean = jnp.sum(conv[0] + conv[1], axis=1, keepdims=True) * (1.0 / C)
        centred = [conv[0] - mean, (conv[1] - mean) * inside]
        square = centred[0] * centred[0] + centred[1] * centred[1]
        inv_std = lax.rsqrt(jnp.sum(square, axis=1, keepdims=True) * (1.0 / C) + EPSILON)
        standard = [c * inv_std for c in centred]
        normed = jnp.concatenate(
            [(standard[t] * gain[t] + shift[t]).astype(BF16) for t in range(2)], axis=1
        )
        upstream = up_ref[pl.ds(row, block_rows)].reshape(cells, CP)
        ups = [upstream[:, t * LANES : (t + 1) * LANES].astype(F32) for t in range(2)]
        grad_branch = [(scale[t] * ups[t]).astype(BF16) for t in range(2)]
        gbranch = jnp.concatenate(grad_branch, axis=1)
        branch = None
        gnormed = None
        for h in range(0, H, CP):
            hidden = slice(h, h + CP)
            pre = jnp.dot(normed, win_ref[:, hidden], preferred_element_type=F32)
            gact = jnp.dot(gbranch, woutt_ref[:, hidden], preferred_element_type=F32)
            square = pre * pre
            half = 0.5 + 0.5 * jnp.tanh(pre * (GELU_A + GELU_B * square))
            act = pre * half
            slope = half + act * (1.0 - half) * (2.0 * GELU_A + 6.0 * GELU_B * square)
            act = act.astype(BF16)
            gpre = (gact * slope).astype(BF16)
            part = jnp.dot(act, wout_ref[hidden, :], preferred_element_type=F32)
            branch = part if branch is None else branch + part
            part = jnp.dot(gpre, wint_ref[hidden, :], preferred_element_type=F32)
            gnormed = part if gnormed is None else gnormed + part
            over = (((0,), (0,)), ((), ()))
            gin_ref[:, hidden] += lax.dot_general(normed, gpre, over, preferred_element_type=F32)
            gout_ref[:, hidden] += lax.dot_general(gbranch, act, over, preferred_element_type=F32)
        feat = feat_ref[pl.ds(row, block_rows)].reshape(cells, CP)
        outs = []
        gs = []
        gn = []
        for t in range(2):
            lanes = slice(t * LANES, (t + 1) * LANES)
            branch_t = branch[:, lanes] + bias_out[t]
            outs.append((feat[:, lanes].astype(F32) + scale[t] * branch_t).astype(BF16))
            gn.append(gnormed[:, lanes])
            sums_ref[4, t] += partial(branch_t * ups[t])
            sums_ref[3, t] += partial(grad_branch[t].astype(F32))
            sums_ref[1, t] += partial(gn[t] * standard[t])
            sums_ref[2, t] += partial(gn[t])
            gs.append(gn[t] * gain[t])
        mean_g = jnp.sum(gs[0] + gs[1], axis=1, keepdims=True) * (1.0 / C)
        both = gs[0] * standard[0] + gs[1] * standard[1]
        mean_gs = jnp.sum(both, axis=1, keepdims=True) * (1.0 / C)
        gconv = []
        for t in range(2):
            grad = ((gs[t] - mean_g - standard[t] * mean_gs) * inv_std).astype(BF16)
            sums_ref[0, t] += partial(grad.astype(F32))
            gconv.append(grad)
        gconv_ref[pl.ds(row, block_rows)] = jnp.concatenate(gconv, axis=1).reshape(
            block_rows, lon_pad, CP
        )
        out = jnp.concatenate(outs, axis=1).reshape(block_rows, lon_pad, CP)
        out_ref[pl.ds(row, block_rows)] = out[:, : out_ref.shape[1], :C]
        return carry

    lax.fori_loop(0, rows // block_rows, body, 0)


def taps_kernel(order, starts, rows, lon_pad, block_rows,
                me_ref, gconv_ref, x_ref, gin_ref, gout_ref, sums_ref,
                g_ref, rows_ref, acc_ref, wo32_ref, small_ref):
    acc_ref[...] = jnp.zeros_like(acc_ref)

    def body(step, carry):
        tile = step % 2
        row = step // 2 * block_rows
        lanes = pl.ds(pl.multiple_of(tile * LANES, LANES), LANES)
        grads = [gconv_ref[row + r, :, lanes].astype(F32) for r in range(block_rows)]
        for b in range(KS):
            windows = [
                x_ref[tile, row + offset, pl.ds(b, lon_pad), :]
                for offset in range(block_rows + KS - 1)
            ]
            for a in range(KS):
                total = None
                for r in range(block_rows):
                    term = grads[r] * windows[r + a]
                    total = term if total is None else total + term
                acc_ref[tile, a * KS + b] += total.reshape(lon_pad // 8, 8, LANES).sum(axis=0)
        return carry

    lax.fori_loop(0, 2 * (rows // block_rows), body, 0)
    rows_ref[...] = jnp.zeros_like(rows_ref)
    small_ref[...] = jnp.zeros_like(small_ref)
    for t in range(2):
        small_ref[t, pl.ds(0, TAPS), :] = jnp.sum(acc_ref[t], axis=1)
        for at, k in ((TAPS, 0), (TAPS + 1, 1), (TAPS + 2, 2), (TAPS + 7, 3), (TAPS + 8, 4)):
            small_ref[t, pl.ds(at, 1), :] = jnp.sum(sums_ref[k, t], axis=0, keepdims=True)
        wo32_ref[t] = gout_ref[pl.ds(t * LANES, LANES), :].T
    outs = join_quarters(
        [[wo32_ref[t, pl.ds(q, C, stride=4), :] for t in range(2)] for q in range(4)]
    )
    tails = join_quarters(
        [[small_ref[t, pl.ds(q, 16, stride=4), :] for t in range(2)] for q in range(4)]
    )
    for j in range(TILES):
        lanes = slice(j * LANES, (j + 1) * LANES)
        rows_ref[j, pl.ds(0, C), :] = gin_ref[pl.ds(0, C), lanes]
        rows_ref[j, pl.ds(ROW_OUT, C), :] = outs[j]
        rows_ref[j, pl.ds(ROW_TAPS, 16), :] = tails[j]
        rows_ref[j, pl.ds(ROW_BIAS_IN, 1), :] = gin_ref[pl.ds(C, 1), lanes]
    me = me_ref[0]
    for position, start in zip(order, starts):
        share = jnp.concatenate(
            [rows_ref[j, pl.ds(start, WINDOW), :] for j in range(TILES)], axis=1
        )
        g_ref[position ^ me] = share.astype(BF16)


def field_kernel(rows, lon_pad, block_rows, pad_ref, taps_ref, up_ref, out_ref, x_ref):
    for t in range(2):
        x_ref[t] = pad_ref[:, :, t * LANES : (t + 1) * LANES].astype(F32)

    def body(block, carry):
        row = block * block_rows

        def store(tile, lon, sums):
            lanes = pl.ds(pl.multiple_of(tile * LANES, LANES), LANES)
            for r in range(block_rows):
                total = sums[r] + up_ref[row + r, pl.ds(lon, 16), lanes].astype(F32)
                out_ref[row + r, pl.ds(lon, 16), lanes] = total.astype(BF16)

        depthwise_block(x_ref, taps_ref, row, block_rows, lon_pad // 8, store, True)
        return carry

    lax.fori_loop(0, rows // block_rows, body, 0)


def shape(dims, kind):
    return jax.ShapeDtypeStruct(dims, kind)


def whole(count):
    return [pl.BlockSpec(memory_space=pltpu.VMEM)] * count


def body(features, params, langevin_noise, upstream):
    rows, cols = features.shape[:2]
    lon_pad = up(cols, 16)
    lon_wide = up(lon_pad + KS - 1, 8)
    block_rows = max(r for r in range(1, 6) if rows % r == 0)
    axes = ("lon", "lat")
    steps = exchange_bits(axes)
    count = 1 << len(steps)
    lat_size = lax.axis_size("lat")
    length = params.shape[0]
    number = lax.axis_index("lon") * lat_size + lax.axis_index("lat")
    place = jnp.int32(0)
    for k in range(len(steps)):
        place = place | (((number >> k) & 1) << (len(steps) - 1 - k))
    place = place.reshape(1).astype(jnp.int32)
    offset = (number * length) % H
    order = [reversed_bits(s, len(steps)) for s in range(count)]
    starts = [s * length // H for s in range(count)]
    w_rows = up(starts[-1] + WINDOW, 8)

    window = lax.dynamic_update_slice(
        jnp.zeros((WINDOW * H,), BF16), params.astype(BF16), (offset,)
    )
    gathered = window.reshape(1, WINDOW, H)
    for axis, bit in steps:
        gathered = jnp.concatenate([gathered, swap(gathered, axis, bit)], axis=0)

    def widen(field, lons):
        return jnp.pad(field, ((0, 0), (0, lons - field.shape[1]), (0, CP - C)))

    padded = widen(padded_field(features), lon_wide)
    x = padded.astype(F32).reshape(rows + KS - 1, lon_wide, 2, LANES).transpose(2, 0, 1, 3)
    feat = widen(features, lon_pad)
    ups = widen(upstream, lon_pad)

    params_in = pltpu.CompilerParams(vmem_limit_bytes=VMEM)
    smem = [pl.BlockSpec(memory_space=pltpu.SMEM)]
    static = (order, starts, rows, lon_pad, block_rows)
    output, gconv, gin, gout, sums, taps = pl.pallas_call(
        lambda *refs: layer_kernel(*static, *refs),
        out_shape=(
            shape((rows, cols, C), BF16),
            shape((rows, lon_pad, CP), BF16),
            shape((CP, H), F32),
            shape((CP, H), F32),
            shape((5, 2, 8, LANES), F32),
            shape((2, 64, LANES), F32),
        ),
        in_specs=smem + whole(4),
        out_specs=tuple(whole(6)),
        scratch_shapes=[
            pltpu.VMEM((TILES, w_rows, LANES), F32),
            pltpu.VMEM((CP, H), BF16),
            pltpu.VMEM((H, CP), BF16),
            pltpu.VMEM((H, CP), BF16),
            pltpu.VMEM((CP, H), BF16),
            pltpu.VMEM((2, H, LANES), F32),
            pltpu.VMEM((2, block_rows, lon_pad, LANES), F32),
        ],
        compiler_params=params_in,
        name="layer",
    )(place, gathered, x, feat, ups)

    grad_padded = widen(padded_field(gconv[:, :cols, :C]), lon_wide)
    grads = pl.pallas_call(
        lambda *refs: taps_kernel(*static, *refs),
        out_shape=shape((count, WINDOW, H), BF16),
        in_specs=smem + whole(5),
        out_specs=whole(1)[0],
        scratch_shapes=[
            pltpu.VMEM((TILES, w_rows, LANES), F32),
            pltpu.VMEM((2, TAPS, 8, LANES), F32),
            pltpu.VMEM((2, H, LANES), F32),
            pltpu.VMEM((2, 64, LANES), F32),
        ],
        compiler_params=params_in,
        name="taps",
    )(place, gconv, x, gin, gout, sums)

    field = pl.pallas_call(
        lambda *refs: field_kernel(rows, lon_pad, block_rows, *refs),
        out_shape=shape((rows, lon_pad, CP), BF16),
        in_specs=whole(3),
        out_specs=whole(1)[0],
        scratch_shapes=[pltpu.VMEM((2, rows + KS - 1, lon_wide, LANES), F32)],
        compiler_params=params_in,
        name="field",
    )(grad_padded, taps, ups)

    values = grads
    kept = None
    for axis, bit in steps[::-1]:
        half = values.shape[0] // 2
        received = swap(values[half:].astype(BF16), axis, bit)
        values = values[:half].astype(F32) + received.astype(F32)
    summed = lax.dynamic_slice(values.reshape(-1), (offset,), (length,))
    new_params = params - STEP_SIZE * summed + NOISE_COEF * langevin_noise
    return (output, field[:, :cols, :C], new_params)


def solution(mesh):
    return jax.shard_map(
        body,
        mesh=mesh,
        in_specs=(
            P("lat", "lon", None),
            P(("lon", "lat")),
            P(("lon", "lat")),
            P("lat", "lon", None),
        ),
        out_specs=(P("lat", "lon", None), P("lat", "lon", None), P(("lon", "lat"))),
        check_vma=False,
    )
```

```python
import math

import jax
import jax.numpy as jnp
from jax import lax
from jax.experimental import pallas as pl
from jax.experimental.pallas import tpu as pltpu
from jax.sharding import PartitionSpec as P

C = 192
H = 768
KS = 7
RAD = KS // 2
LANES = 128
CP = 256
TAPS = KS * KS
EPSILON = 1e-06
STEP_SIZE = 0.003
NOISE_COEF = 0.08
GELU_A = math.sqrt(2.0 / math.pi)
GELU_B = GELU_A * 0.044715
F32 = jnp.float32
BF16 = jnp.bfloat16
ROW_OUT = C
ROW_TAPS = 2 * C
ROW_NORM = ROW_TAPS + TAPS // 4
ROW_BIAS_IN = ROW_NORM + 1
ROW_LAST = ROW_NORM + 2
ROWS = ROW_LAST + 1
TILES = H // LANES
SHARE_LANES = 256
ALL = ((1,), (1,)), ((), ())
OVER = ((0,), (0,)), ((), ())
VMEM = 56 << 20


def exchange_bits(axes):
    steps = []
    for axis in axes:
        bit = lax.axis_size(axis) // 2
        while bit:
            steps.append((axis, bit))
            bit //= 2
    return steps


def swap(values, axis, bit):
    return lax.ppermute(values, axis, [(i, i ^ bit) for i in range(lax.axis_size(axis))])


def shift_both(low_edge, high_edge, axis, periodic):
    count = lax.axis_size(axis)
    forward = [(i, i + 1) for i in range(count - 1)]
    if periodic:
        forward.append((count - 1, 0))
    backward = [(target, source) for source, target in forward]
    return lax.ppermute(high_edge, axis, forward), lax.ppermute(low_edge, axis, backward)


def reversed_bits(number, count):
    result = 0
    for k in range(count):
        result |= ((number >> k) & 1) << (count - 1 - k)
    return result


def up(value, multiple):
    return -(-value // multiple) * multiple


def split_quarter(tiles, quarter):
    lane = lax.broadcasted_iota(jnp.int32, tiles[0].shape, 1)
    low = lane < LANES // 2
    first = 3 * quarter // 2
    if quarter % 2 == 0:
        return tiles[first], jnp.where(low, tiles[first + 1], 0.0)
    left = pltpu.roll(tiles[first], LANES // 2, 1)
    right = pltpu.roll(tiles[first + 1], LANES // 2, 1)
    return jnp.where(low, left, right), jnp.where(low, right, 0.0)


def join_quarters(quarters):
    lane = lax.broadcasted_iota(jnp.int32, quarters[0][0].shape, 1)
    low = lane < LANES // 2
    tiles = []
    for even in (0, 2):
        first, second = quarters[even]
        turned = pltpu.roll(quarters[even + 1][0], LANES // 2, 1)
        last = pltpu.roll(quarters[even + 1][1], LANES // 2, 1)
        tiles += [first, jnp.where(low, second, turned), jnp.where(low, turned, last)]
    return tiles


def get_rows(flat_ref, row, count):
    return [
        flat_ref[j % 2, pl.ds(3 * row + j // 2, count, stride=3), :] for j in range(TILES)
    ]


def put_rows(flat_ref, row, tiles):
    for j in range(TILES):
        flat_ref[j % 2, pl.ds(3 * row + j // 2, tiles[j].shape[0], stride=3), :] = tiles[j]


def assemble(x_ref, first, count, main, west, east, south, north, rows, cols):
    x_ref[...] = jnp.zeros_like(x_ref)
    for t in range(2):
        lanes = slice(t * LANES, min(C, (t + 1) * LANES))
        width = slice(0, lanes.stop - lanes.start)
        low = max(0, first - RAD)
        high = min(rows, first + count - RAD)
        at = slice(low + RAD - first, high + RAD - first)
        x_ref[t, at, 0:RAD, width] = west[low:high, :, lanes].astype(F32)
        x_ref[t, at, RAD : RAD + cols, width] = main[low:high, 0:cols, lanes].astype(F32)
        x_ref[t, at, RAD + cols : 2 * RAD + cols, width] = east[low:high, :, lanes].astype(F32)
        if first < RAD:
            x_ref[t, 0 : RAD - first, 0 : cols + 2 * RAD, width] = south[first:, :, lanes].astype(F32)
        over = first + count - rows - RAD
        if over > 0:
            x_ref[t, count - over : count, 0 : cols + 2 * RAD, width] = north[0:over, :, lanes].astype(F32)


def assemble_kernel(rows, cols, feat_ref, west_ref, east_ref, south_ref, north_ref, up_ref,
                    x_ref, ups_ref):
    assemble(x_ref, 0, x_ref.shape[1], feat_ref, west_ref, east_ref, south_ref, north_ref, rows, cols)
    ups_ref[...] = jnp.zeros_like(ups_ref)
    ups_ref[:, 0:cols, 0:C] = up_ref[...]


def depthwise_block(x_ref, k_ref, row, out_rows, lon_regs, store, flip):
    steps = lon_regs // 2

    def body(step, carry):
        tile = step // steps
        lon = pl.multiple_of(step % steps * 16, 16)
        sums = [None] * out_rows
        for offset in range(out_rows + KS - 1):
            for b in range(KS):
                window = x_ref[tile, row + offset, pl.ds(lon + b, 16), :]
                for r in range(out_rows):
                    a = offset - r
                    if 0 <= a < KS:
                        tap = a * KS + b
                        if flip:
                            tap = TAPS - 1 - tap
                        term = window * k_ref[tile, pl.ds(tap, 1), :]
                        sums[r] = term if sums[r] is None else sums[r] + term
        store(tile, lon, sums)
        return carry

    lax.fori_loop(0, 2 * steps, body, 0)


def layer_kernel(order, starts, rows, lon_pad, block_rows, conv_rows,
                 me_ref, gathered_ref, x_ref, up_ref,
                 out_ref, gconv_ref, gin_ref, gout_ref, sums_ref, taps_ref,
                 w_ref, win_ref, wout_ref, wo32_ref, conv_ref):
    me = me_ref[0]
    w_ref[...] = jnp.zeros_like(w_ref)
    window = gathered_ref.shape[1]
    for position, start in zip(order, starts):
        share = gathered_ref[position ^ me].astype(F32)
        for t in range(2):
            w_ref[t, pl.ds(start, window), :] += share[:, t * LANES : (t + 1) * LANES]
    rest = lax.broadcasted_iota(jnp.int32, (CP - C, LANES), 0)
    mains = get_rows(w_ref, 0, C)
    biases = get_rows(w_ref, ROW_BIAS_IN, 1)
    for j in range(TILES):
        bias = jnp.where(rest == 0, biases[j], 0.0)
        whole = jnp.concatenate([mains[j], bias], axis=0)
        win_ref[:, j * LANES : (j + 1) * LANES] = whole.astype(BF16)
    for quarter in range(4):
        pair = split_quarter(get_rows(w_ref, ROW_OUT, C), quarter)
        tail = split_quarter(get_rows(w_ref, ROW_TAPS, 16), quarter)
        for t in range(2):
            wo32_ref[t, pl.ds(quarter, C, stride=4), :] = pair[t]
            taps_ref[t, pl.ds(quarter, 16, stride=4), :] = tail[t]
    for t in range(2):
        wout_ref[:, t * LANES : (t + 1) * LANES] = wo32_ref[t].astype(BF16)

    def vector(row, quarter):
        at = (row - ROW_TAPS) * 4 + quarter
        return [taps_ref[t, pl.ds(at, 1), :] for t in range(2)]

    cbias = vector(ROW_NORM, 1)
    gain = vector(ROW_NORM, 2)
    shift = vector(ROW_NORM, 3)
    bias_out = vector(ROW_LAST, 0)
    scale = vector(ROW_LAST, 1)
    lane = lax.broadcasted_iota(jnp.int32, (1, LANES), 1)
    inside = (lane < C - LANES).astype(F32)
    shift[1] = shift[1] + (lane == C - LANES).astype(F32)

    gin_ref[...] = jnp.zeros_like(gin_ref)
    gout_ref[...] = jnp.zeros_like(gout_ref)
    sums_ref[...] = jnp.zeros_like(sums_ref)
    cells = block_rows * lon_pad

    def partial(values):
        return values.reshape(cells // 8, 8, LANES).sum(axis=0)

    def body(block, carry):
        row = block * block_rows

        def conv_step(part, carry):
            at = part * conv_rows

            def store(tile, lon, sums):
                for r in range(conv_rows):
                    conv_ref[tile, at + r, pl.ds(lon, 16), :] = sums[r]

            depthwise_block(x_ref, taps_ref, row + at, conv_rows, lon_pad // 8, store, False)
            return carry

        lax.fori_loop(0, block_rows // conv_rows, conv_step, 0)
        conv = [conv_ref[t].reshape(cells, LANES) + cbias[t] for t in range(2)]
        mean = jnp.sum(conv[0] + conv[1], axis=1, keepdims=True) * (1.0 / C)
        centred = [conv[0] - mean, (conv[1] - mean) * inside]
        square = centred[0] * centred[0] + centred[1] * centred[1]
        inv_std = lax.rsqrt(jnp.sum(square, axis=1, keepdims=True) * (1.0 / C) + EPSILON)
        standard = [c * inv_std for c in centred]
        normed = jnp.concatenate(
            [(standard[t] * gain[t] + shift[t]).astype(BF16) for t in range(2)], axis=1
        )
        upstream = up_ref[pl.ds(row, block_rows)].reshape(cells, CP)
        ups = [upstream[:, t * LANES : (t + 1) * LANES].astype(F32) for t in range(2)]
        grad_branch = [(scale[t] * ups[t]).astype(BF16) for t in range(2)]
        gbranch = jnp.concatenate(grad_branch, axis=1)
        branch = None
        gnormed = None
        for h in range(0, H, CP):
            hidden = slice(h, h + CP)
            pre = jnp.dot(normed, win_ref[:, hidden], preferred_element_type=F32)
            gact = lax.dot_general(gbranch, wout_ref[hidden, :], ALL, preferred_element_type=F32)
            square = pre * pre
            half = 0.5 + 0.5 * jnp.tanh(pre * (GELU_A + GELU_B * square))
            act = pre * half
            slope = half + act * (1.0 - half) * (2.0 * GELU_A + 6.0 * GELU_B * square)
            act = act.astype(BF16)
            gpre = (gact * slope).astype(BF16)
            part = jnp.dot(act, wout_ref[hidden, :], preferred_element_type=F32)
            branch = part if branch is None else branch + part
            part = lax.dot_general(gpre, win_ref[:, hidden], ALL, preferred_element_type=F32)
            gnormed = part if gnormed is None else gnormed + part
            gin_ref[:, hidden] += lax.dot_general(normed, gpre, OVER, preferred_element_type=F32)
            gout_ref[:, hidden] += lax.dot_general(gbranch, act, OVER, preferred_element_type=F32)
        outs = []
        gs = []
        gn = []
        for t in range(2):
            lanes = slice(t * LANES, (t + 1) * LANES)
            branch_t = branch[:, lanes] + bias_out[t]
            feat = x_ref[t, pl.ds(row + RAD, block_rows), pl.ds(RAD, lon_pad), :]
            feat = feat.reshape(cells, LANES)
            outs.append((feat + scale[t] * branch_t).astype(BF16))
            gn.append(gnormed[:, lanes])
            sums_ref[4, t] += partial(branch_t * ups[t])
            sums_ref[3, t] += partial(grad_branch[t].astype(F32))
            sums_ref[1, t] += partial(gn[t] * standard[t])
            sums_ref[2, t] += partial(gn[t])
            gs.append(gn[t] * gain[t])
        mean_g = jnp.sum(gs[0] + gs[1], axis=1, keepdims=True) * (1.0 / C)
        both = gs[0] * standard[0] + gs[1] * standard[1]
        mean_gs = jnp.sum(both, axis=1, keepdims=True) * (1.0 / C)
        gconv = []
        for t in range(2):
            grad = ((gs[t] - mean_g - standard[t] * mean_gs) * inv_std).astype(BF16)
            sums_ref[0, t] += partial(grad.astype(F32))
            gconv.append(grad)
        gconv_ref[pl.ds(row, block_rows)] = jnp.concatenate(gconv, axis=1).reshape(
            block_rows, lon_pad, CP
        )
        out = jnp.concatenate(outs, axis=1).reshape(block_rows, lon_pad, CP)
        out_ref[pl.ds(row, block_rows)] = out[:, : out_ref.shape[1], :C]
        return carry

    lax.fori_loop(0, rows // block_rows, body, 0)


def taps_kernel(order, starts, rows, lon_pad, block_rows, conv_rows,
                me_ref, gconv_ref, x_ref, gin_ref, gout_ref, sums_ref,
                g_ref, rows_ref, acc_ref, wo32_ref, small_ref):
    acc_ref[...] = jnp.zeros_like(acc_ref)

    def body(step, carry):
        tile = step % 2
        row = step // 2 * conv_rows
        lanes = pl.ds(pl.multiple_of(tile * LANES, LANES), LANES)
        grads = [gconv_ref[row + r, :, lanes].astype(F32) for r in range(conv_rows)]
        for b in range(KS):
            windows = [
                x_ref[tile, row + offset, pl.ds(b, lon_pad), :]
                for offset in range(conv_rows + KS - 1)
            ]
            for a in range(KS):
                total = None
                for r in range(conv_rows):
                    term = grads[r] * windows[r + a]
                    total = term if total is None else total + term
                acc_ref[tile, a * KS + b] += total.reshape(lon_pad // 8, 8, LANES).sum(axis=0)
        return carry

    lax.fori_loop(0, 2 * (rows // conv_rows), body, 0)
    rows_ref[...] = jnp.zeros_like(rows_ref)
    small_ref[...] = jnp.zeros_like(small_ref)
    for t in range(2):
        small_ref[t, pl.ds(0, TAPS), :] = jnp.sum(acc_ref[t], axis=1)
        for at, k in ((TAPS, 0), (TAPS + 1, 1), (TAPS + 2, 2), (TAPS + 7, 3), (TAPS + 8, 4)):
            small_ref[t, pl.ds(at, 1), :] = jnp.sum(sums_ref[k, t], axis=0, keepdims=True)
        wo32_ref[t] = gout_ref[pl.ds(t * LANES, LANES), :].T
    outs = join_quarters(
        [[wo32_ref[t, pl.ds(q, C, stride=4), :] for t in range(2)] for q in range(4)]
    )
    tails = join_quarters(
        [[small_ref[t, pl.ds(q, 16, stride=4), :] for t in range(2)] for q in range(4)]
    )
    put_rows(rows_ref, 0, [gin_ref[pl.ds(0, C), j * LANES : (j + 1) * LANES] for j in range(TILES)])
    put_rows(rows_ref, ROW_OUT, outs)
    put_rows(rows_ref, ROW_TAPS, tails)
    put_rows(
        rows_ref,
        ROW_BIAS_IN,
        [gin_ref[pl.ds(C, 1), j * LANES : (j + 1) * LANES] for j in range(TILES)],
    )
    me = me_ref[0]
    window = g_ref.shape[1]
    for position, start in zip(order, starts):
        share = [rows_ref[t, pl.ds(start, window), :] for t in range(2)]
        g_ref[position ^ me] = jnp.concatenate(share, axis=1).astype(BF16)


def field_kernel(first, count, rows, cols, lon_pad, conv_rows,
                 taps_ref, up_ref, main_ref, west_ref, east_ref, south_ref, north_ref, *rest):
    out_ref, x_ref, sum_ref = rest[-3:]
    assemble(x_ref, first, count + KS - 1, main_ref, west_ref, east_ref, south_ref, north_ref, rows, cols)

    def body(block, carry):
        row = block * conv_rows

        def store(tile, lon, sums):
            lanes = pl.ds(pl.multiple_of(tile * LANES, LANES), LANES)
            for r in range(conv_rows):
                total = sums[r] + up_ref[row + r, pl.ds(lon, 16), lanes].astype(F32)
                sum_ref[row + r, pl.ds(lon, 16), lanes] = total.astype(BF16)

        depthwise_block(x_ref, taps_ref, row, conv_rows, lon_pad // 8, store, True)
        return carry

    lax.fori_loop(0, count // conv_rows, body, 0)
    out_ref[...] = sum_ref[:, 0 : out_ref.shape[1], 0:C]


def shape(dims, kind):
    return jax.ShapeDtypeStruct(dims, kind)


def whole(count):
    return [pl.BlockSpec(memory_space=pltpu.VMEM)] * count


def halos(block, cols):
    west, east = shift_both(block[:, :RAD, :C], block[:, cols - RAD : cols, :C], "lon", True)

    def wide(rows):
        return jnp.concatenate([west[rows], block[rows, :cols, :C], east[rows]], axis=1)

    south, north = shift_both(wide(slice(0, RAD)), wide(slice(-RAD, None)), "lat", False)
    return west, east, south, north


def cost(micros):
    return pl.CostEstimate(flops=int(micros * 1.1e9), bytes_accessed=0, transcendentals=0)


def body(features, params, langevin_noise, upstream):
    rows, cols = features.shape[:2]
    lon_pad = up(cols, 16)
    lon_wide = up(lon_pad + KS - 1, 8)
    conv_rows = max(r for r in range(1, 6) if rows % r == 0)
    block_rows = max(r for r in range(1, 16) if rows % r == 0 and r % conv_rows == 0)
    axes = ("lon", "lat")
    steps = exchange_bits(axes)
    count = 1 << len(steps)
    lat_size = lax.axis_size("lat")
    length = params.shape[0]
    number = lax.axis_index("lon") * lat_size + lax.axis_index("lat")
    place = jnp.int32(0)
    for k in range(len(steps)):
        place = place | (((number >> k) & 1) << (len(steps) - 1 - k))
    place = place.reshape(1).astype(jnp.int32)
    offset = (number * length) % SHARE_LANES
    order = [reversed_bits(s, len(steps)) for s in range(count)]
    starts = [s * length // SHARE_LANES for s in range(count)]
    spill = SHARE_LANES - math.gcd(SHARE_LANES, length)
    window = up(-(-(length + spill) // SHARE_LANES), 8)
    flat_rows = up(max(starts[-1] + window, 3 * (ROWS + 1)), 8)

    share = lax.dynamic_update_slice(
        jnp.zeros((window * SHARE_LANES,), BF16), params.astype(BF16), (offset,)
    )
    gathered = share.reshape(1, window, SHARE_LANES)
    feature_halos = halos(features, cols)
    for k, (axis, bit) in enumerate(steps):
        if k == len(steps) - 2:
            gathered, upstream = lax.optimization_barrier((gathered, upstream))
        gathered = jnp.concatenate([gathered, swap(gathered, axis, bit)], axis=0)

    compiler_params = pltpu.CompilerParams(vmem_limit_bytes=VMEM)
    smem = [pl.BlockSpec(memory_space=pltpu.SMEM)]
    x, ups = pl.pallas_call(
        lambda *refs: assemble_kernel(rows, cols, *refs),
        out_shape=(
            shape((2, rows + KS - 1, lon_wide, LANES), F32),
            shape((rows, lon_pad, CP), BF16),
        ),
        in_specs=whole(6),
        out_specs=tuple(whole(2)),
        compiler_params=compiler_params,
        cost_estimate=cost(3),
        name="assemble",
    )(features, *feature_halos, upstream)

    static = (order, starts, rows, lon_pad, block_rows, conv_rows)
    output, gconv, gin, gout, sums, taps = pl.pallas_call(
        lambda *refs: layer_kernel(*static, *refs),
        out_shape=(
            shape((rows, cols, C), BF16),
            shape((rows, lon_pad, CP), BF16),
            shape((CP, H), F32),
            shape((CP, H), F32),
            shape((5, 2, 8, LANES), F32),
            shape((2, 64, LANES), F32),
        ),
        in_specs=smem + whole(3),
        out_specs=tuple(whole(6)),
        scratch_shapes=[
            pltpu.VMEM((2, flat_rows, LANES), F32),
            pltpu.VMEM((CP, H), BF16),
            pltpu.VMEM((H, CP), BF16),
            pltpu.VMEM((2, H, LANES), F32),
            pltpu.VMEM((2, block_rows, lon_pad, LANES), F32),
        ],
        compiler_params=compiler_params,
        cost_estimate=cost(22),
        name="layer",
    )(place, gathered, x, ups)

    grad_halos = halos(gconv, cols)
    values = pl.pallas_call(
        lambda *refs: taps_kernel(*static, *refs),
        out_shape=shape((count, window, SHARE_LANES), BF16),
        in_specs=smem + whole(5),
        out_specs=whole(1)[0],
        scratch_shapes=[
            pltpu.VMEM((2, flat_rows, LANES), F32),
            pltpu.VMEM((2, TAPS, 8, LANES), F32),
            pltpu.VMEM((2, H, LANES), F32),
            pltpu.VMEM((2, 64, LANES), F32),
        ],
        compiler_params=compiler_params,
        cost_estimate=cost(11),
        name="taps",
    )(place, gconv, x, gin, gout, sums)

    pieces = 3 if rows % (3 * conv_rows) == 0 else 1
    piece_rows = rows // pieces
    field = None
    for piece in range(pieces):
        before = [] if field is None else [field]
        held = [pl.BlockSpec(memory_space=pl.ANY)] * len(before)
        at = lambda i, piece=piece: (piece, 0, 0)
        field = pl.pallas_call(
            lambda *refs, piece=piece: field_kernel(
                piece * piece_rows, piece_rows, rows, cols, lon_pad, conv_rows, *refs
            ),
            grid=(1,),
            out_shape=shape((rows, cols, C), BF16),
            in_specs=whole(1)
            + [pl.BlockSpec((piece_rows, lon_pad, CP), at)]
            + whole(5)
            + held,
            out_specs=pl.BlockSpec((piece_rows, cols, C), at),
            scratch_shapes=[
                pltpu.VMEM((2, piece_rows + KS - 1, lon_wide, LANES), F32),
                pltpu.VMEM((piece_rows, lon_pad, CP), BF16),
            ],
            input_output_aliases={7: 0} if before else {},
            compiler_params=compiler_params,
            cost_estimate=cost(12 / pieces),
            name="field",
        )(taps, ups, gconv, *grad_halos, *before)

    for axis, bit in steps[::-1]:
        half = values.shape[0] // 2
        received = swap(values[half:].astype(BF16), axis, bit)
        values = values[:half].astype(F32) + received.astype(F32)
    summed = lax.dynamic_slice(values.reshape(-1), (offset,), (length,))
    new_params = params - STEP_SIZE * summed + NOISE_COEF * langevin_noise
    return (output, field, new_params)


def solution(mesh):
    return jax.shard_map(
        body,
        mesh=mesh,
        in_specs=(
            P("lat", "lon", None),
            P(("lon", "lat")),
            P(("lon", "lat")),
            P("lat", "lon", None),
        ),
        out_specs=(P("lat", "lon", None), P("lat", "lon", None), P(("lon", "lat"))),
        check_vma=False,
    )
```

```python
import math

import jax
import jax.numpy as jnp
from jax import lax
from jax.experimental import pallas as pl
from jax.experimental.pallas import tpu as pltpu
from jax.sharding import PartitionSpec as P

C = 192
H = 768
KS = 7
RAD = KS // 2
LANES = 128
CP = 256
TAPS = KS * KS
EPSILON = 1e-06
STEP_SIZE = 0.003
NOISE_COEF = 0.08
GELU_A = math.sqrt(2.0 / math.pi)
GELU_B = GELU_A * 0.044715
F32 = jnp.float32
BF16 = jnp.bfloat16
ROW_OUT = C
ROW_TAPS = 2 * C
ROW_NORM = ROW_TAPS + TAPS // 4
ROW_BIAS_IN = ROW_NORM + 1
ROW_LAST = ROW_NORM + 2
ROWS = ROW_LAST + 1
TILES = H // LANES
SHARE_LANES = 256
ALL = ((1,), (1,)), ((), ())
OVER = ((0,), (0,)), ((), ())
VMEM = 28 << 20


def exchange_bits(axes):
    steps = []
    for axis in axes:
        bit = lax.axis_size(axis) // 2
        while bit:
            steps.append((axis, bit))
            bit //= 2
    return steps


def swap(values, axis, bit):
    return lax.ppermute(values, axis, [(i, i ^ bit) for i in range(lax.axis_size(axis))])


def shift_both(low_edge, high_edge, axis, periodic):
    count = lax.axis_size(axis)
    forward = [(i, i + 1) for i in range(count - 1)]
    if periodic:
        forward.append((count - 1, 0))
    backward = [(target, source) for source, target in forward]
    return lax.ppermute(high_edge, axis, forward), lax.ppermute(low_edge, axis, backward)


def reversed_bits(number, count):
    result = 0
    for k in range(count):
        result |= ((number >> k) & 1) << (count - 1 - k)
    return result


def up(value, multiple):
    return -(-value // multiple) * multiple


def split_quarter(tiles, quarter):
    lane = lax.broadcasted_iota(jnp.int32, tiles[0].shape, 1)
    low = lane < LANES // 2
    first = 3 * quarter // 2
    if quarter % 2 == 0:
        return tiles[first], jnp.where(low, tiles[first + 1], 0.0)
    left = pltpu.roll(tiles[first], LANES // 2, 1)
    right = pltpu.roll(tiles[first + 1], LANES // 2, 1)
    return jnp.where(low, left, right), jnp.where(low, right, 0.0)


def join_quarters(quarters):
    lane = lax.broadcasted_iota(jnp.int32, quarters[0][0].shape, 1)
    low = lane < LANES // 2
    tiles = []
    for even in (0, 2):
        first, second = quarters[even]
        turned = pltpu.roll(quarters[even + 1][0], LANES // 2, 1)
        last = pltpu.roll(quarters[even + 1][1], LANES // 2, 1)
        tiles += [first, jnp.where(low, second, turned), jnp.where(low, turned, last)]
    return tiles


def get_rows(flat_ref, row, count):
    return [
        flat_ref[j % 2, pl.ds(3 * row + j // 2, count, stride=3), :] for j in range(TILES)
    ]


def put_rows(flat_ref, row, tiles):
    for j in range(TILES):
        flat_ref[j % 2, pl.ds(3 * row + j // 2, tiles[j].shape[0], stride=3), :] = tiles[j]


def assemble(x_ref, first, count, main, west, east, south, north, rows, cols):
    x_ref[...] = jnp.zeros_like(x_ref)
    for t in range(2):
        lanes = slice(t * LANES, min(C, (t + 1) * LANES))
        width = slice(0, lanes.stop - lanes.start)
        low = max(0, first - RAD)
        high = min(rows, first + count - RAD)
        at = slice(low + RAD - first, high + RAD - first)
        x_ref[t, at, 0:RAD, width] = west[low:high, :, lanes].astype(F32)
        x_ref[t, at, RAD : RAD + cols, width] = main[low:high, 0:cols, lanes].astype(F32)
        x_ref[t, at, RAD + cols : 2 * RAD + cols, width] = east[low:high, :, lanes].astype(F32)
        if first < RAD:
            x_ref[t, 0 : RAD - first, 0 : cols + 2 * RAD, width] = south[first:, :, lanes].astype(F32)
        over = first + count - rows - RAD
        if over > 0:
            x_ref[t, count - over : count, 0 : cols + 2 * RAD, width] = north[0:over, :, lanes].astype(F32)


def assemble_kernel(rows, cols, feat_ref, west_ref, east_ref, south_ref, north_ref, up_ref,
                    x_ref, ups_ref):
    assemble(x_ref, 0, x_ref.shape[1], feat_ref, west_ref, east_ref, south_ref, north_ref, rows, cols)
    ups_ref[...] = jnp.zeros_like(ups_ref)
    ups_ref[:, 0:cols, 0:C] = up_ref[...]


def depthwise_block(x_ref, k_ref, row, out_rows, lon_regs, store, flip):
    steps = lon_regs // 2

    def body(step, carry):
        tile = step // steps
        lon = pl.multiple_of(step % steps * 16, 16)
        sums = [None] * out_rows
        for offset in range(out_rows + KS - 1):
            for b in range(KS):
                window = x_ref[tile, row + offset, pl.ds(lon + b, 16), :]
                for r in range(out_rows):
                    a = offset - r
                    if 0 <= a < KS:
                        tap = a * KS + b
                        if flip:
                            tap = TAPS - 1 - tap
                        term = window * k_ref[tile, pl.ds(tap, 1), :]
                        sums[r] = term if sums[r] is None else sums[r] + term
        store(tile, lon, sums)
        return carry

    lax.fori_loop(0, 2 * steps, body, 0)


def layer_kernel(order, starts, rows, lon_pad, block_rows, conv_rows,
                 me_ref, gathered_ref, x_ref, up_ref,
                 out_ref, gconv_ref, gin_ref, gout_ref, sums_ref, taps_ref,
                 w_ref, win_ref, wout_ref, wo32_ref, conv_ref):
    me = me_ref[0]
    w_ref[...] = jnp.zeros_like(w_ref)
    window = gathered_ref.shape[1]
    for position, start in zip(order, starts):
        share = gathered_ref[position ^ me].astype(F32)
        for t in range(2):
            w_ref[t, pl.ds(start, window), :] += share[:, t * LANES : (t + 1) * LANES]
    rest = lax.broadcasted_iota(jnp.int32, (CP - C, LANES), 0)
    mains = get_rows(w_ref, 0, C)
    biases = get_rows(w_ref, ROW_BIAS_IN, 1)
    for j in range(TILES):
        bias = jnp.where(rest == 0, biases[j], 0.0)
        whole = jnp.concatenate([mains[j], bias], axis=0)
        win_ref[:, j * LANES : (j + 1) * LANES] = whole.astype(BF16)
    for quarter in range(4):
        pair = split_quarter(get_rows(w_ref, ROW_OUT, C), quarter)
        tail = split_quarter(get_rows(w_ref, ROW_TAPS, 16), quarter)
        for t in range(2):
            wo32_ref[t, pl.ds(quarter, C, stride=4), :] = pair[t]
            taps_ref[t, pl.ds(quarter, 16, stride=4), :] = tail[t]
    for t in range(2):
        wout_ref[:, t * LANES : (t + 1) * LANES] = wo32_ref[t].astype(BF16)

    def vector(row, quarter):
        at = (row - ROW_TAPS) * 4 + quarter
        return [taps_ref[t, pl.ds(at, 1), :] for t in range(2)]

    cbias = vector(ROW_NORM, 1)
    gain = vector(ROW_NORM, 2)
    shift = vector(ROW_NORM, 3)
    bias_out = vector(ROW_LAST, 0)
    scale = vector(ROW_LAST, 1)
    lane = lax.broadcasted_iota(jnp.int32, (1, LANES), 1)
    inside = (lane < C - LANES).astype(F32)
    shift[1] = shift[1] + (lane == C - LANES).astype(F32)

    gin_ref[...] = jnp.zeros_like(gin_ref)
    gout_ref[...] = jnp.zeros_like(gout_ref)
    sums_ref[...] = jnp.zeros_like(sums_ref)
    cells = block_rows * lon_pad

    def partial(values):
        return values.reshape(cells // 8, 8, LANES).sum(axis=0)

    def body(block, carry):
        row = block * block_rows

        def conv_step(part, carry):
            at = part * conv_rows

            def store(tile, lon, sums):
                for r in range(conv_rows):
                    conv_ref[tile, at + r, pl.ds(lon, 16), :] = sums[r]

            depthwise_block(x_ref, taps_ref, row + at, conv_rows, lon_pad // 8, store, False)
            return carry

        lax.fori_loop(0, block_rows // conv_rows, conv_step, 0)
        conv = [conv_ref[t].reshape(cells, LANES) + cbias[t] for t in range(2)]
        mean = jnp.sum(conv[0] + conv[1], axis=1, keepdims=True) * (1.0 / C)
        centred = [conv[0] - mean, (conv[1] - mean) * inside]
        square = centred[0] * centred[0] + centred[1] * centred[1]
        inv_std = lax.rsqrt(jnp.sum(square, axis=1, keepdims=True) * (1.0 / C) + EPSILON)
        standard = [c * inv_std for c in centred]
        normed = jnp.concatenate(
            [(standard[t] * gain[t] + shift[t]).astype(BF16) for t in range(2)], axis=1
        )
        upstream = up_ref[pl.ds(row, block_rows)].reshape(cells, CP)
        ups = [upstream[:, t * LANES : (t + 1) * LANES].astype(F32) for t in range(2)]
        grad_branch = [(scale[t] * ups[t]).astype(BF16) for t in range(2)]
        gbranch = jnp.concatenate(grad_branch, axis=1)
        branch = None
        gnormed = None
        for h in range(0, H, CP):
            hidden = slice(h, h + CP)
            pre = jnp.dot(normed, win_ref[:, hidden], preferred_element_type=F32)
            gact = lax.dot_general(gbranch, wout_ref[hidden, :], ALL, preferred_element_type=F32)
            square = pre * pre
            half = 0.5 + 0.5 * jnp.tanh(pre * (GELU_A + GELU_B * square))
            act = pre * half
            slope = half + act * (1.0 - half) * (2.0 * GELU_A + 6.0 * GELU_B * square)
            act = act.astype(BF16)
            gpre = (gact * slope).astype(BF16)
            part = jnp.dot(act, wout_ref[hidden, :], preferred_element_type=F32)
            branch = part if branch is None else branch + part
            part = lax.dot_general(gpre, win_ref[:, hidden], ALL, preferred_element_type=F32)
            gnormed = part if gnormed is None else gnormed + part
            gin_ref[:, hidden] += lax.dot_general(normed, gpre, OVER, preferred_element_type=F32)
            gout_ref[:, hidden] += lax.dot_general(gbranch, act, OVER, preferred_element_type=F32)
        outs = []
        gs = []
        gn = []
        for t in range(2):
            lanes = slice(t * LANES, (t + 1) * LANES)
            branch_t = branch[:, lanes] + bias_out[t]
            feat = x_ref[t, pl.ds(row + RAD, block_rows), pl.ds(RAD, lon_pad), :]
            feat = feat.reshape(cells, LANES)
            outs.append((feat + scale[t] * branch_t).astype(BF16))
            gn.append(gnormed[:, lanes])
            sums_ref[4, t] += partial(branch_t * ups[t])
            sums_ref[3, t] += partial(grad_branch[t].astype(F32))
            sums_ref[1, t] += partial(gn[t] * standard[t])
            sums_ref[2, t] += partial(gn[t])
            gs.append(gn[t] * gain[t])
        mean_g = jnp.sum(gs[0] + gs[1], axis=1, keepdims=True) * (1.0 / C)
        both = gs[0] * standard[0] + gs[1] * standard[1]
        mean_gs = jnp.sum(both, axis=1, keepdims=True) * (1.0 / C)
        gconv = []
        for t in range(2):
            grad = ((gs[t] - mean_g - standard[t] * mean_gs) * inv_std).astype(BF16)
            sums_ref[0, t] += partial(grad.astype(F32))
            gconv.append(grad)
        gconv_ref[pl.ds(row, block_rows)] = jnp.concatenate(gconv, axis=1).reshape(
            block_rows, lon_pad, CP
        )
        out = jnp.concatenate(outs, axis=1).reshape(block_rows, lon_pad, CP)
        out_ref[pl.ds(row, block_rows)] = out[:, : out_ref.shape[1], :C]
        return carry

    lax.fori_loop(0, rows // block_rows, body, 0)


def taps_kernel(order, starts, rows, lon_pad, block_rows, conv_rows,
                me_ref, gconv_ref, x_ref, gin_ref, gout_ref, sums_ref,
                g_ref, rows_ref, acc_ref, wo32_ref, small_ref):
    acc_ref[...] = jnp.zeros_like(acc_ref)

    def body(step, carry):
        tile = step % 2
        row = step // 2 * conv_rows
        lanes = pl.ds(pl.multiple_of(tile * LANES, LANES), LANES)
        grads = [gconv_ref[row + r, :, lanes].astype(F32) for r in range(conv_rows)]
        for b in range(KS):
            windows = [
                x_ref[tile, row + offset, pl.ds(b, lon_pad), :]
                for offset in range(conv_rows + KS - 1)
            ]
            for a in range(KS):
                total = None
                for r in range(conv_rows):
                    term = grads[r] * windows[r + a]
                    total = term if total is None else total + term
                acc_ref[tile, a * KS + b] += total.reshape(lon_pad // 8, 8, LANES).sum(axis=0)
        return carry

    lax.fori_loop(0, 2 * (rows // conv_rows), body, 0)
    rows_ref[...] = jnp.zeros_like(rows_ref)
    small_ref[...] = jnp.zeros_like(small_ref)
    for t in range(2):
        small_ref[t, pl.ds(0, TAPS), :] = jnp.sum(acc_ref[t], axis=1)
        for at, k in ((TAPS, 0), (TAPS + 1, 1), (TAPS + 2, 2), (TAPS + 7, 3), (TAPS + 8, 4)):
            small_ref[t, pl.ds(at, 1), :] = jnp.sum(sums_ref[k, t], axis=0, keepdims=True)
        wo32_ref[t] = gout_ref[pl.ds(t * LANES, LANES), :].T
    outs = join_quarters(
        [[wo32_ref[t, pl.ds(q, C, stride=4), :] for t in range(2)] for q in range(4)]
    )
    tails = join_quarters(
        [[small_ref[t, pl.ds(q, 16, stride=4), :] for t in range(2)] for q in range(4)]
    )
    put_rows(rows_ref, 0, [gin_ref[pl.ds(0, C), j * LANES : (j + 1) * LANES] for j in range(TILES)])
    put_rows(rows_ref, ROW_OUT, outs)
    put_rows(rows_ref, ROW_TAPS, tails)
    put_rows(
        rows_ref,
        ROW_BIAS_IN,
        [gin_ref[pl.ds(C, 1), j * LANES : (j + 1) * LANES] for j in range(TILES)],
    )
    me = me_ref[0]
    window = g_ref.shape[1]
    for position, start in zip(order, starts):
        share = [rows_ref[t, pl.ds(start, window), :] for t in range(2)]
        g_ref[position ^ me] = jnp.concatenate(share, axis=1).astype(BF16)


def field_kernel(first, count, rows, cols, lon_pad, conv_rows,
                 taps_ref, up_ref, main_ref, west_ref, east_ref, south_ref, north_ref, *rest):
    out_ref, x_ref, sum_ref = rest[-3:]
    assemble(x_ref, first, count + KS - 1, main_ref, west_ref, east_ref, south_ref, north_ref, rows, cols)

    def body(block, carry):
        row = block * conv_rows

        def store(tile, lon, sums):
            lanes = pl.ds(pl.multiple_of(tile * LANES, LANES), LANES)
            for r in range(conv_rows):
                total = sums[r] + up_ref[row + r, pl.ds(lon, 16), lanes].astype(F32)
                sum_ref[row + r, pl.ds(lon, 16), lanes] = total.astype(BF16)

        depthwise_block(x_ref, taps_ref, row, conv_rows, lon_pad // 8, store, True)
        return carry

    lax.fori_loop(0, count // conv_rows, body, 0)
    out_ref[...] = sum_ref[:, 0 : out_ref.shape[1], 0:C]


def shape(dims, kind):
    return jax.ShapeDtypeStruct(dims, kind)


def whole(count):
    return [pl.BlockSpec(memory_space=pltpu.VMEM)] * count


def halos(block, cols):
    west, east = shift_both(block[:, :RAD, :C], block[:, cols - RAD : cols, :C], "lon", True)

    def wide(rows):
        return jnp.concatenate([west[rows], block[rows, :cols, :C], east[rows]], axis=1)

    south, north = shift_both(wide(slice(0, RAD)), wide(slice(-RAD, None)), "lat", False)
    return west, east, south, north


def cost(micros):
    return pl.CostEstimate(flops=int(micros * 1.1e9), bytes_accessed=0, transcendentals=0)


def body(features, params, langevin_noise, upstream):
    rows, cols = features.shape[:2]
    lon_pad = up(cols, 16)
    lon_wide = up(lon_pad + KS - 1, 8)
    conv_rows = max(r for r in range(1, 6) if rows % r == 0)
    block_rows = max(r for r in range(1, 16) if rows % r == 0 and r % conv_rows == 0)
    axes = ("lon", "lat")
    steps = exchange_bits(axes)
    count = 1 << len(steps)
    lat_size = lax.axis_size("lat")
    length = params.shape[0]
    number = lax.axis_index("lon") * lat_size + lax.axis_index("lat")
    place = jnp.int32(0)
    for k in range(len(steps)):
        place = place | (((number >> k) & 1) << (len(steps) - 1 - k))
    place = place.reshape(1).astype(jnp.int32)
    offset = (number * length) % SHARE_LANES
    order = [reversed_bits(s, len(steps)) for s in range(count)]
    starts = [s * length // SHARE_LANES for s in range(count)]
    spill = SHARE_LANES - math.gcd(SHARE_LANES, length)
    window = up(-(-(length + spill) // SHARE_LANES), 8)
    flat_rows = up(max(starts[-1] + window, 3 * (ROWS + 1)), 8)

    share = lax.dynamic_update_slice(
        jnp.zeros((window * SHARE_LANES,), BF16), params.astype(BF16), (offset,)
    )
    gathered = share.reshape(1, window, SHARE_LANES)
    feature_halos = halos(features, cols)
    for k, (axis, bit) in enumerate(steps):
        if k == len(steps) - 2:
            gathered, upstream = lax.optimization_barrier((gathered, upstream))
        gathered = jnp.concatenate([gathered, swap(gathered, axis, bit)], axis=0)

    compiler_params = pltpu.CompilerParams(vmem_limit_bytes=VMEM)
    smem = [pl.BlockSpec(memory_space=pltpu.SMEM)]
    x, ups = pl.pallas_call(
        lambda *refs: assemble_kernel(rows, cols, *refs),
        out_shape=(
            shape((2, rows + KS - 1, lon_wide, LANES), F32),
            shape((rows, lon_pad, CP), BF16),
        ),
        in_specs=whole(6),
        out_specs=tuple(whole(2)),
        compiler_params=compiler_params,
        cost_estimate=cost(3),
        name="assemble",
    )(features, *feature_halos, upstream)

    static = (order, starts, rows, lon_pad, block_rows, conv_rows)
    output, gconv, gin, gout, sums, taps = pl.pallas_call(
        lambda *refs: layer_kernel(*static, *refs),
        out_shape=(
            shape((rows, cols, C), BF16),
            shape((rows, lon_pad, CP), BF16),
            shape((CP, H), F32),
            shape((CP, H), F32),
            shape((5, 2, 8, LANES), F32),
            shape((2, 64, LANES), F32),
        ),
        in_specs=smem + whole(3),
        out_specs=tuple(whole(6)),
        scratch_shapes=[
            pltpu.VMEM((2, flat_rows, LANES), F32),
            pltpu.VMEM((CP, H), BF16),
            pltpu.VMEM((H, CP), BF16),
            pltpu.VMEM((2, H, LANES), F32),
            pltpu.VMEM((2, block_rows, lon_pad, LANES), F32),
        ],
        compiler_params=compiler_params,
        cost_estimate=cost(22),
        name="layer",
    )(place, gathered, x, ups)

    grad_halos = halos(gconv, cols)
    values = pl.pallas_call(
        lambda *refs: taps_kernel(*static, *refs),
        out_shape=shape((count, window, SHARE_LANES), BF16),
        in_specs=smem + whole(5),
        out_specs=whole(1)[0],
        scratch_shapes=[
            pltpu.VMEM((2, flat_rows, LANES), F32),
            pltpu.VMEM((2, TAPS, 8, LANES), F32),
            pltpu.VMEM((2, H, LANES), F32),
            pltpu.VMEM((2, 64, LANES), F32),
        ],
        compiler_params=compiler_params,
        cost_estimate=cost(11),
        name="taps",
    )(place, gconv, x, gin, gout, sums)

    pieces = 3 if rows % (3 * conv_rows) == 0 else 1
    piece_rows = rows // pieces
    field = None
    for piece in range(pieces):
        before = [] if field is None else [field]
        held = [pl.BlockSpec(memory_space=pl.ANY)] * len(before)
        at = lambda i, piece=piece: (piece, 0, 0)
        field = pl.pallas_call(
            lambda *refs, piece=piece: field_kernel(
                piece * piece_rows, piece_rows, rows, cols, lon_pad, conv_rows, *refs
            ),
            grid=(1,),
            out_shape=shape((rows, cols, C), BF16),
            in_specs=whole(1)
            + [pl.BlockSpec((piece_rows, lon_pad, CP), at)]
            + whole(5)
            + held,
            out_specs=pl.BlockSpec((piece_rows, cols, C), at),
            scratch_shapes=[
                pltpu.VMEM((2, piece_rows + KS - 1, lon_wide, LANES), F32),
                pltpu.VMEM((piece_rows, lon_pad, CP), BF16),
            ],
            input_output_aliases={7: 0} if before else {},
            compiler_params=compiler_params,
            cost_estimate=cost(12 / pieces),
            name="field",
        )(taps, ups, gconv, *grad_halos, *before)

    for axis, bit in steps[::-1]:
        half = values.shape[0] // 2
        received = swap(values[half:].astype(BF16), axis, bit)
        values = values[:half].astype(F32) + received.astype(F32)
    summed = lax.dynamic_slice(values.reshape(-1), (offset,), (length,))
    new_params = params - STEP_SIZE * summed + NOISE_COEF * langevin_noise
    return (output, field, new_params)


def solution(mesh):
    return jax.shard_map(
        body,
        mesh=mesh,
        in_specs=(
            P("lat", "lon", None),
            P(("lon", "lat")),
            P(("lon", "lat")),
            P("lat", "lon", None),
        ),
        out_specs=(P("lat", "lon", None), P("lat", "lon", None), P(("lon", "lat"))),
        check_vma=False,
    )
```

```python
import math

import jax
import jax.numpy as jnp
from jax import lax
from jax.experimental import pallas as pl
from jax.experimental.pallas import tpu as pltpu
from jax.sharding import PartitionSpec as P

C = 192
H = 768
KS = 7
RAD = KS // 2
LANES = 128
CP = 256
TAPS = KS * KS
EPSILON = 1e-06
STEP_SIZE = 0.003
NOISE_COEF = 0.08
GELU_A = math.sqrt(2.0 / math.pi)
GELU_B = GELU_A * 0.044715
F32 = jnp.float32
BF16 = jnp.bfloat16
ROW_OUT = C
ROW_TAPS = 2 * C
ROW_NORM = ROW_TAPS + TAPS // 4
ROW_BIAS_IN = ROW_NORM + 1
ROW_LAST = ROW_NORM + 2
ROWS = ROW_LAST + 1
TILES = H // LANES
SHARE_LANES = 256
ALL = ((1,), (1,)), ((), ())
OVER = ((0,), (0,)), ((), ())
VMEM = 28 << 20


def exchange_bits(axes):
    steps = []
    for axis in axes:
        bit = lax.axis_size(axis) // 2
        while bit:
            steps.append((axis, bit))
            bit //= 2
    return steps


def swap(values, axis, bit):
    return lax.ppermute(values, axis, [(i, i ^ bit) for i in range(lax.axis_size(axis))])


def shift_both(low_edge, high_edge, axis, periodic):
    count = lax.axis_size(axis)
    forward = [(i, i + 1) for i in range(count - 1)]
    if periodic:
        forward.append((count - 1, 0))
    backward = [(target, source) for source, target in forward]
    return lax.ppermute(high_edge, axis, forward), lax.ppermute(low_edge, axis, backward)


def reversed_bits(number, count):
    result = 0
    for k in range(count):
        result |= ((number >> k) & 1) << (count - 1 - k)
    return result


def up(value, multiple):
    return -(-value // multiple) * multiple


def split_quarter(tiles, quarter):
    lane = lax.broadcasted_iota(jnp.int32, tiles[0].shape, 1)
    low = lane < LANES // 2
    first = 3 * quarter // 2
    if quarter % 2 == 0:
        return tiles[first], jnp.where(low, tiles[first + 1], 0.0)
    left = pltpu.roll(tiles[first], LANES // 2, 1)
    right = pltpu.roll(tiles[first + 1], LANES // 2, 1)
    return jnp.where(low, left, right), jnp.where(low, right, 0.0)


def join_quarters(quarters):
    lane = lax.broadcasted_iota(jnp.int32, quarters[0][0].shape, 1)
    low = lane < LANES // 2
    tiles = []
    for even in (0, 2):
        first, second = quarters[even]
        turned = pltpu.roll(quarters[even + 1][0], LANES // 2, 1)
        last = pltpu.roll(quarters[even + 1][1], LANES // 2, 1)
        tiles += [first, jnp.where(low, second, turned), jnp.where(low, turned, last)]
    return tiles


def get_rows(flat_ref, row, count):
    return [
        flat_ref[j % 2, pl.ds(3 * row + j // 2, count, stride=3), :] for j in range(TILES)
    ]


def put_rows(flat_ref, row, tiles):
    for j in range(TILES):
        flat_ref[j % 2, pl.ds(3 * row + j // 2, tiles[j].shape[0], stride=3), :] = tiles[j]


def assemble(x_ref, first, count, main, west, east, south, north, rows, cols):
    x_ref[...] = jnp.zeros_like(x_ref)
    for t in range(2):
        lanes = slice(t * LANES, min(C, (t + 1) * LANES))
        width = slice(0, lanes.stop - lanes.start)
        low = max(0, first - RAD)
        high = min(rows, first + count - RAD)
        at = slice(low + RAD - first, high + RAD - first)
        x_ref[t, at, 0:RAD, width] = west[low:high, :, lanes].astype(F32)
        x_ref[t, at, RAD : RAD + cols, width] = main[low:high, 0:cols, lanes].astype(F32)
        x_ref[t, at, RAD + cols : 2 * RAD + cols, width] = east[low:high, :, lanes].astype(F32)
        if first < RAD:
            x_ref[t, 0 : RAD - first, 0 : cols + 2 * RAD, width] = south[first:, :, lanes].astype(F32)
        over = first + count - rows - RAD
        if over > 0:
            x_ref[t, count - over : count, 0 : cols + 2 * RAD, width] = north[0:over, :, lanes].astype(F32)


def assemble_kernel(rows, cols, conv_rows, feat_ref, west_ref, east_ref, south_ref, north_ref, up_ref,
                    v_ref, feats_ref, ups_ref, x_ref):
    assemble(x_ref, 0, x_ref.shape[1], feat_ref, west_ref, east_ref, south_ref, north_ref, rows, cols)
    write_points(x_ref, v_ref, rows // conv_rows, conv_rows)
    feats_ref[...] = jnp.zeros_like(feats_ref)
    feats_ref[:, 0:cols, 0:C] = feat_ref[...]
    ups_ref[...] = jnp.zeros_like(ups_ref)
    ups_ref[:, 0:cols, 0:C] = up_ref[...]


def points_for(out_rows):
    pairs = [1.0, 0.5, 2.0, 1.5, 0.75][: (out_rows + KS - 2) // 2]
    points = [0.0] + [sign * p for p in pairs for sign in (1.0, -1.0)]
    filters = []
    for k, point in enumerate(points):
        scale = math.prod(point - other for i, other in enumerate(points) if i != k)
        filters.append([point**a / scale for a in range(KS)])
    return pairs, filters


def polynomial(roots):
    coefs = [1.0]
    for root in roots:
        coefs = [
            (coefs[i - 1] if i else 0.0) - (root * coefs[i] if i < len(coefs) else 0.0)
            for i in range(len(coefs) + 1)
        ]
    return coefs


def weighted(coefs, values):
    total = None
    for coef, value in zip(coefs, values):
        if coef == 0.0:
            continue
        term = value if coef == 1.0 else value * coef
        total = term if total is None else total + term
    return total


def data_points(pairs, rows):
    squares = [p * p for p in pairs]
    values = [weighted(polynomial(squares), rows[0::2])]
    for p in pairs:
        coefs = polynomial([q for q in squares if q != p * p])
        even = weighted(coefs, rows[2::2])
        odd = weighted([p * c for c in coefs], rows[1::2])
        values += [even + odd, even - odd]
    return values


def grad_points(pairs, rows):
    values = [rows[0]]
    for p in pairs:
        even = weighted([p ** (2 * i) for i in range(len(rows[0::2]))], rows[0::2])
        odd = weighted([p ** (2 * i + 1) for i in range(len(rows[1::2]))], rows[1::2])
        values += [even + odd, even - odd] if odd is not None else [even, even]
    return values


def write_points(x_ref, v_ref, blocks, out_rows):
    pairs, filters = points_for(out_rows)
    count = len(filters)
    lon_regs = x_ref.shape[2] // 8

    def body(step, carry):
        tile = step // lon_regs
        lon = pl.ds(pl.multiple_of(step % lon_regs * 8, 8), 8)

        def block(k, carry):
            rows = [x_ref[tile, k * out_rows + r, lon, :] for r in range(count)]
            for i, value in enumerate(data_points(pairs, rows)):
                v_ref[tile, k * count + i, lon, :] = value
            return carry

        return lax.fori_loop(0, blocks, block, carry, unroll=3 if blocks % 3 == 0 else 1)

    lax.fori_loop(0, 2 * lon_regs, body, 0)


def filter_points(taps_ref, out_rows, u_ref, flip):
    for k, coefs in enumerate(points_for(out_rows)[1]):
        coefs = coefs[::-1] if flip else coefs
        for t in range(2):
            u_ref[t, k, 0:KS, :] = weighted(
                coefs, [taps_ref[t, pl.ds(a * KS, KS), :] for a in range(KS)]
            )


def depthwise_block(v_ref, u_ref, block, out_rows, lon_pad, store, flip):
    pairs, filters = points_for(out_rows)
    count = len(filters)
    chunk = lon_pad // 2 if lon_pad % 16 == 0 else lon_pad

    def body(step, carry):
        tile = step // (lon_pad // chunk)
        lon = pl.multiple_of(step % (lon_pad // chunk) * chunk, 8)

        def product(k):
            total = None
            for b in range(KS):
                tap = KS - 1 - b if flip else b
                term = v_ref[tile, block * count + k, pl.ds(lon + b, chunk), :]
                term = term * u_ref[tile, k, pl.ds(tap, 1), :]
                total = term if total is None else total + term
            return total

        sums = [None] * out_rows
        sums[0] = product(0)
        for i, p in enumerate(pairs):
            plus, minus = product(2 * i + 1), product(2 * i + 2)
            even, odd = plus + minus, plus - minus
            for r in range(out_rows):
                term = odd if r % 2 else even
                term = term if p**r == 1.0 else term * p**r
                sums[r] = term if sums[r] is None else sums[r] + term
        store(tile, lon, chunk, sums)
        return carry

    lax.fori_loop(0, 2 * (lon_pad // chunk), body, 0)


def layer_kernel(order, starts, rows, lon_pad, block_rows, conv_rows,
                 me_ref, gathered_ref, v_ref, feat_ref, up_ref,
                 out_ref, gconv_ref, gin_ref, gout_ref, sums_ref, flipped_ref,
                 u_ref, taps_ref, w_ref, win_ref, wout_ref, wo32_ref, conv_ref):
    me = me_ref[0]
    w_ref[...] = jnp.zeros_like(w_ref)
    window = gathered_ref.shape[1]
    for position, start in zip(order, starts):
        share = gathered_ref[position ^ me].astype(F32)
        for t in range(2):
            w_ref[t, pl.ds(start, window), :] += share[:, t * LANES : (t + 1) * LANES]
    rest = lax.broadcasted_iota(jnp.int32, (CP - C, LANES), 0)
    mains = get_rows(w_ref, 0, C)
    biases = get_rows(w_ref, ROW_BIAS_IN, 1)
    for j in range(TILES):
        bias = jnp.where(rest == 0, biases[j], 0.0)
        whole = jnp.concatenate([mains[j], bias], axis=0)
        win_ref[:, j * LANES : (j + 1) * LANES] = whole.astype(BF16)
    for quarter in range(4):
        pair = split_quarter(get_rows(w_ref, ROW_OUT, C), quarter)
        tail = split_quarter(get_rows(w_ref, ROW_TAPS, 16), quarter)
        for t in range(2):
            wo32_ref[t, pl.ds(quarter, C, stride=4), :] = pair[t]
            taps_ref[t, pl.ds(quarter, 16, stride=4), :] = tail[t]
    for t in range(2):
        wout_ref[:, t * LANES : (t + 1) * LANES] = wo32_ref[t].astype(BF16)

    def vector(row, quarter):
        at = (row - ROW_TAPS) * 4 + quarter
        return [taps_ref[t, pl.ds(at, 1), :] for t in range(2)]

    filter_points(taps_ref, conv_rows, u_ref, False)
    filter_points(taps_ref, conv_rows, flipped_ref, True)
    cbias = vector(ROW_NORM, 1)
    gain = vector(ROW_NORM, 2)
    shift = vector(ROW_NORM, 3)
    bias_out = vector(ROW_LAST, 0)
    scale = vector(ROW_LAST, 1)
    lane = lax.broadcasted_iota(jnp.int32, (1, LANES), 1)
    inside = (lane < C - LANES).astype(F32)
    shift[1] = shift[1] + (lane == C - LANES).astype(F32)

    gin_ref[...] = jnp.zeros_like(gin_ref)
    gout_ref[...] = jnp.zeros_like(gout_ref)
    sums_ref[...] = jnp.zeros_like(sums_ref)
    cells = block_rows * lon_pad

    def partial(values):
        return values.reshape(cells // 8, 8, LANES).sum(axis=0)

    def body(block, carry):
        row = block * block_rows

        def conv_step(part, carry):
            at = part * conv_rows

            def store(tile, lon, chunk, sums):
                for r in range(conv_rows):
                    conv_ref[tile, at + r, pl.ds(lon, chunk), :] = sums[r]

            at_block = block * (block_rows // conv_rows) + part
            depthwise_block(v_ref, u_ref, at_block, conv_rows, lon_pad, store, False)
            return carry

        lax.fori_loop(0, block_rows // conv_rows, conv_step, 0)
        conv = [conv_ref[t].reshape(cells, LANES) + cbias[t] for t in range(2)]
        mean = jnp.sum(conv[0] + conv[1], axis=1, keepdims=True) * (1.0 / C)
        centred = [conv[0] - mean, (conv[1] - mean) * inside]
        square = centred[0] * centred[0] + centred[1] * centred[1]
        inv_std = lax.rsqrt(jnp.sum(square, axis=1, keepdims=True) * (1.0 / C) + EPSILON)
        standard = [c * inv_std for c in centred]
        normed = jnp.concatenate(
            [(standard[t] * gain[t] + shift[t]).astype(BF16) for t in range(2)], axis=1
        )
        upstream = up_ref[pl.ds(row, block_rows)].reshape(cells, CP)
        ups = [upstream[:, t * LANES : (t + 1) * LANES].astype(F32) for t in range(2)]
        grad_branch = [(scale[t] * ups[t]).astype(BF16) for t in range(2)]
        gbranch = jnp.concatenate(grad_branch, axis=1)
        branch = None
        gnormed = None
        for h in range(0, H, CP):
            hidden = slice(h, h + CP)
            pre = jnp.dot(normed, win_ref[:, hidden], preferred_element_type=F32)
            gact = lax.dot_general(gbranch, wout_ref[hidden, :], ALL, preferred_element_type=F32)
            square = pre * pre
            half = 0.5 + 0.5 * jnp.tanh(pre * (GELU_A + GELU_B * square))
            act = pre * half
            slope = half + act * (1.0 - half) * (2.0 * GELU_A + 6.0 * GELU_B * square)
            act = act.astype(BF16)
            gpre = (gact * slope).astype(BF16)
            part = jnp.dot(act, wout_ref[hidden, :], preferred_element_type=F32)
            branch = part if branch is None else branch + part
            part = lax.dot_general(gpre, win_ref[:, hidden], ALL, preferred_element_type=F32)
            gnormed = part if gnormed is None else gnormed + part
            gin_ref[:, hidden] += lax.dot_general(normed, gpre, OVER, preferred_element_type=F32)
            gout_ref[:, hidden] += lax.dot_general(gbranch, act, OVER, preferred_element_type=F32)
        outs = []
        gs = []
        gn = []
        for t in range(2):
            lanes = slice(t * LANES, (t + 1) * LANES)
            branch_t = branch[:, lanes] + bias_out[t]
            feat = feat_ref[pl.ds(row, block_rows), :, lanes].reshape(cells, LANES).astype(F32)
            outs.append((feat + scale[t] * branch_t).astype(BF16))
            gn.append(gnormed[:, lanes])
            sums_ref[4, t] += partial(branch_t * ups[t])
            sums_ref[3, t] += partial(grad_branch[t].astype(F32))
            sums_ref[1, t] += partial(gn[t] * standard[t])
            sums_ref[2, t] += partial(gn[t])
            gs.append(gn[t] * gain[t])
        mean_g = jnp.sum(gs[0] + gs[1], axis=1, keepdims=True) * (1.0 / C)
        both = gs[0] * standard[0] + gs[1] * standard[1]
        mean_gs = jnp.sum(both, axis=1, keepdims=True) * (1.0 / C)
        gconv = []
        for t in range(2):
            grad = ((gs[t] - mean_g - standard[t] * mean_gs) * inv_std).astype(BF16)
            sums_ref[0, t] += partial(grad.astype(F32))
            gconv.append(grad)
        gconv_ref[pl.ds(row, block_rows)] = jnp.concatenate(gconv, axis=1).reshape(
            block_rows, lon_pad, CP
        )
        out = jnp.concatenate(outs, axis=1).reshape(block_rows, lon_pad, CP)
        out_ref[pl.ds(row, block_rows)] = out[:, : out_ref.shape[1], :C]
        return carry

    lax.fori_loop(0, rows // block_rows, body, 0)


def taps_kernel(order, starts, rows, lon_pad, block_rows, conv_rows,
                me_ref, gconv_ref, v_ref, gin_ref, gout_ref, sums_ref,
                g_ref, rows_ref, acc_ref, wo32_ref, small_ref):
    acc_ref[...] = jnp.zeros_like(acc_ref)
    pairs, filters = points_for(conv_rows)
    count = len(filters)

    def body(step, carry):
        tile = step % 2
        block = step // 2
        lanes = pl.ds(pl.multiple_of(tile * LANES, LANES), LANES)
        grads = grad_points(
            pairs,
            [gconv_ref[block * conv_rows + r, :, lanes].astype(F32) for r in range(conv_rows)],
        )
        for k in range(count):
            for b in range(KS):
                term = grads[k] * v_ref[tile, block * count + k, pl.ds(b, lon_pad), :]
                acc_ref[tile, k, b] += term.reshape(lon_pad // 8, 8, LANES).sum(axis=0)
        return carry

    lax.fori_loop(0, 2 * (rows // conv_rows), body, 0)
    rows_ref[...] = jnp.zeros_like(rows_ref)
    small_ref[...] = jnp.zeros_like(small_ref)
    for t in range(2):
        totals = [jnp.sum(acc_ref[t, k], axis=1) for k in range(count)]
        for a in range(KS):
            small_ref[t, pl.ds(a * KS, KS), :] = weighted([f[a] for f in filters], totals)
        for at, k in ((TAPS, 0), (TAPS + 1, 1), (TAPS + 2, 2), (TAPS + 7, 3), (TAPS + 8, 4)):
            small_ref[t, pl.ds(at, 1), :] = jnp.sum(sums_ref[k, t], axis=0, keepdims=True)
        wo32_ref[t] = gout_ref[pl.ds(t * LANES, LANES), :].T
    outs = join_quarters(
        [[wo32_ref[t, pl.ds(q, C, stride=4), :] for t in range(2)] for q in range(4)]
    )
    tails = join_quarters(
        [[small_ref[t, pl.ds(q, 16, stride=4), :] for t in range(2)] for q in range(4)]
    )
    put_rows(rows_ref, 0, [gin_ref[pl.ds(0, C), j * LANES : (j + 1) * LANES] for j in range(TILES)])
    put_rows(rows_ref, ROW_OUT, outs)
    put_rows(rows_ref, ROW_TAPS, tails)
    put_rows(
        rows_ref,
        ROW_BIAS_IN,
        [gin_ref[pl.ds(C, 1), j * LANES : (j + 1) * LANES] for j in range(TILES)],
    )
    me = me_ref[0]
    window = g_ref.shape[1]
    for position, start in zip(order, starts):
        share = [rows_ref[t, pl.ds(start, window), :] for t in range(2)]
        g_ref[position ^ me] = jnp.concatenate(share, axis=1).astype(BF16)


def field_kernel(first, count, rows, cols, lon_pad, conv_rows,
                 u_ref, up_ref, main_ref, west_ref, east_ref, south_ref, north_ref, *rest):
    out_ref, x_ref, v_ref, sum_ref = rest[-4:]
    assemble(x_ref, first, count + KS - 1, main_ref, west_ref, east_ref, south_ref, north_ref, rows, cols)
    write_points(x_ref, v_ref, count // conv_rows, conv_rows)

    def body(block, carry):
        row = block * conv_rows

        def store(tile, lon, chunk, sums):
            lanes = pl.ds(pl.multiple_of(tile * LANES, LANES), LANES)
            for r in range(conv_rows):
                total = sums[r] + up_ref[row + r, pl.ds(lon, chunk), lanes].astype(F32)
                sum_ref[row + r, pl.ds(lon, chunk), lanes] = total

        depthwise_block(v_ref, u_ref, block, conv_rows, lon_pad, store, True)
        return carry

    lax.fori_loop(0, count // conv_rows, body, 0)
    out_ref[...] = sum_ref[:, 0 : out_ref.shape[1], 0:C].astype(BF16)


def shape(dims, kind):
    return jax.ShapeDtypeStruct(dims, kind)


def whole(count):
    return [pl.BlockSpec(memory_space=pltpu.VMEM)] * count


def halos(block, cols):
    west, east = shift_both(block[:, :RAD, :C], block[:, cols - RAD : cols, :C], "lon", True)

    def wide(rows):
        return jnp.concatenate([west[rows], block[rows, :cols, :C], east[rows]], axis=1)

    south, north = shift_both(wide(slice(0, RAD)), wide(slice(-RAD, None)), "lat", False)
    return west, east, south, north


def cost(micros):
    return pl.CostEstimate(flops=int(micros * 1.1e9), bytes_accessed=0, transcendentals=0)


def body(features, params, langevin_noise, upstream):
    rows, cols = features.shape[:2]
    lon_pad = up(cols, 16)
    lon_wide = up(lon_pad + KS - 1, 8)
    conv_rows = max(r for r in (1, 3, 5) if rows % r == 0)
    points = conv_rows + KS - 1
    blocks = rows // conv_rows
    block_rows = max(r for r in range(1, 16) if rows % r == 0 and r % conv_rows == 0)
    axes = ("lon", "lat")
    steps = exchange_bits(axes)
    count = 1 << len(steps)
    lat_size = lax.axis_size("lat")
    length = params.shape[0]
    number = lax.axis_index("lon") * lat_size + lax.axis_index("lat")
    place = jnp.int32(0)
    for k in range(len(steps)):
        place = place | (((number >> k) & 1) << (len(steps) - 1 - k))
    place = place.reshape(1).astype(jnp.int32)
    offset = (number * length) % SHARE_LANES
    order = [reversed_bits(s, len(steps)) for s in range(count)]
    starts = [s * length // SHARE_LANES for s in range(count)]
    spill = SHARE_LANES - math.gcd(SHARE_LANES, length)
    window = up(-(-(length + spill) // SHARE_LANES), 8)
    flat_rows = up(max(starts[-1] + window, 3 * (ROWS + 1)), 8)

    share = lax.dynamic_update_slice(
        jnp.zeros((window * SHARE_LANES,), BF16), params.astype(BF16), (offset,)
    )
    gathered = share.reshape(1, window, SHARE_LANES)
    feature_halos = halos(features, cols)
    for k, (axis, bit) in enumerate(steps):
        if k == len(steps) - 2:
            gathered, upstream = lax.optimization_barrier((gathered, upstream))
        gathered = jnp.concatenate([gathered, swap(gathered, axis, bit)], axis=0)

    compiler_params = pltpu.CompilerParams(vmem_limit_bytes=VMEM)
    smem = [pl.BlockSpec(memory_space=pltpu.SMEM)]
    data, feats, ups = pl.pallas_call(
        lambda *refs: assemble_kernel(rows, cols, conv_rows, *refs),
        out_shape=(
            shape((2, blocks * points, lon_wide, LANES), F32),
            shape((rows, lon_pad, CP), BF16),
            shape((rows, lon_pad, CP), BF16),
        ),
        in_specs=whole(6),
        out_specs=tuple(whole(3)),
        scratch_shapes=[pltpu.VMEM((2, rows + KS - 1, lon_wide, LANES), F32)],
        compiler_params=compiler_params,
        cost_estimate=cost(3),
        name="assemble",
    )(features, *feature_halos, upstream)

    static = (order, starts, rows, lon_pad, block_rows, conv_rows)
    output, gconv, gin, gout, sums, flipped = pl.pallas_call(
        lambda *refs: layer_kernel(*static, *refs),
        out_shape=(
            shape((rows, cols, C), BF16),
            shape((rows, lon_pad, CP), BF16),
            shape((CP, H), F32),
            shape((CP, H), F32),
            shape((5, 2, 8, LANES), F32),
            shape((2, points, 8, LANES), F32),
        ),
        in_specs=smem + whole(4),
        out_specs=tuple(whole(6)),
        scratch_shapes=[
            pltpu.VMEM((2, points, 8, LANES), F32),
            pltpu.VMEM((2, 64, LANES), F32),
            pltpu.VMEM((2, flat_rows, LANES), F32),
            pltpu.VMEM((CP, H), BF16),
            pltpu.VMEM((H, CP), BF16),
            pltpu.VMEM((2, H, LANES), F32),
            pltpu.VMEM((2, block_rows, lon_pad, LANES), F32),
        ],
        compiler_params=compiler_params,
        cost_estimate=cost(22),
        name="layer",
    )(place, gathered, data, feats, ups)

    grad_halos = halos(gconv, cols)
    values = pl.pallas_call(
        lambda *refs: taps_kernel(*static, *refs),
        out_shape=shape((count, window, SHARE_LANES), BF16),
        in_specs=smem + whole(5),
        out_specs=whole(1)[0],
        scratch_shapes=[
            pltpu.VMEM((2, flat_rows, LANES), F32),
            pltpu.VMEM((2, points, KS, 8, LANES), F32),
            pltpu.VMEM((2, H, LANES), F32),
            pltpu.VMEM((2, 64, LANES), F32),
        ],
        compiler_params=compiler_params,
        cost_estimate=cost(11),
        name="taps",
    )(place, gconv, data, gin, gout, sums)

    pieces = 3 if rows % (3 * conv_rows) == 0 else 1
    piece_rows = rows // pieces
    field = None
    for piece in range(pieces):
        before = [] if field is None else [field]
        held = [pl.BlockSpec(memory_space=pl.ANY)] * len(before)
        at = lambda i, piece=piece: (piece, 0, 0)
        field = pl.pallas_call(
            lambda *refs, piece=piece: field_kernel(
                piece * piece_rows, piece_rows, rows, cols, lon_pad, conv_rows, *refs
            ),
            grid=(1,),
            out_shape=shape((rows, cols, C), BF16),
            in_specs=whole(1)
            + [pl.BlockSpec((piece_rows, lon_pad, CP), at)]
            + whole(5)
            + held,
            out_specs=pl.BlockSpec((piece_rows, cols, C), at),
            scratch_shapes=[
                pltpu.VMEM((2, piece_rows + KS - 1, lon_wide, LANES), F32),
                pltpu.VMEM((2, piece_rows // conv_rows * points, lon_wide, LANES), F32),
                pltpu.VMEM((piece_rows, lon_pad, CP), F32),
            ],
            input_output_aliases={7: 0} if before else {},
            compiler_params=compiler_params,
            cost_estimate=cost(12 / pieces),
            name="field",
        )(flipped, ups, gconv, *grad_halos, *before)

    for axis, bit in steps[::-1]:
        half = values.shape[0] // 2
        received = swap(values[half:].astype(BF16), axis, bit)
        values = values[:half].astype(F32) + received.astype(F32)
    summed = lax.dynamic_slice(values.reshape(-1), (offset,), (length,))
    new_params = params - STEP_SIZE * summed + NOISE_COEF * langevin_noise
    return (output, field, new_params)


def solution(mesh):
    return jax.shard_map(
        body,
        mesh=mesh,
        in_specs=(
            P("lat", "lon", None),
            P(("lon", "lat")),
            P(("lon", "lat")),
            P("lat", "lon", None),
        ),
        out_specs=(P("lat", "lon", None), P("lat", "lon", None), P(("lon", "lat"))),
        check_vma=False,
    )
```

```python
import math

import jax
import jax.numpy as jnp
from jax import lax
from jax.experimental import pallas as pl
from jax.experimental.pallas import tpu as pltpu
from jax.sharding import PartitionSpec as P

C = 192
H = 768
KS = 7
RAD = KS // 2
LANES = 128
CP = 256
TAPS = KS * KS
EPSILON = 1e-06
STEP_SIZE = 0.003
NOISE_COEF = 0.08
GELU_A = math.sqrt(2.0 / math.pi)
GELU_B = GELU_A * 0.044715
F32 = jnp.float32
BF16 = jnp.bfloat16
ROW_OUT = C
ROW_TAPS = 2 * C
ROW_NORM = ROW_TAPS + TAPS // 4
ROW_BIAS_IN = ROW_NORM + 1
ROW_LAST = ROW_NORM + 2
ROWS = ROW_LAST + 1
TILES = H // LANES
SHARE_LANES = 256
ALL = ((1,), (1,)), ((), ())
OVER = ((0,), (0,)), ((), ())
VMEM = 28 << 20


def exchange_groups():
    lon, lat = lax.axis_size("lon"), lax.axis_size("lat")
    bits = [(lon >> k, 0) for k in range(1, lon.bit_length())]
    bits += [(0, lat >> k) for k in range(1, lat.bit_length())]
    groups = []
    k = 0
    while k < len(bits):
        if k + 1 < len(bits) and bits[k][0] == 1 and bits[k + 1][0] == 0:
            (lon_bit, _), (_, lat_bit) = bits[k : k + 2]
            groups.append([(lon_bit, 0), (0, lat_bit), (lon_bit, lat_bit)])
            k += 2
        else:
            groups.append([bits[k]])
            k += 1
    return groups, len(bits)


def swap(values, mask):
    lon, lat = lax.axis_size("lon"), lax.axis_size("lat")
    pairs = [
        (i * lat + j, (i ^ mask[0]) * lat + (j ^ mask[1])) for i in range(lon) for j in range(lat)
    ]
    return lax.ppermute(values, ("lon", "lat"), pairs)


def shift_both(low_edge, high_edge, axis, periodic):
    count = lax.axis_size(axis)
    if count % 2:
        forward = [(i, (i + 1) % count) for i in range(count if periodic else count - 1)]
        backward = [(target, source) for source, target in forward]
        return lax.ppermute(high_edge, axis, forward), lax.ppermute(low_edge, axis, backward)
    even = lax.axis_index(axis) % 2 == 0
    near = [(i, i ^ 1) for i in range(count)]
    odds = [(i, (i + 1) % count) for i in range(1, count if periodic else count - 1, 2)]
    far = odds + [(target, source) for source, target in odds]
    near = lax.ppermute(jnp.where(even, high_edge, low_edge), axis, near)
    far = lax.ppermute(jnp.where(even, low_edge, high_edge), axis, far)
    return jnp.where(even, far, near), jnp.where(even, near, far)


def reversed_bits(number, count):
    result = 0
    for k in range(count):
        result |= ((number >> k) & 1) << (count - 1 - k)
    return result


def up(value, multiple):
    return -(-value // multiple) * multiple


def split_quarter(tiles, quarter):
    lane = lax.broadcasted_iota(jnp.int32, tiles[0].shape, 1)
    low = lane < LANES // 2
    first = 3 * quarter // 2
    if quarter % 2 == 0:
        return tiles[first], jnp.where(low, tiles[first + 1], 0.0)
    left = pltpu.roll(tiles[first], LANES // 2, 1)
    right = pltpu.roll(tiles[first + 1], LANES // 2, 1)
    return jnp.where(low, left, right), jnp.where(low, right, 0.0)


def join_quarters(quarters):
    lane = lax.broadcasted_iota(jnp.int32, quarters[0][0].shape, 1)
    low = lane < LANES // 2
    tiles = []
    for even in (0, 2):
        first, second = quarters[even]
        turned = pltpu.roll(quarters[even + 1][0], LANES // 2, 1)
        last = pltpu.roll(quarters[even + 1][1], LANES // 2, 1)
        tiles += [first, jnp.where(low, second, turned), jnp.where(low, turned, last)]
    return tiles


def get_rows(flat_ref, row, count):
    return [
        flat_ref[j % 2, pl.ds(3 * row + j // 2, count, stride=3), :] for j in range(TILES)
    ]


def put_rows(flat_ref, row, tiles):
    for j in range(TILES):
        flat_ref[j % 2, pl.ds(3 * row + j // 2, tiles[j].shape[0], stride=3), :] = tiles[j]


def assemble(x_ref, first, count, main, west, east, south, north, rows, cols):
    x_ref[...] = jnp.zeros_like(x_ref)
    for t in range(2):
        lanes = slice(t * LANES, min(C, (t + 1) * LANES))
        width = slice(0, lanes.stop - lanes.start)
        low = max(0, first - RAD)
        high = min(rows, first + count - RAD)
        at = slice(low + RAD - first, high + RAD - first)
        x_ref[t, at, 0:RAD, width] = west[low:high, :, lanes].astype(F32)
        x_ref[t, at, RAD : RAD + cols, width] = main[low:high, 0:cols, lanes].astype(F32)
        x_ref[t, at, RAD + cols : 2 * RAD + cols, width] = east[low:high, :, lanes].astype(F32)
        if first < RAD:
            x_ref[t, 0 : RAD - first, 0 : cols + 2 * RAD, width] = south[first:, :, lanes].astype(F32)
        over = first + count - rows - RAD
        if over > 0:
            x_ref[t, count - over : count, 0 : cols + 2 * RAD, width] = north[0:over, :, lanes].astype(F32)


def edge_kernel(cols, field_hbm, west_ref, east_ref, field_ref):
    pltpu.sync_copy(field_hbm, field_ref)
    west_ref[...] = field_ref[:, 0:RAD, :]
    east_ref[...] = field_ref[:, cols - RAD : cols, :]


def wide_kernel(rows, cols, field_ref, west_ref, east_ref, south_ref, north_ref):
    for out_ref, first in ((south_ref, 0), (north_ref, rows - RAD)):
        at = slice(first, first + RAD)
        out_ref[:, 0:RAD, :] = west_ref[at]
        out_ref[:, RAD : RAD + cols, :] = field_ref[at, 0:cols, :]
        out_ref[:, RAD + cols : 2 * RAD + cols, :] = east_ref[at]


def assemble_kernel(rows, cols, conv_rows, feat_ref, west_ref, east_ref, south_ref, north_ref, up_ref,
                    v_ref, feats_ref, ups_ref, x_ref):
    assemble(x_ref, 0, x_ref.shape[1], feat_ref, west_ref, east_ref, south_ref, north_ref, rows, cols)
    write_points(x_ref, v_ref, rows // conv_rows, conv_rows)
    feats_ref[...] = jnp.zeros_like(feats_ref)
    feats_ref[:, 0:cols, 0:C] = feat_ref[...]
    ups_ref[...] = jnp.zeros_like(ups_ref)
    ups_ref[:, 0:cols, 0:C] = up_ref[...]


def points_for(out_rows):
    pairs = [1.0, 0.5, 2.0, 1.5, 0.75][: (out_rows + KS - 2) // 2]
    points = [0.0] + [sign * p for p in pairs for sign in (1.0, -1.0)]
    filters = []
    for k, point in enumerate(points):
        scale = math.prod(point - other for i, other in enumerate(points) if i != k)
        filters.append([point**a / scale for a in range(KS)])
    return pairs, filters


def polynomial(roots):
    coefs = [1.0]
    for root in roots:
        coefs = [
            (coefs[i - 1] if i else 0.0) - (root * coefs[i] if i < len(coefs) else 0.0)
            for i in range(len(coefs) + 1)
        ]
    return coefs


def weighted(coefs, values):
    total = None
    for coef, value in zip(coefs, values):
        if coef == 0.0:
            continue
        term = value if coef == 1.0 else value * coef
        total = term if total is None else total + term
    return total


def data_points(pairs, rows):
    squares = [p * p for p in pairs]
    values = [weighted(polynomial(squares), rows[0::2])]
    for p in pairs:
        coefs = polynomial([q for q in squares if q != p * p])
        even = weighted(coefs, rows[2::2])
        odd = weighted([p * c for c in coefs], rows[1::2])
        values += [even + odd, even - odd]
    return values


def grad_points(pairs, rows):
    values = [rows[0]]
    for p in pairs:
        even = weighted([p ** (2 * i) for i in range(len(rows[0::2]))], rows[0::2])
        odd = weighted([p ** (2 * i + 1) for i in range(len(rows[1::2]))], rows[1::2])
        values += [even + odd, even - odd] if odd is not None else [even, even]
    return values


def write_points(x_ref, v_ref, blocks, out_rows):
    pairs, filters = points_for(out_rows)
    count = len(filters)
    lon_regs = x_ref.shape[2] // 8

    def body(step, carry):
        tile = step // lon_regs
        lon = pl.ds(pl.multiple_of(step % lon_regs * 8, 8), 8)

        def block(k, carry):
            rows = [x_ref[tile, k * out_rows + r, lon, :] for r in range(count)]
            for i, value in enumerate(data_points(pairs, rows)):
                v_ref[tile, k * count + i, lon, :] = value
            return carry

        return lax.fori_loop(0, blocks, block, carry, unroll=3 if blocks % 3 == 0 else 1)

    lax.fori_loop(0, 2 * lon_regs, body, 0)


def filter_points(taps_ref, out_rows, u_ref, flip):
    for k, coefs in enumerate(points_for(out_rows)[1]):
        coefs = coefs[::-1] if flip else coefs
        for t in range(2):
            u_ref[t, k, 0:KS, :] = weighted(
                coefs, [taps_ref[t, pl.ds(a * KS, KS), :] for a in range(KS)]
            )


def depthwise_block(v_ref, u_ref, block, out_rows, lon_pad, store, flip):
    pairs, filters = points_for(out_rows)
    count = len(filters)
    chunk = lon_pad // 2 if lon_pad % 16 == 0 else lon_pad

    def body(step, carry):
        tile = step // (lon_pad // chunk)
        lon = pl.multiple_of(step % (lon_pad // chunk) * chunk, 8)

        def product(k):
            total = None
            for b in range(KS):
                tap = KS - 1 - b if flip else b
                term = v_ref[tile, block * count + k, pl.ds(lon + b, chunk), :]
                term = term * u_ref[tile, k, pl.ds(tap, 1), :]
                total = term if total is None else total + term
            return total

        sums = [None] * out_rows
        sums[0] = product(0)
        for i, p in enumerate(pairs):
            plus, minus = product(2 * i + 1), product(2 * i + 2)
            even, odd = plus + minus, plus - minus
            for r in range(out_rows):
                term = odd if r % 2 else even
                term = term if p**r == 1.0 else term * p**r
                sums[r] = term if sums[r] is None else sums[r] + term
        store(tile, lon, chunk, sums)
        return carry

    lax.fori_loop(0, 2 * (lon_pad // chunk), body, 0)


def layer_kernel(order, starts, rows, lon_pad, block_rows, conv_rows,
                 me_ref, gathered_ref, v_ref, feat_ref, up_ref,
                 out_hbm, gconv_ref, gin_ref, gout_ref, sums_ref, flipped_ref,
                 out_ref, out_sem, u_ref, taps_ref, w_ref, win_ref, wout_ref, wo32_ref, conv_ref):
    me = me_ref[0]
    w_ref[...] = jnp.zeros_like(w_ref)
    window = gathered_ref.shape[1]
    for position, start in zip(order, starts):
        share = gathered_ref[position ^ me].astype(F32)
        for t in range(2):
            w_ref[t, pl.ds(start, window), :] += share[:, t * LANES : (t + 1) * LANES]
    rest = lax.broadcasted_iota(jnp.int32, (CP - C, LANES), 0)
    mains = get_rows(w_ref, 0, C)
    biases = get_rows(w_ref, ROW_BIAS_IN, 1)
    for j in range(TILES):
        bias = jnp.where(rest == 0, biases[j], 0.0)
        whole = jnp.concatenate([mains[j], bias], axis=0)
        win_ref[:, j * LANES : (j + 1) * LANES] = whole.astype(BF16)
    for quarter in range(4):
        pair = split_quarter(get_rows(w_ref, ROW_OUT, C), quarter)
        tail = split_quarter(get_rows(w_ref, ROW_TAPS, 16), quarter)
        for t in range(2):
            wo32_ref[t, pl.ds(quarter, C, stride=4), :] = pair[t]
            taps_ref[t, pl.ds(quarter, 16, stride=4), :] = tail[t]
    for t in range(2):
        wout_ref[:, t * LANES : (t + 1) * LANES] = wo32_ref[t].astype(BF16)

    def vector(row, quarter):
        at = (row - ROW_TAPS) * 4 + quarter
        return [taps_ref[t, pl.ds(at, 1), :] for t in range(2)]

    filter_points(taps_ref, conv_rows, u_ref, False)
    filter_points(taps_ref, conv_rows, flipped_ref, True)
    cbias = vector(ROW_NORM, 1)
    gain = vector(ROW_NORM, 2)
    shift = vector(ROW_NORM, 3)
    bias_out = vector(ROW_LAST, 0)
    scale = vector(ROW_LAST, 1)
    lane = lax.broadcasted_iota(jnp.int32, (1, LANES), 1)
    inside = (lane < C - LANES).astype(F32)
    shift[1] = shift[1] + (lane == C - LANES).astype(F32)

    gin_ref[...] = jnp.zeros_like(gin_ref)
    gout_ref[...] = jnp.zeros_like(gout_ref)
    sums_ref[...] = jnp.zeros_like(sums_ref)
    cells = block_rows * lon_pad

    def partial(values):
        return values.reshape(cells // 8, 8, LANES).sum(axis=0)

    def body(block, carry):
        row = block * block_rows

        def conv_step(part, carry):
            at = part * conv_rows

            def store(tile, lon, chunk, sums):
                for r in range(conv_rows):
                    conv_ref[tile, at + r, pl.ds(lon, chunk), :] = sums[r]

            at_block = block * (block_rows // conv_rows) + part
            depthwise_block(v_ref, u_ref, at_block, conv_rows, lon_pad, store, False)
            return carry

        lax.fori_loop(0, block_rows // conv_rows, conv_step, 0)
        conv = [conv_ref[t].reshape(cells, LANES) + cbias[t] for t in range(2)]
        mean = jnp.sum(conv[0] + conv[1], axis=1, keepdims=True) * (1.0 / C)
        centred = [conv[0] - mean, (conv[1] - mean) * inside]
        square = centred[0] * centred[0] + centred[1] * centred[1]
        inv_std = lax.rsqrt(jnp.sum(square, axis=1, keepdims=True) * (1.0 / C) + EPSILON)
        standard = [c * inv_std for c in centred]
        normed = jnp.concatenate(
            [(standard[t] * gain[t] + shift[t]).astype(BF16) for t in range(2)], axis=1
        )
        upstream = up_ref[pl.ds(row, block_rows)].reshape(cells, CP)
        ups = [upstream[:, t * LANES : (t + 1) * LANES].astype(F32) for t in range(2)]
        grad_branch = [(scale[t] * ups[t]).astype(BF16) for t in range(2)]
        gbranch = jnp.concatenate(grad_branch, axis=1)
        branch = None
        gnormed = None
        for h in range(0, H, CP):
            hidden = slice(h, h + CP)
            pre = jnp.dot(normed, win_ref[:, hidden], preferred_element_type=F32)
            gact = lax.dot_general(gbranch, wout_ref[hidden, :], ALL, preferred_element_type=F32)
            square = pre * pre
            half = 0.5 + 0.5 * jnp.tanh(pre * (GELU_A + GELU_B * square))
            act = pre * half
            slope = half + act * (1.0 - half) * (2.0 * GELU_A + 6.0 * GELU_B * square)
            act = act.astype(BF16)
            gpre = (gact * slope).astype(BF16)
            part = jnp.dot(act, wout_ref[hidden, :], preferred_element_type=F32)
            branch = part if branch is None else branch + part
            part = lax.dot_general(gpre, win_ref[:, hidden], ALL, preferred_element_type=F32)
            gnormed = part if gnormed is None else gnormed + part
            gin_ref[:, hidden] += lax.dot_general(normed, gpre, OVER, preferred_element_type=F32)
            gout_ref[:, hidden] += lax.dot_general(gbranch, act, OVER, preferred_element_type=F32)
        outs = []
        gs = []
        gn = []
        for t in range(2):
            lanes = slice(t * LANES, (t + 1) * LANES)
            branch_t = branch[:, lanes] + bias_out[t]
            feat = feat_ref[pl.ds(row, block_rows), :, lanes].reshape(cells, LANES).astype(F32)
            outs.append((feat + scale[t] * branch_t).astype(BF16))
            gn.append(gnormed[:, lanes])
            sums_ref[4, t] += partial(branch_t * ups[t])
            sums_ref[3, t] += partial(grad_branch[t].astype(F32))
            sums_ref[1, t] += partial(gn[t] * standard[t])
            sums_ref[2, t] += partial(gn[t])
            gs.append(gn[t] * gain[t])
        mean_g = jnp.sum(gs[0] + gs[1], axis=1, keepdims=True) * (1.0 / C)
        both = gs[0] * standard[0] + gs[1] * standard[1]
        mean_gs = jnp.sum(both, axis=1, keepdims=True) * (1.0 / C)
        gconv = []
        for t in range(2):
            grad = ((gs[t] - mean_g - standard[t] * mean_gs) * inv_std).astype(BF16)
            sums_ref[0, t] += partial(grad.astype(F32))
            gconv.append(grad)
        gconv_ref[pl.ds(row, block_rows)] = jnp.concatenate(gconv, axis=1).reshape(
            block_rows, lon_pad, CP
        )
        out = jnp.concatenate(outs, axis=1).reshape(block_rows, lon_pad, CP)
        out_ref[pl.ds(row, block_rows)] = out[:, : out_ref.shape[1], :C]
        out_copy(block).start()
        return carry

    def out_copy(block):
        at = pl.ds(block * block_rows, block_rows)
        return pltpu.make_async_copy(out_ref.at[at], out_hbm.at[at], out_sem.at[block])

    lax.fori_loop(0, rows // block_rows, body, 0)
    for block in range(rows // block_rows):
        out_copy(block).wait()


def taps_kernel(order, starts, rows, lon_pad, block_rows, conv_rows,
                me_ref, gconv_ref, v_ref, gin_ref, gout_ref, sums_ref,
                g_ref, rows_ref, acc_ref, wo32_ref, small_ref):
    acc_ref[...] = jnp.zeros_like(acc_ref)
    pairs, filters = points_for(conv_rows)
    count = len(filters)

    def body(step, carry):
        tile = step % 2
        block = step // 2
        lanes = pl.ds(pl.multiple_of(tile * LANES, LANES), LANES)
        grads = grad_points(
            pairs,
            [gconv_ref[block * conv_rows + r, :, lanes].astype(F32) for r in range(conv_rows)],
        )
        for k in range(count):
            for b in range(KS):
                term = grads[k] * v_ref[tile, block * count + k, pl.ds(b, lon_pad), :]
                acc_ref[tile, k, b] += term.reshape(lon_pad // 8, 8, LANES).sum(axis=0)
        return carry

    lax.fori_loop(0, 2 * (rows // conv_rows), body, 0)
    rows_ref[...] = jnp.zeros_like(rows_ref)
    small_ref[...] = jnp.zeros_like(small_ref)
    for t in range(2):
        totals = [jnp.sum(acc_ref[t, k], axis=1) for k in range(count)]
        for a in range(KS):
            small_ref[t, pl.ds(a * KS, KS), :] = weighted([f[a] for f in filters], totals)
        for at, k in ((TAPS, 0), (TAPS + 1, 1), (TAPS + 2, 2), (TAPS + 7, 3), (TAPS + 8, 4)):
            small_ref[t, pl.ds(at, 1), :] = jnp.sum(sums_ref[k, t], axis=0, keepdims=True)
        wo32_ref[t] = gout_ref[pl.ds(t * LANES, LANES), :].T
    outs = join_quarters(
        [[wo32_ref[t, pl.ds(q, C, stride=4), :] for t in range(2)] for q in range(4)]
    )
    tails = join_quarters(
        [[small_ref[t, pl.ds(q, 16, stride=4), :] for t in range(2)] for q in range(4)]
    )
    put_rows(rows_ref, 0, [gin_ref[pl.ds(0, C), j * LANES : (j + 1) * LANES] for j in range(TILES)])
    put_rows(rows_ref, ROW_OUT, outs)
    put_rows(rows_ref, ROW_TAPS, tails)
    put_rows(
        rows_ref,
        ROW_BIAS_IN,
        [gin_ref[pl.ds(C, 1), j * LANES : (j + 1) * LANES] for j in range(TILES)],
    )
    me = me_ref[0]
    window = g_ref.shape[1]
    for position, start in zip(order, starts):
        share = [rows_ref[t, pl.ds(start, window), :] for t in range(2)]
        g_ref[position ^ me] = jnp.concatenate(share, axis=1).astype(BF16)


def field_kernel(first, count, rows, cols, lon_pad, conv_rows,
                 u_ref, up_ref, main_ref, west_ref, east_ref, south_ref, north_ref, *rest):
    out_hbm, x_ref, v_ref, sum_ref, out_ref, out_sem = rest[-6:]
    assemble(x_ref, first, count + KS - 1, main_ref, west_ref, east_ref, south_ref, north_ref, rows, cols)
    write_points(x_ref, v_ref, count // conv_rows, conv_rows)

    def body(block, carry):
        row = block * conv_rows

        def store(tile, lon, chunk, sums):
            lanes = pl.ds(pl.multiple_of(tile * LANES, LANES), LANES)
            for r in range(conv_rows):
                total = sums[r] + up_ref[first + row + r, pl.ds(lon, chunk), lanes].astype(F32)
                sum_ref[r, pl.ds(lon, chunk), lanes] = total

        depthwise_block(v_ref, u_ref, block, conv_rows, lon_pad, store, True)
        out_ref[pl.ds(row, conv_rows)] = sum_ref[:, 0:cols, 0:C].astype(BF16)
        out_copy(block).start()
        return carry

    def out_copy(block):
        row = block * conv_rows
        return pltpu.make_async_copy(
            out_ref.at[pl.ds(row, conv_rows)],
            out_hbm.at[pl.ds(first + row, conv_rows)],
            out_sem.at[block],
        )

    lax.fori_loop(0, count // conv_rows, body, 0)
    for block in range(count // conv_rows):
        out_copy(block).wait()


def shape(dims, kind):
    return jax.ShapeDtypeStruct(dims, kind)


def whole(count):
    return [pl.BlockSpec(memory_space=pltpu.VMEM)] * count


def cost(micros):
    return pl.CostEstimate(flops=int(micros * 1.1e9), bytes_accessed=0, transcendentals=0)


def body(features, params, langevin_noise, upstream):
    rows, cols = features.shape[:2]
    lon_pad = up(cols, 16)
    lon_wide = up(lon_pad + KS - 1, 8)
    conv_rows = max(r for r in (1, 3, 5) if rows % r == 0)
    points = conv_rows + KS - 1
    blocks = rows // conv_rows
    block_rows = max(r for r in range(1, 16) if rows % r == 0 and r % conv_rows == 0)
    groups, bits = exchange_groups()
    count = 1 << bits
    lat_size = lax.axis_size("lat")
    length = params.shape[0]
    number = lax.axis_index("lon") * lat_size + lax.axis_index("lat")
    place = jnp.int32(0)
    for k in range(bits):
        place = place | (((number >> k) & 1) << (bits - 1 - k))
    place = place.reshape(1).astype(jnp.int32)
    offset = (number * length) % SHARE_LANES
    order = [reversed_bits(s, bits) for s in range(count)]
    starts = [s * length // SHARE_LANES for s in range(count)]
    spill = SHARE_LANES - math.gcd(SHARE_LANES, length)
    window = up(-(-(length + spill) // SHARE_LANES), 8)
    flat_rows = up(max(starts[-1] + window, 3 * (ROWS + 1)), 8)

    share = lax.dynamic_update_slice(
        jnp.zeros((window * SHARE_LANES,), BF16), params.astype(BF16), (offset,)
    )
    gathered = share.reshape(1, window, SHARE_LANES)
    compiler_params = pltpu.CompilerParams(vmem_limit_bytes=VMEM)
    edges = pl.pallas_call(
        lambda *refs: edge_kernel(cols, *refs),
        out_shape=(shape((rows, RAD, C), BF16),) * 2,
        in_specs=[pl.BlockSpec(memory_space=pl.ANY)],
        out_specs=tuple(whole(2)),
        scratch_shapes=[pltpu.VMEM((rows, cols, C), BF16)],
        compiler_params=compiler_params,
        cost_estimate=cost(1),
        name="edges",
    )(features)
    west, east = shift_both(*edges, "lon", True)
    for k, group in enumerate(groups):
        parts = [swap(gathered, mask) for mask in group]
        if k == max(0, len(groups) - 2):
            west, east, _ = lax.optimization_barrier((west, east, parts[0]))
            wides = pl.pallas_call(
                lambda *refs: wide_kernel(rows, cols, *refs),
                out_shape=(shape((RAD, cols + 2 * RAD, C), BF16),) * 2,
                in_specs=whole(3),
                out_specs=tuple(whole(2)),
                compiler_params=compiler_params,
                cost_estimate=cost(1),
                name="wides",
            )(features, west, east)
            south, north = shift_both(*wides, "lat", False)
        gathered = jnp.concatenate([gathered, *parts], axis=0)
        if k == max(0, len(groups) - 2):
            gathered, upstream = lax.optimization_barrier((gathered, upstream))
    feature_halos = (west, east, south, north)

    smem = [pl.BlockSpec(memory_space=pltpu.SMEM)]
    data, feats, ups = pl.pallas_call(
        lambda *refs: assemble_kernel(rows, cols, conv_rows, *refs),
        out_shape=(
            shape((2, blocks * points, lon_wide, LANES), F32),
            shape((rows, lon_pad, CP), BF16),
            shape((rows, lon_pad, CP), BF16),
        ),
        in_specs=whole(6),
        out_specs=tuple(whole(3)),
        scratch_shapes=[pltpu.VMEM((2, rows + KS - 1, lon_wide, LANES), F32)],
        compiler_params=compiler_params,
        cost_estimate=cost(3),
        name="assemble",
    )(features, *feature_halos, upstream)

    static = (order, starts, rows, lon_pad, block_rows, conv_rows)
    output, gconv, gin, gout, sums, flipped = pl.pallas_call(
        lambda *refs: layer_kernel(*static, *refs),
        out_shape=(
            shape((rows, cols, C), BF16),
            shape((rows, lon_pad, CP), BF16),
            shape((CP, H), F32),
            shape((CP, H), F32),
            shape((5, 2, 8, LANES), F32),
            shape((2, points, 8, LANES), F32),
        ),
        in_specs=smem + whole(4),
        out_specs=(pl.BlockSpec(memory_space=pl.ANY), *whole(5)),
        scratch_shapes=[
            pltpu.VMEM((rows, cols, C), BF16),
            pltpu.SemaphoreType.DMA((rows // block_rows,)),
            pltpu.VMEM((2, points, 8, LANES), F32),
            pltpu.VMEM((2, 64, LANES), F32),
            pltpu.VMEM((2, flat_rows, LANES), F32),
            pltpu.VMEM((CP, H), BF16),
            pltpu.VMEM((H, CP), BF16),
            pltpu.VMEM((2, H, LANES), F32),
            pltpu.VMEM((2, block_rows, lon_pad, LANES), F32),
        ],
        compiler_params=compiler_params,
        cost_estimate=cost(22),
        name="layer",
    )(place, gathered, data, feats, ups)

    values = pl.pallas_call(
        lambda *refs: taps_kernel(*static, *refs),
        out_shape=shape((count, window, SHARE_LANES), BF16),
        in_specs=smem + whole(5),
        out_specs=whole(1)[0],
        scratch_shapes=[
            pltpu.VMEM((2, flat_rows, LANES), F32),
            pltpu.VMEM((2, points, KS, 8, LANES), F32),
            pltpu.VMEM((2, H, LANES), F32),
            pltpu.VMEM((2, 64, LANES), F32),
        ],
        compiler_params=compiler_params,
        cost_estimate=cost(11),
        name="taps",
    )(place, gconv, data, gin, gout, sums)

    west, east = shift_both(gconv[:, :RAD, :C], gconv[:, cols - RAD : cols, :C], "lon", True)
    pieces = 3 if rows % (3 * conv_rows) == 0 else 1
    piece_rows = rows // pieces
    field = None

    def field_piece(piece, south, north, field):
        before = [] if field is None else [field]
        held = [pl.BlockSpec(memory_space=pl.ANY)] * len(before)
        return pl.pallas_call(
            lambda *refs: field_kernel(
                piece * piece_rows, piece_rows, rows, cols, lon_pad, conv_rows, *refs
            ),
            out_shape=shape((rows, cols, C), BF16),
            in_specs=whole(7) + held,
            out_specs=pl.BlockSpec(memory_space=pl.ANY),
            scratch_shapes=[
                pltpu.VMEM((2, piece_rows + KS - 1, lon_wide, LANES), F32),
                pltpu.VMEM((2, piece_rows // conv_rows * points, lon_wide, LANES), F32),
                pltpu.VMEM((conv_rows, lon_pad, CP), F32),
                pltpu.VMEM((piece_rows, cols, C), BF16),
                pltpu.SemaphoreType.DMA((piece_rows // conv_rows,)),
            ],
            input_output_aliases={7: 0} if before else {},
            compiler_params=compiler_params,
            cost_estimate=cost(10 / pieces),
            name="field",
        )(flipped, ups, gconv, west, east, south, north, *before)

    for k, group in enumerate(groups[::-1]):
        if k == min(1, len(groups) - 1):
            values, west, east = lax.optimization_barrier((values, west, east))
        part = values.shape[0] // (len(group) + 1)
        received = [
            swap(values[(i + 1) * part : (i + 2) * part].astype(BF16), mask)
            for i, mask in enumerate(group)
        ]
        if k == min(1, len(groups) - 1):
            def wide(at):
                return jnp.concatenate([west[at], gconv[at, :cols, :C], east[at]], axis=1)

            wides = (wide(slice(0, RAD)), wide(slice(rows - RAD, rows)))
            if pieces == 3:
                field = field_piece(1, *wides, None)
        if k == min(2, len(groups) - 1):
            south, north = shift_both(*wides, "lat", False)
            for piece in ([0, 2] if pieces == 3 else [0]):
                field = field_piece(piece, south, north, field)
        values = values[:part].astype(F32)
        for other in received:
            values = values + other.astype(F32)
        if k == 1 and len(groups) > 2:
            values, wides = lax.optimization_barrier((values, wides))
    summed = lax.dynamic_slice(values.reshape(-1), (offset,), (length,))
    new_params = params - STEP_SIZE * summed + NOISE_COEF * langevin_noise
    return (output, field, new_params)


def solution(mesh):
    return jax.shard_map(
        body,
        mesh=mesh,
        in_specs=(
            P("lat", "lon", None),
            P(("lon", "lat")),
            P(("lon", "lat")),
            P("lat", "lon", None),
        ),
        out_specs=(P("lat", "lon", None), P("lat", "lon", None), P(("lon", "lat"))),
        check_vma=False,
    )
```

```python
import math

import jax
import jax.numpy as jnp
from jax import lax
from jax.experimental import pallas as pl
from jax.experimental.pallas import tpu as pltpu
from jax.sharding import PartitionSpec as P

C = 192
H = 768
KS = 7
RAD = KS // 2
LANES = 128
CP = 256
TAPS = KS * KS
EPSILON = 1e-06
STEP_SIZE = 0.003
NOISE_COEF = 0.08
GELU_A = math.sqrt(2.0 / math.pi)
GELU_B = GELU_A * 0.044715
F32 = jnp.float32
BF16 = jnp.bfloat16
ROW_OUT = C
ROW_TAPS = 2 * C
ROW_NORM = ROW_TAPS + TAPS // 4
ROW_BIAS_IN = ROW_NORM + 1
ROW_LAST = ROW_NORM + 2
ROWS = ROW_LAST + 1
TILES = H // LANES
SHARE_LANES = 256
CHUNK = 256
ALL = ((1,), (1,)), ((), ())
OVER = ((0,), (0,)), ((), ())
VMEM = 28 << 20


def exchange_groups():
    lon, lat = lax.axis_size("lon"), lax.axis_size("lat")
    bits = [(lon >> k, 0) for k in range(1, lon.bit_length())]
    bits += [(0, lat >> k) for k in range(1, lat.bit_length())]
    groups = []
    k = 0
    while k < len(bits):
        if k + 1 < len(bits) and bits[k][0] == 1 and bits[k + 1][0] == 0:
            (lon_bit, _), (_, lat_bit) = bits[k : k + 2]
            groups.append([(lon_bit, 0), (0, lat_bit), (lon_bit, lat_bit)])
            k += 2
        else:
            groups.append([bits[k]])
            k += 1
    return groups, len(bits)


def swap(values, mask):
    lon, lat = lax.axis_size("lon"), lax.axis_size("lat")
    pairs = [
        (i * lat + j, (i ^ mask[0]) * lat + (j ^ mask[1])) for i in range(lon) for j in range(lat)
    ]
    return lax.ppermute(values, ("lon", "lat"), pairs)


def shift_both(low_edge, high_edge, axis, periodic):
    count = lax.axis_size(axis)
    if count % 2:
        forward = [(i, (i + 1) % count) for i in range(count if periodic else count - 1)]
        backward = [(target, source) for source, target in forward]
        return lax.ppermute(high_edge, axis, forward), lax.ppermute(low_edge, axis, backward)
    even = lax.axis_index(axis) % 2 == 0
    near = [(i, i ^ 1) for i in range(count)]
    odds = [(i, (i + 1) % count) for i in range(1, count if periodic else count - 1, 2)]
    far = odds + [(target, source) for source, target in odds]
    near = lax.ppermute(jnp.where(even, high_edge, low_edge), axis, near)
    far = lax.ppermute(jnp.where(even, low_edge, high_edge), axis, far)
    return jnp.where(even, far, near), jnp.where(even, near, far)


def reversed_bits(number, count):
    result = 0
    for k in range(count):
        result |= ((number >> k) & 1) << (count - 1 - k)
    return result


def up(value, multiple):
    return -(-value // multiple) * multiple


def split_quarter(tiles, quarter):
    lane = lax.broadcasted_iota(jnp.int32, tiles[0].shape, 1)
    low = lane < LANES // 2
    first = 3 * quarter // 2
    if quarter % 2 == 0:
        return tiles[first], jnp.where(low, tiles[first + 1], 0.0)
    left = pltpu.roll(tiles[first], LANES // 2, 1)
    right = pltpu.roll(tiles[first + 1], LANES // 2, 1)
    return jnp.where(low, left, right), jnp.where(low, right, 0.0)


def join_quarters(quarters):
    lane = lax.broadcasted_iota(jnp.int32, quarters[0][0].shape, 1)
    low = lane < LANES // 2
    tiles = []
    for even in (0, 2):
        first, second = quarters[even]
        turned = pltpu.roll(quarters[even + 1][0], LANES // 2, 1)
        last = pltpu.roll(quarters[even + 1][1], LANES // 2, 1)
        tiles += [first, jnp.where(low, second, turned), jnp.where(low, turned, last)]
    return tiles


def get_rows(flat_ref, row, count):
    return [
        flat_ref[j % 2, pl.ds(3 * row + j // 2, count, stride=3), :] for j in range(TILES)
    ]


def put_rows(flat_ref, row, tiles):
    for j in range(TILES):
        flat_ref[j % 2, pl.ds(3 * row + j // 2, tiles[j].shape[0], stride=3), :] = tiles[j]


def assemble(x_ref, base, first, count, main, west, east, south, north, rows, cols):
    for t in range(2):
        lanes = slice(t * LANES, min(C, (t + 1) * LANES))
        width = slice(0, lanes.stop - lanes.start)
        low = max(0, first - RAD)
        high = min(rows, first + count - RAD)
        at = slice(base + low + RAD - first, base + high + RAD - first)
        x_ref[t, at, 0:RAD, width] = west[low:high, :, lanes].astype(F32)
        x_ref[t, at, RAD : RAD + cols, width] = main[low:high, 0:cols, lanes].astype(F32)
        x_ref[t, at, RAD + cols : 2 * RAD + cols, width] = east[low:high, :, lanes].astype(F32)
        wide = slice(0, cols + 2 * RAD)
        if first < RAD:
            at = slice(base, base + RAD - first)
            x_ref[t, at, wide, width] = south[first:, :, lanes].astype(F32)
        over = first + count - rows - RAD
        if over > 0:
            at = slice(base + count - over, base + count)
            x_ref[t, at, wide, width] = north[0:over, :, lanes].astype(F32)


def field_points(ranges, conv_rows, x_ref, v_ref, main, west, east, south, north, rows, cols):
    x_ref[...] = jnp.zeros_like(x_ref)
    base = done = 0
    for first, count in ranges:
        span = count * conv_rows + KS - 1
        assemble(
            x_ref, base, first * conv_rows, span, main, west, east, south, north, rows, cols
        )
        write_points(x_ref, base, v_ref, done, count, conv_rows)
        base += span
        done += count


def padded_rows(ranges, conv_rows):
    return sum(count * conv_rows + KS - 1 for _, count in ranges)


def block_count(ranges):
    return sum(count for _, count in ranges)


def over_blocks(ranges, step):
    done = 0
    for first, count in ranges:

        def body(i, carry, done=done, first=first):
            step(done + i, first + i)
            return carry

        lax.fori_loop(0, count, body, 0)
        done += count


def edge_kernel(cols, field_hbm, west_ref, east_ref, field_ref):
    pltpu.sync_copy(field_hbm, field_ref)
    west_ref[...] = field_ref[:, 0:RAD, :]
    east_ref[...] = field_ref[:, cols - RAD : cols, :]


def wide_kernel(rows, cols, field_ref, west_ref, east_ref, south_ref, north_ref):
    for out_ref, first in ((south_ref, 0), (north_ref, rows - RAD)):
        at = slice(first, first + RAD)
        out_ref[:, 0:RAD, :] = west_ref[at]
        out_ref[:, RAD : RAD + cols, :] = field_ref[at, 0:cols, :]
        out_ref[:, RAD + cols : 2 * RAD + cols, :] = east_ref[at]


def inner_kernel(ranges, rows, cols, conv_rows, feat_ref, west_ref, east_ref, up_ref,
                 v_ref, feats_ref, ups_ref, x_ref):
    field_points(
        ranges, conv_rows, x_ref, v_ref, feat_ref, west_ref, east_ref, None, None, rows, cols
    )
    feats_ref[...] = jnp.zeros_like(feats_ref)
    feats_ref[:, 0:cols, 0:C] = feat_ref[...]
    ups_ref[...] = jnp.zeros_like(ups_ref)
    ups_ref[:, 0:cols, 0:C] = up_ref[...]


def outer_kernel(ranges, rows, cols, conv_rows, feat_ref, west_ref, east_ref, south_ref, north_ref,
                 v_ref, x_ref):
    field_points(
        ranges, conv_rows, x_ref, v_ref, feat_ref, west_ref, east_ref, south_ref, north_ref, rows,
        cols,
    )


def points_for(out_rows):
    pairs = [1.0, 0.5, 2.0, 1.5, 0.75][: (out_rows + KS - 2) // 2]
    points = [0.0] + [sign * p for p in pairs for sign in (1.0, -1.0)]
    filters = []
    for k, point in enumerate(points):
        scale = math.prod(point - other for i, other in enumerate(points) if i != k)
        filters.append([point**a / scale for a in range(KS)])
    return pairs, filters


def polynomial(roots):
    coefs = [1.0]
    for root in roots:
        coefs = [
            (coefs[i - 1] if i else 0.0) - (root * coefs[i] if i < len(coefs) else 0.0)
            for i in range(len(coefs) + 1)
        ]
    return coefs


def weighted(coefs, values):
    total = None
    for coef, value in zip(coefs, values):
        if coef == 0.0:
            continue
        term = value if coef == 1.0 else value * coef
        total = term if total is None else total + term
    return total


def data_points(pairs, rows):
    squares = [p * p for p in pairs]
    values = [weighted(polynomial(squares), rows[0::2])]
    for p in pairs:
        coefs = polynomial([q for q in squares if q != p * p])
        even = weighted(coefs, rows[2::2])
        odd = weighted([p * c for c in coefs], rows[1::2])
        values += [even + odd, even - odd]
    return values


def grad_points(pairs, rows):
    values = [rows[0]]
    for p in pairs:
        even = weighted([p ** (2 * i) for i in range(len(rows[0::2]))], rows[0::2])
        odd = weighted([p ** (2 * i + 1) for i in range(len(rows[1::2]))], rows[1::2])
        values += [even + odd, even - odd] if odd is not None else [even, even]
    return values


def write_points(x_ref, base, v_ref, done, blocks, out_rows):
    pairs, filters = points_for(out_rows)
    count = len(filters)
    lon_regs = x_ref.shape[2] // 8

    def body(step, carry):
        tile = step // lon_regs
        lon = pl.ds(pl.multiple_of(step % lon_regs * 8, 8), 8)

        def block(k, carry):
            rows = [x_ref[tile, base + k * out_rows + r, lon, :] for r in range(count)]
            for i, value in enumerate(data_points(pairs, rows)):
                v_ref[tile, (done + k) * count + i, lon, :] = value
            return carry

        return lax.fori_loop(0, blocks, block, carry, unroll=blocks <= 4)

    lax.fori_loop(0, 2 * lon_regs, body, 0)


def filter_points(taps_ref, out_rows, u_ref, flip):
    for k, coefs in enumerate(points_for(out_rows)[1]):
        coefs = coefs[::-1] if flip else coefs
        for t in range(2):
            u_ref[t, k, 0:KS, :] = weighted(
                coefs, [taps_ref[t, pl.ds(a * KS, KS), :] for a in range(KS)]
            )


def depthwise_block(v_ref, u_ref, block, out_rows, lon_pad, store, flip):
    pairs, filters = points_for(out_rows)
    count = len(filters)
    chunk = lon_pad

    def body(step, carry):
        tile = step // (lon_pad // chunk)
        lon = pl.multiple_of(step % (lon_pad // chunk) * chunk, 8)

        def product(k):
            total = None
            for b in range(KS):
                tap = KS - 1 - b if flip else b
                term = v_ref[tile, block * count + k, pl.ds(lon + b, chunk), :]
                term = term * u_ref[tile, k, pl.ds(tap, 1), :]
                total = term if total is None else total + term
            return total

        sums = [None] * out_rows
        sums[0] = product(0)
        for i, p in enumerate(pairs):
            plus, minus = product(2 * i + 1), product(2 * i + 2)
            even, odd = plus + minus, plus - minus
            for r in range(out_rows):
                term = odd if r % 2 else even
                term = term if p**r == 1.0 else term * p**r
                sums[r] = term if sums[r] is None else sums[r] + term
        store(tile, lon, chunk, sums)
        return carry

    lax.fori_loop(0, 2 * (lon_pad // chunk), body, 0)


def layer_kernel(order, starts, rows, lon_pad, block_rows, conv_rows, inner, outer,
                 me_ref, gathered_ref, inner_ref, outer_ref, feat_ref, up_ref,
                 out_ref, gconv_ref, gin_ref, gout_ref, sums_ref, flipped_ref,
                 u_ref, taps_ref, w_ref, win_ref, wout_ref, wo32_ref, conv_ref, act_ref, gpre_ref):
    me = me_ref[0]
    w_ref[...] = jnp.zeros_like(w_ref)
    window = gathered_ref.shape[1]
    for position, start in zip(order, starts):
        share = gathered_ref[position ^ me].astype(F32)
        for t in range(2):
            w_ref[t, pl.ds(start, window), :] += share[:, t * LANES : (t + 1) * LANES]
    rest = lax.broadcasted_iota(jnp.int32, (CP - C, LANES), 0)
    mains = get_rows(w_ref, 0, C)
    biases = get_rows(w_ref, ROW_BIAS_IN, 1)
    for j in range(TILES):
        bias = jnp.where(rest == 0, biases[j], 0.0)
        whole = jnp.concatenate([mains[j], bias], axis=0)
        win_ref[:, j * LANES : (j + 1) * LANES] = whole.astype(BF16)
    for quarter in range(4):
        pair = split_quarter(get_rows(w_ref, ROW_OUT, C), quarter)
        tail = split_quarter(get_rows(w_ref, ROW_TAPS, 16), quarter)
        for t in range(2):
            wo32_ref[t, pl.ds(quarter, C, stride=4), :] = pair[t]
            taps_ref[t, pl.ds(quarter, 16, stride=4), :] = tail[t]
    for t in range(2):
        wout_ref[:, t * LANES : (t + 1) * LANES] = wo32_ref[t].astype(BF16)

    def vector(row, quarter):
        at = (row - ROW_TAPS) * 4 + quarter
        return [taps_ref[t, pl.ds(at, 1), :] for t in range(2)]

    filter_points(taps_ref, conv_rows, u_ref, False)
    filter_points(taps_ref, conv_rows, flipped_ref, True)
    cbias = vector(ROW_NORM, 1)
    gain = vector(ROW_NORM, 2)
    shift = vector(ROW_NORM, 3)
    bias_out = vector(ROW_LAST, 0)
    scale = vector(ROW_LAST, 1)
    lane = lax.broadcasted_iota(jnp.int32, (1, LANES), 1)
    inside = (lane < C - LANES).astype(F32)
    shift[1] = shift[1] + (lane == C - LANES).astype(F32)

    gin_ref[...] = jnp.zeros_like(gin_ref)
    gout_ref[...] = jnp.zeros_like(gout_ref)
    sums_ref[...] = jnp.zeros_like(sums_ref)
    cells = block_rows * lon_pad

    def partial(values):
        return values.reshape(cells // 8, 8, LANES).sum(axis=0)

    for v_ref, ranges in ((inner_ref, inner), (outer_ref, outer)):

        def conv_step(place, block, v_ref=v_ref):
            def store(tile, lon, chunk, sums):
                for r in range(conv_rows):
                    conv_ref[tile, block * conv_rows + r, pl.ds(lon, chunk), :] = sums[r]

            depthwise_block(v_ref, u_ref, place, conv_rows, lon_pad, store, False)

        over_blocks(ranges, conv_step)

    def body(block, carry):
        row = block * block_rows
        conv = [
            conv_ref[t, pl.ds(row, block_rows)].reshape(cells, LANES) + cbias[t] for t in range(2)
        ]
        mean = jnp.sum(conv[0] + conv[1], axis=1, keepdims=True) * (1.0 / C)
        centred = [conv[0] - mean, (conv[1] - mean) * inside]
        square = centred[0] * centred[0] + centred[1] * centred[1]
        inv_std = lax.rsqrt(jnp.sum(square, axis=1, keepdims=True) * (1.0 / C) + EPSILON)
        standard = [c * inv_std for c in centred]
        normed = jnp.concatenate(
            [(standard[t] * gain[t] + shift[t]).astype(BF16) for t in range(2)], axis=1
        )
        upstream = up_ref[pl.ds(row, block_rows)].reshape(cells, CP)
        ups = [upstream[:, t * LANES : (t + 1) * LANES].astype(F32) for t in range(2)]
        grad_branch = [(scale[t] * ups[t]).astype(BF16) for t in range(2)]
        gbranch = jnp.concatenate(grad_branch, axis=1)
        for h in range(0, H, CHUNK):
            hidden = slice(h, h + CHUNK)
            pre = jnp.dot(normed, win_ref[:, hidden], preferred_element_type=F32)
            gact = lax.dot_general(gbranch, wout_ref[hidden, :], ALL, preferred_element_type=F32)
            square = pre * pre
            half = 0.5 + 0.5 * jnp.tanh(pre * (GELU_A + GELU_B * square))
            act = pre * half
            slope = half + act * (1.0 - half) * (2.0 * GELU_A + 6.0 * GELU_B * square)
            act_ref[:, hidden] = act.astype(BF16)
            gpre_ref[:, hidden] = (gact * slope).astype(BF16)
        act = act_ref[...]
        gpre = gpre_ref[...]
        branch = jnp.dot(act, wout_ref[...], preferred_element_type=F32)
        gnormed = lax.dot_general(gpre, win_ref[...], ALL, preferred_element_type=F32)
        gin_ref[...] += lax.dot_general(normed, gpre, OVER, preferred_element_type=F32)
        gout_ref[...] += lax.dot_general(gbranch, act, OVER, preferred_element_type=F32)
        outs = []
        gs = []
        gn = []
        for t in range(2):
            lanes = slice(t * LANES, (t + 1) * LANES)
            branch_t = branch[:, lanes] + bias_out[t]
            feat = feat_ref[pl.ds(row, block_rows), :, lanes].reshape(cells, LANES).astype(F32)
            outs.append((feat + scale[t] * branch_t).astype(BF16))
            gn.append(gnormed[:, lanes])
            sums_ref[4, t] += partial(branch_t * ups[t])
            sums_ref[3, t] += partial(grad_branch[t].astype(F32))
            sums_ref[1, t] += partial(gn[t] * standard[t])
            sums_ref[2, t] += partial(gn[t])
            gs.append(gn[t] * gain[t])
        mean_g = jnp.sum(gs[0] + gs[1], axis=1, keepdims=True) * (1.0 / C)
        both = gs[0] * standard[0] + gs[1] * standard[1]
        mean_gs = jnp.sum(both, axis=1, keepdims=True) * (1.0 / C)
        gconv = []
        for t in range(2):
            grad = ((gs[t] - mean_g - standard[t] * mean_gs) * inv_std).astype(BF16)
            sums_ref[0, t] += partial(grad.astype(F32))
            gconv.append(grad)
        gconv_ref[pl.ds(row, block_rows)] = jnp.concatenate(gconv, axis=1).reshape(
            block_rows, lon_pad, CP
        )
        out = jnp.concatenate(outs, axis=1).reshape(block_rows, lon_pad, CP)
        out_ref[pl.ds(row, block_rows)] = out[:, : out_ref.shape[1], :C]
        return carry

    lax.fori_loop(0, rows // block_rows, body, 0)


def taps_kernel(order, starts, rows, lon_pad, block_rows, conv_rows, inner, outer,
                me_ref, gconv_ref, inner_ref, outer_ref, gin_ref, gout_ref, sums_ref, done_ref,
                g_ref, done_hbm, rows_ref, acc_ref, wo32_ref, small_ref, done_sem):
    done_copy = pltpu.make_async_copy(done_ref, done_hbm, done_sem)
    done_copy.start()
    acc_ref[...] = jnp.zeros_like(acc_ref)
    pairs, filters = points_for(conv_rows)
    count = len(filters)

    for v_ref, ranges in ((inner_ref, inner), (outer_ref, outer)):

        def step(place, block, v_ref=v_ref):
            def side(tile, carry):
                lanes = pl.ds(pl.multiple_of(tile * LANES, LANES), LANES)
                grads = grad_points(
                    pairs,
                    [
                        gconv_ref[block * conv_rows + r, :, lanes].astype(F32)
                        for r in range(conv_rows)
                    ],
                )
                for k in range(count):
                    for b in range(KS):
                        term = grads[k] * v_ref[tile, place * count + k, pl.ds(b, lon_pad), :]
                        acc_ref[tile, k, b] += term.reshape(lon_pad // 8, 8, LANES).sum(axis=0)
                return carry

            lax.fori_loop(0, 2, side, 0)

        over_blocks(ranges, step)

    rows_ref[...] = jnp.zeros_like(rows_ref)
    small_ref[...] = jnp.zeros_like(small_ref)
    for t in range(2):
        totals = [jnp.sum(acc_ref[t, k], axis=1) for k in range(count)]
        for a in range(KS):
            small_ref[t, pl.ds(a * KS, KS), :] = weighted([f[a] for f in filters], totals)
        for at, k in ((TAPS, 0), (TAPS + 1, 1), (TAPS + 2, 2), (TAPS + 7, 3), (TAPS + 8, 4)):
            small_ref[t, pl.ds(at, 1), :] = jnp.sum(sums_ref[k, t], axis=0, keepdims=True)
        wo32_ref[t] = gout_ref[pl.ds(t * LANES, LANES), :].T
    outs = join_quarters(
        [[wo32_ref[t, pl.ds(q, C, stride=4), :] for t in range(2)] for q in range(4)]
    )
    tails = join_quarters(
        [[small_ref[t, pl.ds(q, 16, stride=4), :] for t in range(2)] for q in range(4)]
    )
    put_rows(rows_ref, 0, [gin_ref[pl.ds(0, C), j * LANES : (j + 1) * LANES] for j in range(TILES)])
    put_rows(rows_ref, ROW_OUT, outs)
    put_rows(rows_ref, ROW_TAPS, tails)
    put_rows(
        rows_ref,
        ROW_BIAS_IN,
        [gin_ref[pl.ds(C, 1), j * LANES : (j + 1) * LANES] for j in range(TILES)],
    )
    me = me_ref[0]
    window = g_ref.shape[1]
    for position, start in zip(order, starts):
        share = [rows_ref[t, pl.ds(start, window), :] for t in range(2)]
        g_ref[position ^ me] = jnp.concatenate(share, axis=1).astype(BF16)
    done_copy.wait()


def field_kernel(ranges, rows, cols, lon_pad, conv_rows, lat_halos, before, last, begun,
                 u_ref, up_ref, main_ref, west_ref, east_ref, *rest):
    rest = list(rest)
    south_ref, north_ref = (rest.pop(0), rest.pop(0)) if lat_halos else (None, None)
    before_ref = rest.pop(0) if before else None
    if begun:
        rest.pop(0)
    out_hbm = rest.pop(0) if before or last else None
    out_ref = None if last else rest.pop(0)
    x_ref, v_ref, sum_ref, before_sem, out_sem, own_ref = rest
    out_ref = own_ref if last else out_ref
    if before:
        before_copy = pltpu.make_async_copy(before_ref, out_hbm.at[pl.ds(*before)], before_sem)
        before_copy.start()
    field_points(
        ranges, conv_rows, x_ref, v_ref, main_ref, west_ref, east_ref, south_ref, north_ref, rows,
        cols,
    )

    def step(place, block):
        row = block * conv_rows

        def store(tile, lon, chunk, sums):
            lanes = pl.ds(pl.multiple_of(tile * LANES, LANES), LANES)
            for r in range(conv_rows):
                total = sums[r] + up_ref[row + r, pl.ds(lon, chunk), lanes].astype(F32)
                sum_ref[r, pl.ds(lon, chunk), lanes] = total

        depthwise_block(v_ref, u_ref, place, conv_rows, lon_pad, store, True)
        out_ref[pl.ds(place * conv_rows, conv_rows)] = sum_ref[:, 0:cols, 0:C].astype(BF16)
        if last:
            out_copy(place, block).start()

    def out_copy(place, block):
        return pltpu.make_async_copy(
            out_ref.at[pl.ds(place * conv_rows, conv_rows)],
            out_hbm.at[pl.ds(block * conv_rows, conv_rows)],
            out_sem.at[place],
        )

    over_blocks(ranges, step)
    if last:
        over_blocks(ranges, lambda place, block: out_copy(place, block).wait())
    if before:
        before_copy.wait()


def shape(dims, kind):
    return jax.ShapeDtypeStruct(dims, kind)


def whole(count):
    return [pl.BlockSpec(memory_space=pltpu.VMEM)] * count


def cost(micros):
    return pl.CostEstimate(flops=int(micros * 1.1e9), bytes_accessed=0, transcendentals=0)


def body(features, params, langevin_noise, upstream):
    rows, cols = features.shape[:2]
    lon_pad = up(cols, 16)
    lon_wide = up(lon_pad + KS - 1, 8)
    conv_rows = max(r for r in (1, 3, 5) if rows % r == 0)
    points = conv_rows + KS - 1
    blocks = rows // conv_rows
    block_rows = max(r for r in range(1, 16) if rows % r == 0 and r % conv_rows == 0)
    groups, bits = exchange_groups()
    count = 1 << bits
    lat_size = lax.axis_size("lat")
    length = params.shape[0]
    number = lax.axis_index("lon") * lat_size + lax.axis_index("lat")
    place = jnp.int32(0)
    for k in range(bits):
        place = place | (((number >> k) & 1) << (bits - 1 - k))
    place = place.reshape(1).astype(jnp.int32)
    offset = (number * length) % SHARE_LANES
    order = [reversed_bits(s, bits) for s in range(count)]
    starts = [s * length // SHARE_LANES for s in range(count)]
    spill = SHARE_LANES - math.gcd(SHARE_LANES, length)
    window = up(-(-(length + spill) // SHARE_LANES), 8)
    flat_rows = up(max(starts[-1] + window, 3 * (ROWS + 1)), 8)

    share = jnp.pad(params, (SHARE_LANES, window * SHARE_LANES - length))
    share = lax.dynamic_slice(share, (SHARE_LANES - offset,), (window * SHARE_LANES,)).astype(BF16)
    gathered = share.reshape(1, window, SHARE_LANES)
    compiler_params = pltpu.CompilerParams(vmem_limit_bytes=VMEM)
    smem = [pl.BlockSpec(memory_space=pltpu.SMEM)]
    margin = -(-RAD // conv_rows)
    inner = [(margin, blocks - 2 * margin)]
    outer = [(0, margin), (blocks - margin, margin)]
    edges = pl.pallas_call(
        lambda *refs: edge_kernel(cols, *refs),
        out_shape=(shape((rows, RAD, C), BF16),) * 2,
        in_specs=[pl.BlockSpec(memory_space=pltpu.HBM)],
        out_specs=tuple(whole(2)),
        scratch_shapes=[pltpu.VMEM((rows, cols, C), BF16)],
        compiler_params=compiler_params,
        cost_estimate=cost(1),
        name="edges",
    )(features)
    west, east = shift_both(*edges, "lon", True)
    for k, group in enumerate(groups):
        parts = [swap(gathered, mask) for mask in group]
        if k == max(0, len(groups) - 2):
            west, east, _, upstream = lax.optimization_barrier((west, east, parts[0], upstream))
            wides = pl.pallas_call(
                lambda *refs: wide_kernel(rows, cols, *refs),
                out_shape=(shape((RAD, cols + 2 * RAD, C), BF16),) * 2,
                in_specs=whole(3),
                out_specs=tuple(whole(2)),
                compiler_params=compiler_params,
                cost_estimate=cost(1),
                name="wides",
            )(features, west, east)
            south, north = shift_both(*wides, "lat", False)
            inner_data, feats, ups = pl.pallas_call(
                lambda *refs: inner_kernel(inner, rows, cols, conv_rows, *refs),
                out_shape=(
                    shape((2, block_count(inner) * points, lon_wide, LANES), F32),
                    shape((rows, lon_pad, CP), BF16),
                    shape((rows, lon_pad, CP), BF16),
                ),
                in_specs=whole(4),
                out_specs=tuple(whole(3)),
                scratch_shapes=[pltpu.VMEM((2, padded_rows(inner, conv_rows), lon_wide, LANES), F32)],
                compiler_params=compiler_params,
                cost_estimate=cost(2.5),
                name="inner",
            )(features, west, east, upstream)
        gathered = jnp.concatenate([gathered, *parts], axis=0)
        if k == max(0, len(groups) - 2):
            gathered, inner_data = lax.optimization_barrier((gathered, inner_data))

    outer_data = pl.pallas_call(
        lambda *refs: outer_kernel(outer, rows, cols, conv_rows, *refs),
        out_shape=shape((2, block_count(outer) * points, lon_wide, LANES), F32),
        in_specs=whole(5),
        out_specs=whole(1)[0],
        scratch_shapes=[pltpu.VMEM((2, padded_rows(outer, conv_rows), lon_wide, LANES), F32)],
        compiler_params=compiler_params,
        cost_estimate=cost(1),
        name="outer",
    )(features, west, east, south, north)

    static = (order, starts, rows, lon_pad, block_rows, conv_rows, inner, outer)
    output, gconv, gin, gout, sums, flipped = pl.pallas_call(
        lambda *refs: layer_kernel(*static, *refs),
        out_shape=(
            shape((rows, cols, C), BF16),
            shape((rows, lon_pad, CP), BF16),
            shape((CP, H), F32),
            shape((CP, H), F32),
            shape((5, 2, 8, LANES), F32),
            shape((2, points, 8, LANES), F32),
        ),
        in_specs=smem + whole(5),
        out_specs=tuple(whole(6)),
        scratch_shapes=[
            pltpu.VMEM((2, points, 8, LANES), F32),
            pltpu.VMEM((2, 64, LANES), F32),
            pltpu.VMEM((2, flat_rows, LANES), F32),
            pltpu.VMEM((CP, H), BF16),
            pltpu.VMEM((H, CP), BF16),
            pltpu.VMEM((2, H, LANES), F32),
            pltpu.VMEM((2, rows, lon_pad, LANES), F32),
            pltpu.VMEM((block_rows * lon_pad, H), BF16),
            pltpu.VMEM((block_rows * lon_pad, H), BF16),
        ],
        compiler_params=compiler_params,
        cost_estimate=cost(22),
        name="layer",
    )(place, gathered, inner_data, outer_data, feats, ups)

    values, output = pl.pallas_call(
        lambda *refs: taps_kernel(*static, *refs),
        out_shape=(
            shape((count, window, SHARE_LANES), BF16),
            shape((rows, cols, C), BF16),
        ),
        in_specs=smem + whole(7),
        out_specs=(*whole(1), pl.BlockSpec(memory_space=pl.ANY)),
        scratch_shapes=[
            pltpu.VMEM((2, flat_rows, LANES), F32),
            pltpu.VMEM((2, points, KS, 8, LANES), F32),
            pltpu.VMEM((2, H, LANES), F32),
            pltpu.VMEM((2, 64, LANES), F32),
            pltpu.SemaphoreType.DMA(()),
        ],
        compiler_params=compiler_params,
        cost_estimate=cost(11),
        name="taps",
    )(place, gconv, inner_data, outer_data, gin, gout, sums, output)

    west, east = shift_both(gconv[:, :RAD, :C], gconv[:, cols - RAD : cols, :C], "lon", True)
    field = None

    def field_piece(ranges, lat_halos, before, field, last):
        count = block_count(ranges)
        own = shape((count * conv_rows, cols, C), BF16)
        operands = [flipped, ups, gconv, west, east, *lat_halos]
        in_specs = whole(len(operands))
        span = None
        if before is not None:
            span = (before[0], before[1].shape[0])
            operands.append(before[1])
            in_specs += whole(1)
        if field is not None:
            operands.append(field)
            in_specs.append(pl.BlockSpec(memory_space=pl.ANY))
        out_shape = []
        out_specs = []
        if before is not None or last:
            out_shape.append(shape((rows, cols, C), BF16))
            out_specs.append(pl.BlockSpec(memory_space=pl.ANY))
        if not last:
            out_shape.append(own)
            out_specs += whole(1)
        results = pl.pallas_call(
            lambda *refs: field_kernel(
                ranges, rows, cols, lon_pad, conv_rows, bool(lat_halos), span, last,
                field is not None, *refs
            ),
            out_shape=tuple(out_shape),
            in_specs=in_specs,
            out_specs=tuple(out_specs),
            scratch_shapes=[
                pltpu.VMEM((2, padded_rows(ranges, conv_rows), lon_wide, LANES), F32),
                pltpu.VMEM((2, count * points, lon_wide, LANES), F32),
                pltpu.VMEM((conv_rows, lon_pad, CP), F32),
                pltpu.SemaphoreType.DMA(()),
                pltpu.SemaphoreType.DMA((count,)),
                pltpu.VMEM(own.shape if last else (8, LANES), BF16),
            ],
            input_output_aliases={} if field is None else {len(operands) - 1: 0},
            compiler_params=compiler_params,
            cost_estimate=cost(1.1 * count),
            name="field",
        )(*operands)
        return (None if last else results[-1]), (results[0] if out_shape[0] is not own else None)

    early = (inner[0][1] + 1) // 2
    for k, group in enumerate(groups[::-1]):
        if k == min(1, len(groups) - 1):
            values, west, east = lax.optimization_barrier((values, west, east))
        part = values.shape[0] // (len(group) + 1)
        received = [
            swap(values[(i + 1) * part : (i + 2) * part].astype(BF16), mask)
            for i, mask in enumerate(group)
        ]
        if k == min(1, len(groups) - 1):
            def wide(at):
                return jnp.concatenate([west[at], gconv[at, :cols, :C], east[at]], axis=1)

            wides = (wide(slice(0, RAD)), wide(slice(rows - RAD, rows)))
            piece, _ = field_piece([(margin, early)], (), None, None, False)
        if k == min(2, len(groups) - 1):
            lat_halos = shift_both(*wides, "lat", False)
            piece, _ = lax.optimization_barrier((piece, values))
            at = margin * conv_rows
            late = [(margin + early, inner[0][1] - early)]
            piece, field = field_piece(late, (), (at, piece), None, False)
            at = (margin + early) * conv_rows
            _, field = field_piece(outer, lat_halos, (at, piece), field, True)
        values = values[:part].astype(F32)
        for other in received:
            values = values + other.astype(F32)
        if k == 1 and len(groups) > 2:
            values, wides = lax.optimization_barrier((values, wides))
    summed = lax.dynamic_slice(values.reshape(-1), (offset,), (length,))
    new_params = params - STEP_SIZE * summed + NOISE_COEF * langevin_noise
    return (output, field, new_params)


def solution(mesh):
    return jax.shard_map(
        body,
        mesh=mesh,
        in_specs=(
            P("lat", "lon", None),
            P(("lon", "lat")),
            P(("lon", "lat")),
            P("lat", "lon", None),
        ),
        out_specs=(P("lat", "lon", None), P("lat", "lon", None), P(("lon", "lat"))),
        check_vma=False,
    )
```

```python
import math

import jax
import jax.numpy as jnp
from jax import lax
from jax.experimental import pallas as pl
from jax.experimental.pallas import tpu as pltpu
from jax.sharding import PartitionSpec as P

C = 192
H = 768
KS = 7
RAD = KS // 2
LANES = 128
CP = 256
TAPS = KS * KS
EPSILON = 1e-06
STEP_SIZE = 0.003
NOISE_COEF = 0.08
GELU_A = math.sqrt(2.0 / math.pi)
GELU_B = GELU_A * 0.044715
F32 = jnp.float32
BF16 = jnp.bfloat16
ROW_OUT = C
ROW_TAPS = 2 * C
ROW_NORM = ROW_TAPS + TAPS // 4
ROW_BIAS_IN = ROW_NORM + 1
ROW_LAST = ROW_NORM + 2
ROWS = ROW_LAST + 1
TILES = H // LANES
SHARE_LANES = 256
CHUNK = 256
ALL = ((1,), (1,)), ((), ())
OVER = ((0,), (0,)), ((), ())
VMEM = 28 << 20


def exchange_groups():
    lon, lat = lax.axis_size("lon"), lax.axis_size("lat")
    bits = [(lon >> k, 0) for k in range(1, lon.bit_length())]
    bits += [(0, lat >> k) for k in range(1, lat.bit_length())]
    groups = []
    k = 0
    while k < len(bits):
        if k + 1 < len(bits) and bits[k][0] == 1 and bits[k + 1][0] == 0:
            (lon_bit, _), (_, lat_bit) = bits[k : k + 2]
            groups.append([(lon_bit, 0), (0, lat_bit), (lon_bit, lat_bit)])
            k += 2
        else:
            groups.append([bits[k]])
            k += 1
    return groups, len(bits)


def swap(values, mask):
    lon, lat = lax.axis_size("lon"), lax.axis_size("lat")
    pairs = [
        (i * lat + j, (i ^ mask[0]) * lat + (j ^ mask[1])) for i in range(lon) for j in range(lat)
    ]
    return lax.ppermute(values, ("lon", "lat"), pairs)


def send_edges(low_edge, high_edge, axis, periodic):
    count = lax.axis_size(axis)
    even = lax.axis_index(axis) % 2 == 0
    near = [(i, i ^ 1) for i in range(count)]
    odds = [(i, (i + 1) % count) for i in range(1, count if periodic else count - 1, 2)]
    far = odds + [(target, source) for source, target in odds]
    near = lax.ppermute(jnp.where(even, high_edge, low_edge), axis, near)
    far = lax.ppermute(jnp.where(even, low_edge, high_edge), axis, far)
    return near, far


def edges_from(near, far, axis):
    even = lax.axis_index(axis) % 2 == 0
    return jnp.where(even, far, near), jnp.where(even, near, far)


def shift_both(low_edge, high_edge, axis, periodic):
    return edges_from(*send_edges(low_edge, high_edge, axis, periodic), axis)


def reversed_bits(number, count):
    result = 0
    for k in range(count):
        result |= ((number >> k) & 1) << (count - 1 - k)
    return result


def up(value, multiple):
    return -(-value // multiple) * multiple


def split_quarter(tiles, quarter):
    lane = lax.broadcasted_iota(jnp.int32, tiles[0].shape, 1)
    low = lane < LANES // 2
    first = 3 * quarter // 2
    if quarter % 2 == 0:
        return tiles[first], jnp.where(low, tiles[first + 1], 0.0)
    left = pltpu.roll(tiles[first], LANES // 2, 1)
    right = pltpu.roll(tiles[first + 1], LANES // 2, 1)
    return jnp.where(low, left, right), jnp.where(low, right, 0.0)


def join_quarters(quarters):
    lane = lax.broadcasted_iota(jnp.int32, quarters[0][0].shape, 1)
    low = lane < LANES // 2
    tiles = []
    for even in (0, 2):
        first, second = quarters[even]
        turned = pltpu.roll(quarters[even + 1][0], LANES // 2, 1)
        last = pltpu.roll(quarters[even + 1][1], LANES // 2, 1)
        tiles += [first, jnp.where(low, second, turned), jnp.where(low, turned, last)]
    return tiles


def get_rows(flat_ref, row, count):
    return [
        flat_ref[j % 2, pl.ds(3 * row + j // 2, count, stride=3), :] for j in range(TILES)
    ]


def put_rows(flat_ref, row, tiles):
    for j in range(TILES):
        flat_ref[j % 2, pl.ds(3 * row + j // 2, tiles[j].shape[0], stride=3), :] = tiles[j]


def assemble(x_ref, base, first, count, main, west, east, south, north, rows, cols):
    for t in range(2):
        lanes = slice(t * LANES, min(C, (t + 1) * LANES))
        width = slice(0, lanes.stop - lanes.start)
        low = max(0, first - RAD)
        high = min(rows, first + count - RAD)
        at = slice(base + low + RAD - first, base + high + RAD - first)
        if main.shape[2] == CP:
            span = slice(RAD, RAD + main.shape[1])
            x_ref[t, at, span, :] = main[low:high, :, t * LANES : (t + 1) * LANES].astype(F32)
        else:
            x_ref[t, at, RAD : RAD + cols, width] = main[low:high, 0:cols, lanes].astype(F32)
        x_ref[t, at, 0:RAD, width] = west[low:high, :, lanes].astype(F32)
        x_ref[t, at, RAD + cols : 2 * RAD + cols, width] = east[low:high, :, lanes].astype(F32)
        wide = slice(0, cols + 2 * RAD)
        if first < RAD:
            at = slice(base, base + RAD - first)
            x_ref[t, at] = jnp.zeros_like(x_ref[t, at])
            x_ref[t, at, wide, width] = south[first:, :, lanes].astype(F32)
        over = first + count - rows - RAD
        if over > 0:
            at = slice(base + count - over, base + count)
            x_ref[t, at] = jnp.zeros_like(x_ref[t, at])
            x_ref[t, at, wide, width] = north[0:over, :, lanes].astype(F32)


def field_points(ranges, conv_rows, x_ref, v_ref, main, west, east, south, north, rows, cols):
    if main.shape[1:] == (x_ref.shape[2] - 8, CP):
        for t in range(2):
            for lon in (0, x_ref.shape[2] - 8):
                x_ref[t, :, lon : lon + 8, :] = jnp.zeros_like(x_ref[t, :, lon : lon + 8, :])
    else:
        x_ref[...] = jnp.zeros_like(x_ref)
    base = done = 0
    for first, count in ranges:
        span = count * conv_rows + KS - 1
        assemble(
            x_ref, base, first * conv_rows, span, main, west, east, south, north, rows, cols
        )
        write_points(x_ref, base, v_ref, done, count, conv_rows)
        base += span
        done += count


def padded_rows(ranges, conv_rows):
    return sum(count * conv_rows + KS - 1 for _, count in ranges)


def block_count(ranges):
    return sum(count for _, count in ranges)


def over_blocks(ranges, step):
    done = 0
    for first, count in ranges:

        def body(i, carry, done=done, first=first):
            step(done + i, first + i)
            return carry

        lax.fori_loop(0, count, body, 0)
        done += count


def edge_kernel(cols, field_hbm, west_ref, east_ref, field_ref):
    pltpu.sync_copy(field_hbm, field_ref)
    west_ref[...] = field_ref[:, 0:RAD, :]
    east_ref[...] = field_ref[:, cols - RAD : cols, :]


def wide_kernel(rows, cols, field_ref, west_ref, east_ref, south_ref, north_ref):
    for out_ref, first in ((south_ref, 0), (north_ref, rows - RAD)):
        at = slice(first, first + RAD)
        out_ref[:, 0:RAD, :] = west_ref[at]
        out_ref[:, RAD : RAD + cols, :] = field_ref[at, 0:cols, :]
        out_ref[:, RAD + cols : 2 * RAD + cols, :] = east_ref[at]


def inner_kernel(ranges, rows, cols, conv_rows, feat_ref, west_ref, east_ref, up_ref,
                 v_ref, feats_ref, ups_ref, x_ref):
    field_points(
        ranges, conv_rows, x_ref, v_ref, feat_ref, west_ref, east_ref, None, None, rows, cols
    )
    feats_ref[...] = jnp.zeros_like(feats_ref)
    feats_ref[:, 0:cols, 0:C] = feat_ref[...]
    ups_ref[...] = jnp.zeros_like(ups_ref)
    ups_ref[:, 0:cols, 0:C] = up_ref[...]


def outer_kernel(ranges, rows, cols, conv_rows, feat_ref, west_ref, east_ref, south_ref, north_ref,
                 v_ref, x_ref):
    field_points(
        ranges, conv_rows, x_ref, v_ref, feat_ref, west_ref, east_ref, south_ref, north_ref, rows,
        cols,
    )


def points_for(out_rows):
    pairs = [1.0, 0.5, 2.0, 1.5, 0.75][: (out_rows + KS - 2) // 2]
    points = [0.0] + [sign * p for p in pairs for sign in (1.0, -1.0)]
    filters = []
    for k, point in enumerate(points):
        scale = math.prod(point - other for i, other in enumerate(points) if i != k)
        filters.append([point**a / scale for a in range(KS)])
    return pairs, filters


def polynomial(roots):
    coefs = [1.0]
    for root in roots:
        coefs = [
            (coefs[i - 1] if i else 0.0) - (root * coefs[i] if i < len(coefs) else 0.0)
            for i in range(len(coefs) + 1)
        ]
    return coefs


def weighted(coefs, values):
    total = None
    for coef, value in zip(coefs, values):
        if coef == 0.0:
            continue
        term = value if coef == 1.0 else value * coef
        total = term if total is None else total + term
    return total


def data_points(pairs, rows):
    squares = [p * p for p in pairs]
    values = [weighted(polynomial(squares), rows[0::2])]
    for p in pairs:
        coefs = polynomial([q for q in squares if q != p * p])
        even = weighted(coefs, rows[2::2])
        odd = weighted([p * c for c in coefs], rows[1::2])
        values += [even + odd, even - odd]
    return values


def grad_points(pairs, rows):
    values = [rows[0]]
    for p in pairs:
        even = weighted([p ** (2 * i) for i in range(len(rows[0::2]))], rows[0::2])
        odd = weighted([p ** (2 * i + 1) for i in range(len(rows[1::2]))], rows[1::2])
        values += [even + odd, even - odd] if odd is not None else [even, even]
    return values


def write_points(x_ref, base, v_ref, done, blocks, out_rows):
    pairs, filters = points_for(out_rows)
    count = len(filters)
    lon_regs = x_ref.shape[2] // 8

    def body(step, carry):
        tile = step // lon_regs
        lon = pl.ds(pl.multiple_of(step % lon_regs * 8, 8), 8)

        def block(k, carry):
            rows = [x_ref[tile, base + k * out_rows + r, lon, :] for r in range(count)]
            for i, value in enumerate(data_points(pairs, rows)):
                v_ref[tile, (done + k) * count + i, lon, :] = value
            return carry

        return lax.fori_loop(0, blocks, block, carry, unroll=blocks <= 4)

    lax.fori_loop(0, 2 * lon_regs, body, 0)


def filter_points(taps_ref, out_rows, u_ref, flip):
    for k, coefs in enumerate(points_for(out_rows)[1]):
        coefs = coefs[::-1] if flip else coefs
        for t in range(2):
            u_ref[t, k, 0:KS, :] = weighted(
                coefs, [taps_ref[t, pl.ds(a * KS, KS), :] for a in range(KS)]
            )


def depthwise_block(v_ref, u_ref, block, out_rows, lon_pad, store, flip):
    pairs, filters = points_for(out_rows)
    count = len(filters)
    chunk = lon_pad

    def body(step, carry):
        tile = step // (lon_pad // chunk)
        lon = pl.multiple_of(step % (lon_pad // chunk) * chunk, 8)

        def product(k):
            total = None
            for b in range(KS):
                tap = KS - 1 - b if flip else b
                term = v_ref[tile, block * count + k, pl.ds(lon + b, chunk), :]
                term = term * u_ref[tile, k, pl.ds(tap, 1), :]
                total = term if total is None else total + term
            return total

        sums = [None] * out_rows
        sums[0] = product(0)
        for i, p in enumerate(pairs):
            plus, minus = product(2 * i + 1), product(2 * i + 2)
            even, odd = plus + minus, plus - minus
            for r in range(out_rows):
                term = odd if r % 2 else even
                term = term if p**r == 1.0 else term * p**r
                sums[r] = term if sums[r] is None else sums[r] + term
        store(tile, lon, chunk, sums)
        return carry

    lax.fori_loop(0, 2 * (lon_pad // chunk), body, 0)


def layer_kernel(order, starts, rows, lon_pad, block_rows, conv_rows, inner, outer,
                 me_ref, gathered_ref, inner_ref, outer_ref, feat_ref, up_ref,
                 out_ref, gconv_ref, gin_ref, gout_ref, sums_ref, flipped_ref,
                 u_ref, taps_ref, w_ref, win_ref, wout_ref, wo32_ref, conv_ref, act_ref, gpre_ref):
    me = me_ref[0]
    window = gathered_ref.shape[1]
    w_ref[:, 0:8, :] = jnp.zeros_like(w_ref[:, 0:8, :])
    w_ref[:, starts[-1] :, :] = jnp.zeros_like(w_ref[:, starts[-1] :, :])
    for position, start in zip(order, starts):
        share = gathered_ref[position ^ me].astype(F32)
        for t in range(2):
            part = share[:, t * LANES : (t + 1) * LANES]
            first = w_ref[t, pl.ds(start, 1), :] + part[0:1]
            w_ref[t, pl.ds(start, window), :] = part
            w_ref[t, pl.ds(start, 1), :] = first
    rest = lax.broadcasted_iota(jnp.int32, (CP - C, LANES), 0)
    mains = get_rows(w_ref, 0, C)
    biases = get_rows(w_ref, ROW_BIAS_IN, 1)
    for j in range(TILES):
        bias = jnp.where(rest == 0, biases[j], 0.0)
        whole = jnp.concatenate([mains[j], bias], axis=0)
        win_ref[:, j * LANES : (j + 1) * LANES] = whole.astype(BF16)
    out_rows = get_rows(w_ref, ROW_OUT, C)
    tail_rows = get_rows(w_ref, ROW_TAPS, 16)
    for quarter in range(4):
        pair = split_quarter(out_rows, quarter)
        tail = split_quarter(tail_rows, quarter)
        for t in range(2):
            wo32_ref[t, pl.ds(quarter, C, stride=4), :] = pair[t]
            taps_ref[t, pl.ds(quarter, 16, stride=4), :] = tail[t]
    for t in range(2):
        wout_ref[:, t * LANES : (t + 1) * LANES] = wo32_ref[t].astype(BF16)

    def vector(row, quarter):
        at = (row - ROW_TAPS) * 4 + quarter
        return [taps_ref[t, pl.ds(at, 1), :] for t in range(2)]

    filter_points(taps_ref, conv_rows, u_ref, False)
    filter_points(taps_ref, conv_rows, flipped_ref, True)
    cbias = vector(ROW_NORM, 1)
    gain = vector(ROW_NORM, 2)
    shift = vector(ROW_NORM, 3)
    bias_out = vector(ROW_LAST, 0)
    scale = vector(ROW_LAST, 1)
    lane = lax.broadcasted_iota(jnp.int32, (1, LANES), 1)
    inside = (lane < C - LANES).astype(F32)
    shift[1] = shift[1] + (lane == C - LANES).astype(F32)

    gin_ref[...] = jnp.zeros_like(gin_ref)
    gout_ref[...] = jnp.zeros_like(gout_ref)
    sums_ref[...] = jnp.zeros_like(sums_ref)
    cells = block_rows * lon_pad

    def partial(values):
        return values.reshape(cells // 8, 8, LANES).sum(axis=0)

    for v_ref, ranges in ((inner_ref, inner), (outer_ref, outer)):

        def conv_step(place, block, v_ref=v_ref):
            def store(tile, lon, chunk, sums):
                for r in range(conv_rows):
                    conv_ref[tile, block * conv_rows + r, pl.ds(lon, chunk), :] = sums[r]

            depthwise_block(v_ref, u_ref, place, conv_rows, lon_pad, store, False)

        over_blocks(ranges, conv_step)

    def body(block, carry):
        row = block * block_rows
        conv = [
            conv_ref[t, pl.ds(row, block_rows)].reshape(cells, LANES) + cbias[t] for t in range(2)
        ]
        mean = jnp.sum(conv[0] + conv[1], axis=1, keepdims=True) * (1.0 / C)
        centred = [conv[0] - mean, (conv[1] - mean) * inside]
        square = centred[0] * centred[0] + centred[1] * centred[1]
        inv_std = lax.rsqrt(jnp.sum(square, axis=1, keepdims=True) * (1.0 / C) + EPSILON)
        standard = [c * inv_std for c in centred]
        normed = jnp.concatenate(
            [(standard[t] * gain[t] + shift[t]).astype(BF16) for t in range(2)], axis=1
        )
        upstream = up_ref[pl.ds(row, block_rows)].reshape(cells, CP)
        ups = [upstream[:, t * LANES : (t + 1) * LANES].astype(F32) for t in range(2)]
        grad_branch = [(scale[t] * ups[t]).astype(BF16) for t in range(2)]
        gbranch = jnp.concatenate(grad_branch, axis=1)
        for h in range(0, H, CHUNK):
            hidden = slice(h, h + CHUNK)
            pre = jnp.dot(normed, win_ref[:, hidden], preferred_element_type=F32)
            gact = lax.dot_general(gbranch, wout_ref[hidden, :], ALL, preferred_element_type=F32)
            square = pre * pre
            half = 0.5 + 0.5 * jnp.tanh(pre * (GELU_A + GELU_B * square))
            act = pre * half
            slope = half + act * (1.0 - half) * (2.0 * GELU_A + 6.0 * GELU_B * square)
            act_ref[:, hidden] = act.astype(BF16)
            gpre_ref[:, hidden] = (gact * slope).astype(BF16)
        act = act_ref[...]
        gpre = gpre_ref[...]
        branch = jnp.dot(act, wout_ref[...], preferred_element_type=F32)
        gnormed = lax.dot_general(gpre, win_ref[...], ALL, preferred_element_type=F32)
        gin_ref[...] += lax.dot_general(normed, gpre, OVER, preferred_element_type=F32)
        gout_ref[...] += lax.dot_general(gbranch, act, OVER, preferred_element_type=F32)
        outs = []
        gs = []
        gn = []
        for t in range(2):
            lanes = slice(t * LANES, (t + 1) * LANES)
            branch_t = branch[:, lanes] + bias_out[t]
            feat = feat_ref[pl.ds(row, block_rows), :, lanes].reshape(cells, LANES).astype(F32)
            outs.append((feat + scale[t] * branch_t).astype(BF16))
            gn.append(gnormed[:, lanes])
            sums_ref[4, t] += partial(branch_t * ups[t])
            sums_ref[3, t] += partial(grad_branch[t].astype(F32))
            sums_ref[1, t] += partial(gn[t] * standard[t])
            sums_ref[2, t] += partial(gn[t])
            gs.append(gn[t] * gain[t])
        mean_g = jnp.sum(gs[0] + gs[1], axis=1, keepdims=True) * (1.0 / C)
        both = gs[0] * standard[0] + gs[1] * standard[1]
        mean_gs = jnp.sum(both, axis=1, keepdims=True) * (1.0 / C)
        gconv = []
        for t in range(2):
            grad = ((gs[t] - mean_g - standard[t] * mean_gs) * inv_std).astype(BF16)
            sums_ref[0, t] += partial(grad.astype(F32))
            gconv.append(grad)
        gconv_ref[pl.ds(row, block_rows)] = jnp.concatenate(gconv, axis=1).reshape(
            block_rows, lon_pad, CP
        )
        out = jnp.concatenate(outs, axis=1).reshape(block_rows, lon_pad, CP)
        out_ref[pl.ds(row, block_rows)] = out[:, : out_ref.shape[1], :C]
        return carry

    lax.fori_loop(0, rows // block_rows, body, 0)


def taps_kernel(order, starts, rows, lon_pad, block_rows, conv_rows, inner, outer,
                me_ref, gconv_ref, inner_ref, outer_ref, gin_ref, gout_ref, sums_ref, done_ref,
                g_ref, done_hbm, rows_ref, acc_ref, wo32_ref, small_ref, done_sem):
    done_copy = pltpu.make_async_copy(done_ref, done_hbm, done_sem)
    done_copy.start()
    acc_ref[...] = jnp.zeros_like(acc_ref)
    pairs, filters = points_for(conv_rows)
    count = len(filters)

    for v_ref, ranges in ((inner_ref, inner), (outer_ref, outer)):

        def step(place, block, v_ref=v_ref):
            def side(tile, carry):
                lanes = pl.ds(pl.multiple_of(tile * LANES, LANES), LANES)
                grads = grad_points(
                    pairs,
                    [
                        gconv_ref[block * conv_rows + r, :, lanes].astype(F32)
                        for r in range(conv_rows)
                    ],
                )
                for k in range(count):
                    for b in range(KS):
                        term = grads[k] * v_ref[tile, place * count + k, pl.ds(b, lon_pad), :]
                        acc_ref[tile, k, b] += term.reshape(lon_pad // 8, 8, LANES).sum(axis=0)
                return carry

            lax.fori_loop(0, 2, side, 0)

        over_blocks(ranges, step)

    rows_ref[...] = jnp.zeros_like(rows_ref)
    small_ref[...] = jnp.zeros_like(small_ref)
    for t in range(2):
        totals = [jnp.sum(acc_ref[t, k], axis=1) for k in range(count)]
        for a in range(KS):
            small_ref[t, pl.ds(a * KS, KS), :] = weighted([f[a] for f in filters], totals)
        for at, k in ((TAPS, 0), (TAPS + 1, 1), (TAPS + 2, 2), (TAPS + 7, 3), (TAPS + 8, 4)):
            small_ref[t, pl.ds(at, 1), :] = jnp.sum(sums_ref[k, t], axis=0, keepdims=True)
        wo32_ref[t] = gout_ref[pl.ds(t * LANES, LANES), :].T
    outs = join_quarters(
        [[wo32_ref[t, pl.ds(q, C, stride=4), :] for t in range(2)] for q in range(4)]
    )
    tails = join_quarters(
        [[small_ref[t, pl.ds(q, 16, stride=4), :] for t in range(2)] for q in range(4)]
    )
    put_rows(rows_ref, 0, [gin_ref[pl.ds(0, C), j * LANES : (j + 1) * LANES] for j in range(TILES)])
    put_rows(rows_ref, ROW_OUT, outs)
    put_rows(rows_ref, ROW_TAPS, tails)
    put_rows(
        rows_ref,
        ROW_BIAS_IN,
        [gin_ref[pl.ds(C, 1), j * LANES : (j + 1) * LANES] for j in range(TILES)],
    )
    me = me_ref[0]
    window = g_ref.shape[1]
    for position, start in zip(order, starts):
        share = [rows_ref[t, pl.ds(start, window), :] for t in range(2)]
        g_ref[position ^ me] = jnp.concatenate(share, axis=1).astype(BF16)
    done_copy.wait()


def field_kernel(ranges, rows, cols, lon_pad, conv_rows, lat_halos, before, last, begun,
                 u_ref, up_ref, main_ref, west_ref, east_ref, *rest):
    rest = list(rest)
    south_ref, north_ref = (rest.pop(0), rest.pop(0)) if lat_halos else (None, None)
    before_ref = rest.pop(0) if before else None
    if begun:
        rest.pop(0)
    out_hbm = rest.pop(0) if before or last else None
    out_ref = None if last else rest.pop(0)
    x_ref, v_ref, sum_ref, before_sem, out_sem, own_ref = rest
    out_ref = own_ref if last else out_ref
    if before:
        before_copy = pltpu.make_async_copy(before_ref, out_hbm.at[pl.ds(*before)], before_sem)
        before_copy.start()
    field_points(
        ranges, conv_rows, x_ref, v_ref, main_ref, west_ref, east_ref, south_ref, north_ref, rows,
        cols,
    )

    def step(place, block):
        row = block * conv_rows

        def store(tile, lon, chunk, sums):
            lanes = pl.ds(pl.multiple_of(tile * LANES, LANES), LANES)
            for r in range(conv_rows):
                total = sums[r] + up_ref[row + r, pl.ds(lon, chunk), lanes].astype(F32)
                sum_ref[r, pl.ds(lon, chunk), lanes] = total

        depthwise_block(v_ref, u_ref, place, conv_rows, lon_pad, store, True)
        out_ref[pl.ds(place * conv_rows, conv_rows)] = sum_ref[:, 0:cols, 0:C].astype(BF16)
        if last:
            out_copy(place, block).start()

    def out_copy(place, block):
        return pltpu.make_async_copy(
            out_ref.at[pl.ds(place * conv_rows, conv_rows)],
            out_hbm.at[pl.ds(block * conv_rows, conv_rows)],
            out_sem.at[place],
        )

    over_blocks(ranges, step)
    if last:
        over_blocks(ranges, lambda place, block: out_copy(place, block).wait())
    if before:
        before_copy.wait()


def shape(dims, kind):
    return jax.ShapeDtypeStruct(dims, kind)


def whole(count):
    return [pl.BlockSpec(memory_space=pltpu.VMEM)] * count


def cost(micros):
    return pl.CostEstimate(flops=int(micros * 1.1e9), bytes_accessed=0, transcendentals=0)


def body(features, params, langevin_noise, upstream):
    rows, cols = features.shape[:2]
    lon_pad = up(cols, 16)
    lon_wide = up(lon_pad + KS - 1, 8)
    conv_rows = max(r for r in (1, 3, 5) if rows % r == 0)
    points = conv_rows + KS - 1
    blocks = rows // conv_rows
    block_rows = max(r for r in range(1, 16) if rows % r == 0 and r % conv_rows == 0)
    groups, bits = exchange_groups()
    count = 1 << bits
    lat_size = lax.axis_size("lat")
    length = params.shape[0]
    number = lax.axis_index("lon") * lat_size + lax.axis_index("lat")
    place = jnp.int32(0)
    for k in range(bits):
        place = place | (((number >> k) & 1) << (bits - 1 - k))
    place = place.reshape(1).astype(jnp.int32)
    offset = (number * length) % SHARE_LANES
    order = [reversed_bits(s, bits) for s in range(count)]
    starts = [s * length // SHARE_LANES for s in range(count)]
    spill = SHARE_LANES - math.gcd(SHARE_LANES, length)
    window = up(-(-(length + spill) // SHARE_LANES), 8)
    flat_rows = up(max(starts[-1] + window, 3 * (ROWS + 1)), 8)

    share = jnp.pad(params, (SHARE_LANES, window * SHARE_LANES - length))
    share = lax.dynamic_slice(share, (SHARE_LANES - offset,), (window * SHARE_LANES,)).astype(BF16)
    gathered = share.reshape(1, window, SHARE_LANES)
    compiler_params = pltpu.CompilerParams(vmem_limit_bytes=VMEM)
    smem = [pl.BlockSpec(memory_space=pltpu.SMEM)]
    margin = -(-RAD // conv_rows)
    inner = [(margin, blocks - 2 * margin)]
    outer = [(0, margin), (blocks - margin, margin)]
    edges = pl.pallas_call(
        lambda *refs: edge_kernel(cols, *refs),
        out_shape=(shape((rows, RAD, C), BF16),) * 2,
        in_specs=[pl.BlockSpec(memory_space=pltpu.HBM)],
        out_specs=tuple(whole(2)),
        scratch_shapes=[pltpu.VMEM((rows, cols, C), BF16)],
        compiler_params=compiler_params,
        cost_estimate=cost(1),
        name="edges",
    )(features)
    for k, group in enumerate(groups):
        parts = [swap(gathered, mask) for mask in group]
        if k == min(1, len(groups) - 1):
            west, east = shift_both(*edges, "lon", True)
        if k == max(0, len(groups) - 2):
            west, east, _, upstream = lax.optimization_barrier((west, east, gathered, upstream))
            wides = pl.pallas_call(
                lambda *refs: wide_kernel(rows, cols, *refs),
                out_shape=(shape((RAD, cols + 2 * RAD, C), BF16),) * 2,
                in_specs=whole(3),
                out_specs=tuple(whole(2)),
                compiler_params=compiler_params,
                cost_estimate=cost(1),
                name="wides",
            )(features, west, east)
            south, north = shift_both(*wides, "lat", False)
            inner_data, feats, ups = pl.pallas_call(
                lambda *refs: inner_kernel(inner, rows, cols, conv_rows, *refs),
                out_shape=(
                    shape((2, block_count(inner) * points, lon_wide, LANES), F32),
                    shape((rows, lon_pad, CP), BF16),
                    shape((rows, lon_pad, CP), BF16),
                ),
                in_specs=whole(4),
                out_specs=tuple(whole(3)),
                scratch_shapes=[pltpu.VMEM((2, padded_rows(inner, conv_rows), lon_wide, LANES), F32)],
                compiler_params=compiler_params,
                cost_estimate=cost(2.5),
                name="inner",
            )(features, west, east, upstream)
        gathered = jnp.concatenate([gathered, *parts], axis=0)
        if k == 0:
            edges, _ = lax.optimization_barrier((edges, gathered))
        if k == max(0, len(groups) - 2):
            gathered, inner_data = lax.optimization_barrier((gathered, inner_data))

    outer_data = pl.pallas_call(
        lambda *refs: outer_kernel(outer, rows, cols, conv_rows, *refs),
        out_shape=shape((2, block_count(outer) * points, lon_wide, LANES), F32),
        in_specs=whole(5),
        out_specs=whole(1)[0],
        scratch_shapes=[pltpu.VMEM((2, padded_rows(outer, conv_rows), lon_wide, LANES), F32)],
        compiler_params=compiler_params,
        cost_estimate=cost(1),
        name="outer",
    )(features, west, east, south, north)

    static = (order, starts, rows, lon_pad, block_rows, conv_rows, inner, outer)
    output, gconv, gin, gout, sums, flipped = pl.pallas_call(
        lambda *refs: layer_kernel(*static, *refs),
        out_shape=(
            shape((rows, cols, C), BF16),
            shape((rows, lon_pad, CP), BF16),
            shape((CP, H), F32),
            shape((CP, H), F32),
            shape((5, 2, 8, LANES), F32),
            shape((2, points, 8, LANES), F32),
        ),
        in_specs=smem + whole(5),
        out_specs=tuple(whole(6)),
        scratch_shapes=[
            pltpu.VMEM((2, points, 8, LANES), F32),
            pltpu.VMEM((2, 64, LANES), F32),
            pltpu.VMEM((2, flat_rows, LANES), F32),
            pltpu.VMEM((CP, H), BF16),
            pltpu.VMEM((H, CP), BF16),
            pltpu.VMEM((2, H, LANES), F32),
            pltpu.VMEM((2, rows, lon_pad, LANES), F32),
            pltpu.VMEM((block_rows * lon_pad, H), BF16),
            pltpu.VMEM((block_rows * lon_pad, H), BF16),
        ],
        compiler_params=compiler_params,
        cost_estimate=cost(22),
        name="layer",
    )(place, gathered, inner_data, outer_data, feats, ups)

    values, output = pl.pallas_call(
        lambda *refs: taps_kernel(*static, *refs),
        out_shape=(
            shape((count, window, SHARE_LANES), BF16),
            shape((rows, cols, C), BF16),
        ),
        in_specs=smem + whole(7),
        out_specs=(*whole(1), pl.BlockSpec(memory_space=pl.ANY)),
        scratch_shapes=[
            pltpu.VMEM((2, flat_rows, LANES), F32),
            pltpu.VMEM((2, points, KS, 8, LANES), F32),
            pltpu.VMEM((2, H, LANES), F32),
            pltpu.VMEM((2, 64, LANES), F32),
            pltpu.SemaphoreType.DMA(()),
        ],
        compiler_params=compiler_params,
        cost_estimate=cost(11),
        name="taps",
    )(place, gconv, inner_data, outer_data, gin, gout, sums, output)

    west, east = shift_both(gconv[:, :RAD, :C], gconv[:, cols - RAD : cols, :C], "lon", True)
    field = None

    def field_piece(ranges, lat_halos, before, field, last):
        count = block_count(ranges)
        own = shape((count * conv_rows, cols, C), BF16)
        operands = [flipped, ups, gconv, west, east, *lat_halos]
        in_specs = whole(len(operands))
        span = None
        if before is not None:
            span = (before[0], before[1].shape[0])
            operands.append(before[1])
            in_specs += whole(1)
        if field is not None:
            operands.append(field)
            in_specs.append(pl.BlockSpec(memory_space=pl.ANY))
        out_shape = []
        out_specs = []
        if before is not None or last:
            out_shape.append(shape((rows, cols, C), BF16))
            out_specs.append(pl.BlockSpec(memory_space=pl.ANY))
        if not last:
            out_shape.append(own)
            out_specs += whole(1)
        results = pl.pallas_call(
            lambda *refs: field_kernel(
                ranges, rows, cols, lon_pad, conv_rows, bool(lat_halos), span, last,
                field is not None, *refs
            ),
            out_shape=tuple(out_shape),
            in_specs=in_specs,
            out_specs=tuple(out_specs),
            scratch_shapes=[
                pltpu.VMEM((2, padded_rows(ranges, conv_rows), lon_wide, LANES), F32),
                pltpu.VMEM((2, count * points, lon_wide, LANES), F32),
                pltpu.VMEM((conv_rows, lon_pad, CP), F32),
                pltpu.SemaphoreType.DMA(()),
                pltpu.SemaphoreType.DMA((count,)),
                pltpu.VMEM(own.shape if last else (8, LANES), BF16),
            ],
            input_output_aliases={} if field is None else {len(operands) - 1: 0},
            compiler_params=compiler_params,
            cost_estimate=cost(1.1 * count),
            name="field",
        )(*operands)
        return (None if last else results[-1]), (results[0] if out_shape[0] is not own else None)

    early = (inner[0][1] + 1) // 2
    for k, group in enumerate(groups[::-1]):
        if k > 2:
            values, piece = lax.optimization_barrier((values, piece))
        if k == min(1, len(groups) - 1):
            values, west, east = lax.optimization_barrier((values, west, east))
        part = values.shape[0] // (len(group) + 1)
        sent = [values[(i + 1) * part : (i + 2) * part].astype(BF16) for i in range(len(group))]
        if k == min(1, len(groups) - 1):

            def wide(at):
                return jnp.concatenate([west[at], gconv[at, :cols, :C], east[at]], axis=1)

            wides = (wide(slice(0, RAD)), wide(slice(rows - RAD, rows)))
        received = [swap(one, mask) for one, mask in zip(sent, group)]
        if k == min(1, len(groups) - 1):
            piece, _ = field_piece([(margin, early)], (), None, None, False)
        if k == min(2, len(groups) - 1):
            lat_halos = shift_both(*wides, "lat", False)
            piece, _ = lax.optimization_barrier((piece, values))
            at = margin * conv_rows
            late = [(margin + early, inner[0][1] - early)]
            piece, field = field_piece(late, (), (at, piece), None, False)
        values = values[:part].astype(F32)
        for other in received:
            values = values + other.astype(F32)
        if k == 1 and len(groups) > 2:
            values, wides = lax.optimization_barrier((values, wides))
    at = (margin + early) * conv_rows
    _, field = field_piece(outer, lat_halos, (at, piece), field, True)
    summed = lax.dynamic_slice(values.reshape(-1), (offset,), (length,))
    new_params = params - STEP_SIZE * summed + NOISE_COEF * langevin_noise
    return (output, field, new_params)


def solution(mesh):
    return jax.shard_map(
        body,
        mesh=mesh,
        in_specs=(
            P("lat", "lon", None),
            P(("lon", "lat")),
            P(("lon", "lat")),
            P("lat", "lon", None),
        ),
        out_specs=(P("lat", "lon", None), P("lat", "lon", None), P(("lon", "lat"))),
        check_vma=False,
    )
```

```python
import math

import jax
import jax.numpy as jnp
from jax import lax
from jax.experimental import pallas as pl
from jax.experimental.pallas import tpu as pltpu
from jax.sharding import PartitionSpec as P

C = 192
H = 768
KS = 7
RAD = KS // 2
LANES = 128
CP = 256
TAPS = KS * KS
EPSILON = 1e-06
STEP_SIZE = 0.003
NOISE_COEF = 0.08
GELU_A = math.sqrt(2.0 / math.pi)
GELU_B = GELU_A * 0.044715
F32 = jnp.float32
BF16 = jnp.bfloat16
ROW_OUT = C
ROW_TAPS = 2 * C
ROW_NORM = ROW_TAPS + TAPS // 4
ROW_BIAS_IN = ROW_NORM + 1
ROW_LAST = ROW_NORM + 2
ROWS = ROW_LAST + 1
TILES = H // LANES
SHARE_LANES = 256
CHUNK = 256
GIN_ROWS = C + 8
ALL = ((1,), (1,)), ((), ())
OVER = ((0,), (0,)), ((), ())
VMEM = 28 << 20


def exchange_groups():
    lon, lat = lax.axis_size("lon"), lax.axis_size("lat")
    bits = [(lon >> k, 0) for k in range(1, lon.bit_length())]
    bits += [(0, lat >> k) for k in range(1, lat.bit_length())]
    groups = []
    k = 0
    while k < len(bits):
        if k + 1 < len(bits) and bits[k][0] == 1 and bits[k + 1][0] == 0:
            (lon_bit, _), (_, lat_bit) = bits[k : k + 2]
            groups.append([(lon_bit, 0), (0, lat_bit), (lon_bit, lat_bit)])
            k += 2
        else:
            groups.append([bits[k]])
            k += 1
    return groups, len(bits)


def swap(values, mask):
    lon, lat = lax.axis_size("lon"), lax.axis_size("lat")
    pairs = [
        (i * lat + j, (i ^ mask[0]) * lat + (j ^ mask[1])) for i in range(lon) for j in range(lat)
    ]
    return lax.ppermute(values, ("lon", "lat"), pairs)


def send_edges(low_edge, high_edge, axis, periodic):
    count = lax.axis_size(axis)
    even = lax.axis_index(axis) % 2 == 0
    near = [(i, i ^ 1) for i in range(count)]
    odds = [(i, (i + 1) % count) for i in range(1, count if periodic else count - 1, 2)]
    far = odds + [(target, source) for source, target in odds]
    near = lax.ppermute(jnp.where(even, high_edge, low_edge), axis, near)
    far = lax.ppermute(jnp.where(even, low_edge, high_edge), axis, far)
    return near, far


def edges_from(near, far, axis):
    even = lax.axis_index(axis) % 2 == 0
    return jnp.where(even, far, near), jnp.where(even, near, far)


def shift_both(low_edge, high_edge, axis, periodic):
    return edges_from(*send_edges(low_edge, high_edge, axis, periodic), axis)


def reversed_bits(number, count):
    result = 0
    for k in range(count):
        result |= ((number >> k) & 1) << (count - 1 - k)
    return result


def up(value, multiple):
    return -(-value // multiple) * multiple


def split_quarter(tiles, quarter):
    lane = lax.broadcasted_iota(jnp.int32, tiles[0].shape, 1)
    low = lane < LANES // 2
    first = 3 * quarter // 2
    if quarter % 2 == 0:
        return tiles[first], jnp.where(low, tiles[first + 1], 0.0)
    left = pltpu.roll(tiles[first], LANES // 2, 1)
    right = pltpu.roll(tiles[first + 1], LANES // 2, 1)
    return jnp.where(low, left, right), jnp.where(low, right, 0.0)


def join_quarters(quarters):
    lane = lax.broadcasted_iota(jnp.int32, quarters[0][0].shape, 1)
    low = lane < LANES // 2
    tiles = []
    for even in (0, 2):
        first, second = quarters[even]
        turned = pltpu.roll(quarters[even + 1][0], LANES // 2, 1)
        last = pltpu.roll(quarters[even + 1][1], LANES // 2, 1)
        tiles += [first, jnp.where(low, second, turned), jnp.where(low, turned, last)]
    return tiles


def get_rows(flat_ref, row, count):
    return [
        flat_ref[j % 2, pl.ds(3 * row + j // 2, count, stride=3), :] for j in range(TILES)
    ]


def put_rows(flat_ref, row, tiles):
    for j in range(TILES):
        flat_ref[j % 2, pl.ds(3 * row + j // 2, tiles[j].shape[0], stride=3), :] = tiles[j]


def assemble(x_ref, base, first, count, main, west, east, south, north, rows, cols):
    for t in range(2):
        lanes = slice(t * LANES, min(C, (t + 1) * LANES))
        width = slice(0, lanes.stop - lanes.start)
        low = max(0, first - RAD)
        high = min(rows, first + count - RAD)
        at = slice(base + low + RAD - first, base + high + RAD - first)
        if main.shape[2] == CP:
            span = slice(RAD, RAD + main.shape[1])
            x_ref[t, at, span, :] = main[low:high, :, t * LANES : (t + 1) * LANES].astype(F32)
        else:
            x_ref[t, at, RAD : RAD + cols, width] = main[low:high, 0:cols, lanes].astype(F32)
        x_ref[t, at, 0:RAD, width] = west[low:high, :, lanes].astype(F32)
        x_ref[t, at, RAD + cols : 2 * RAD + cols, width] = east[low:high, :, lanes].astype(F32)
        wide = slice(0, cols + 2 * RAD)
        if first < RAD:
            at = slice(base, base + RAD - first)
            x_ref[t, at] = jnp.zeros_like(x_ref[t, at])
            x_ref[t, at, wide, width] = south[first:, :, lanes].astype(F32)
        over = first + count - rows - RAD
        if over > 0:
            at = slice(base + count - over, base + count)
            x_ref[t, at] = jnp.zeros_like(x_ref[t, at])
            x_ref[t, at, wide, width] = north[0:over, :, lanes].astype(F32)


def field_points(ranges, conv_rows, x_ref, v_ref, main, west, east, south, north, rows, cols):
    if main.shape[1:] == (x_ref.shape[2] - 8, CP):
        for t in range(2):
            for lon in (0, x_ref.shape[2] - 8):
                x_ref[t, :, lon : lon + 8, :] = jnp.zeros_like(x_ref[t, :, lon : lon + 8, :])
    else:
        x_ref[...] = jnp.zeros_like(x_ref)
    base = done = 0
    for first, count in ranges:
        span = count * conv_rows + KS - 1
        assemble(
            x_ref, base, first * conv_rows, span, main, west, east, south, north, rows, cols
        )
        write_points(x_ref, base, v_ref, done, count, conv_rows)
        base += span
        done += count


def padded_rows(ranges, conv_rows):
    return sum(count * conv_rows + KS - 1 for _, count in ranges)


def block_count(ranges):
    return sum(count for _, count in ranges)


def over_blocks(ranges, step):
    done = 0
    for first, count in ranges:

        def body(i, carry, done=done, first=first):
            step(done + i, first + i)
            return carry

        lax.fori_loop(0, count, body, 0)
        done += count


def edge_kernel(cols, field_hbm, west_ref, east_ref, field_ref):
    pltpu.sync_copy(field_hbm, field_ref)
    west_ref[...] = field_ref[:, 0:RAD, :]
    east_ref[...] = field_ref[:, cols - RAD : cols, :]


def wide_kernel(rows, cols, field_ref, west_ref, east_ref, south_ref, north_ref):
    for out_ref, first in ((south_ref, 0), (north_ref, rows - RAD)):
        at = slice(first, first + RAD)
        out_ref[:, 0:RAD, :] = west_ref[at]
        out_ref[:, RAD : RAD + cols, :] = field_ref[at, 0:cols, :]
        out_ref[:, RAD + cols : 2 * RAD + cols, :] = east_ref[at]


def inner_kernel(ranges, rows, cols, conv_rows, feat_ref, west_ref, east_ref, up_ref,
                 v_ref, feats_ref, ups_ref, x_ref):
    field_points(
        ranges, conv_rows, x_ref, v_ref, feat_ref, west_ref, east_ref, None, None, rows, cols
    )
    feats_ref[...] = jnp.zeros_like(feats_ref)
    feats_ref[:, 0:cols, 0:C] = feat_ref[...]
    ups_ref[...] = jnp.zeros_like(ups_ref)
    ups_ref[:, 0:cols, 0:C] = up_ref[...]


def outer_kernel(ranges, rows, cols, conv_rows, feat_ref, west_ref, east_ref, south_ref, north_ref,
                 v_ref, x_ref):
    field_points(
        ranges, conv_rows, x_ref, v_ref, feat_ref, west_ref, east_ref, south_ref, north_ref, rows,
        cols,
    )


def points_for(out_rows):
    pairs = [1.0, 0.5, 2.0, 1.5, 0.75][: (out_rows + KS - 2) // 2]
    points = [0.0] + [sign * p for p in pairs for sign in (1.0, -1.0)]
    filters = []
    for k, point in enumerate(points):
        scale = math.prod(point - other for i, other in enumerate(points) if i != k)
        filters.append([point**a / scale for a in range(KS)])
    return pairs, filters


def polynomial(roots):
    coefs = [1.0]
    for root in roots:
        coefs = [
            (coefs[i - 1] if i else 0.0) - (root * coefs[i] if i < len(coefs) else 0.0)
            for i in range(len(coefs) + 1)
        ]
    return coefs


def weighted(coefs, values):
    total = None
    for coef, value in zip(coefs, values):
        if coef == 0.0:
            continue
        term = value if coef == 1.0 else value * coef
        total = term if total is None else total + term
    return total


def data_points(pairs, rows):
    squares = [p * p for p in pairs]
    values = [weighted(polynomial(squares), rows[0::2])]
    for p in pairs:
        coefs = polynomial([q for q in squares if q != p * p])
        even = weighted(coefs, rows[2::2])
        odd = weighted([p * c for c in coefs], rows[1::2])
        values += [even + odd, even - odd]
    return values


def grad_points(pairs, rows):
    values = [rows[0]]
    for p in pairs:
        even = weighted([p ** (2 * i) for i in range(len(rows[0::2]))], rows[0::2])
        odd = weighted([p ** (2 * i + 1) for i in range(len(rows[1::2]))], rows[1::2])
        values += [even + odd, even - odd] if odd is not None else [even, even]
    return values


def write_points(x_ref, base, v_ref, done, blocks, out_rows):
    pairs, filters = points_for(out_rows)
    count = len(filters)
    lon_regs = x_ref.shape[2] // 8

    def body(step, carry):
        tile = step // lon_regs
        lon = pl.ds(pl.multiple_of(step % lon_regs * 8, 8), 8)

        def block(k, carry):
            rows = [x_ref[tile, base + k * out_rows + r, lon, :] for r in range(count)]
            for i, value in enumerate(data_points(pairs, rows)):
                v_ref[tile, (done + k) * count + i, lon, :] = value
            return carry

        return lax.fori_loop(0, blocks, block, carry, unroll=True)

    lax.fori_loop(0, 2 * lon_regs, body, 0)


def filter_points(taps_ref, out_rows, u_ref, flip):
    for k, coefs in enumerate(points_for(out_rows)[1]):
        coefs = coefs[::-1] if flip else coefs
        for t in range(2):
            u_ref[t, k, 0:KS, :] = weighted(
                coefs, [taps_ref[t, pl.ds(a * KS, KS), :] for a in range(KS)]
            )


def depthwise_block(v_ref, u_ref, block, out_rows, lon_pad, store, flip, unroll):
    pairs, filters = points_for(out_rows)
    count = len(filters)
    chunk = lon_pad

    def body(step, carry):
        tile = step // (lon_pad // chunk)
        lon = pl.multiple_of(step % (lon_pad // chunk) * chunk, 8)

        def product(k):
            total = None
            for b in range(KS):
                tap = KS - 1 - b if flip else b
                term = v_ref[tile, block * count + k, pl.ds(lon + b, chunk), :]
                term = term * u_ref[tile, k, pl.ds(tap, 1), :]
                total = term if total is None else total + term
            return total

        sums = [None] * out_rows
        sums[0] = product(0)
        for i, p in enumerate(pairs):
            plus, minus = product(2 * i + 1), product(2 * i + 2)
            even, odd = plus + minus, plus - minus
            for r in range(out_rows):
                term = odd if r % 2 else even
                term = term if p**r == 1.0 else term * p**r
                sums[r] = term if sums[r] is None else sums[r] + term
        store(tile, lon, chunk, sums)
        return carry

    lax.fori_loop(0, 2 * (lon_pad // chunk), body, 0, unroll=unroll)


def layer_kernel(order, starts, rows, lon_pad, block_rows, conv_rows, inner, outer,
                 me_ref, gathered_ref, inner_ref, outer_ref, feat_ref, up_ref,
                 out_ref, gconv_ref, gin_ref, gout_ref, sums_ref, flipped_ref,
                 u_ref, taps_ref, w_ref, win_ref, wout_ref, wo32_ref, conv_ref, act_ref, gpre_ref):
    me = me_ref[0]
    window = gathered_ref.shape[1]
    w_ref[:, 0:8, :] = jnp.zeros_like(w_ref[:, 0:8, :])
    w_ref[:, starts[-1] :, :] = jnp.zeros_like(w_ref[:, starts[-1] :, :])
    for position, start in zip(order, starts):
        share = gathered_ref[position ^ me].astype(F32)
        for t in range(2):
            part = share[:, t * LANES : (t + 1) * LANES]
            first = w_ref[t, pl.ds(start, 1), :] + part[0:1]
            w_ref[t, pl.ds(start, window), :] = part
            w_ref[t, pl.ds(start, 1), :] = first
    rest = lax.broadcasted_iota(jnp.int32, (CP - C, LANES), 0)
    mains = get_rows(w_ref, 0, C)
    biases = get_rows(w_ref, ROW_BIAS_IN, 1)
    for j in range(TILES):
        bias = jnp.where(rest == 0, biases[j], 0.0)
        whole = jnp.concatenate([mains[j], bias], axis=0)
        win_ref[:, j * LANES : (j + 1) * LANES] = whole.astype(BF16)
    out_rows = get_rows(w_ref, ROW_OUT, C)
    tail_rows = get_rows(w_ref, ROW_TAPS, 16)
    for quarter in range(4):
        pair = split_quarter(out_rows, quarter)
        tail = split_quarter(tail_rows, quarter)
        for t in range(2):
            wo32_ref[t, pl.ds(quarter, C, stride=4), :] = pair[t]
            taps_ref[t, pl.ds(quarter, 16, stride=4), :] = tail[t]
    for t in range(2):
        wout_ref[:, t * LANES : (t + 1) * LANES] = wo32_ref[t].astype(BF16)

    def vector(row, quarter):
        at = (row - ROW_TAPS) * 4 + quarter
        return [taps_ref[t, pl.ds(at, 1), :] for t in range(2)]

    filter_points(taps_ref, conv_rows, u_ref, False)
    filter_points(taps_ref, conv_rows, flipped_ref, True)
    cbias = vector(ROW_NORM, 1)
    gain = vector(ROW_NORM, 2)
    shift = vector(ROW_NORM, 3)
    bias_out = vector(ROW_LAST, 0)
    scale = vector(ROW_LAST, 1)
    lane = lax.broadcasted_iota(jnp.int32, (1, LANES), 1)
    inside = (lane < C - LANES).astype(F32)
    shift[1] = shift[1] + (lane == C - LANES).astype(F32)

    gin_ref[...] = jnp.zeros_like(gin_ref)
    gout_ref[...] = jnp.zeros_like(gout_ref)
    sums_ref[...] = jnp.zeros_like(sums_ref)
    cells = block_rows * lon_pad

    def partial(values):
        return values.reshape(cells // 8, 8, LANES).sum(axis=0)

    for v_ref, ranges in ((inner_ref, inner), (outer_ref, outer)):

        def conv_step(place, block, v_ref=v_ref):
            def store(tile, lon, chunk, sums):
                for r in range(conv_rows):
                    conv_ref[tile, block * conv_rows + r, pl.ds(lon, chunk), :] = sums[r]

            depthwise_block(v_ref, u_ref, place, conv_rows, lon_pad, store, False, False)

        over_blocks(ranges, conv_step)

    def body(block, carry):
        row = block * block_rows
        conv = [
            conv_ref[t, pl.ds(row, block_rows)].reshape(cells, LANES) + cbias[t] for t in range(2)
        ]
        mean = jnp.sum(conv[0] + conv[1], axis=1, keepdims=True) * (1.0 / C)
        centred = [conv[0] - mean, (conv[1] - mean) * inside]
        square = centred[0] * centred[0] + centred[1] * centred[1]
        inv_std = lax.rsqrt(jnp.sum(square, axis=1, keepdims=True) * (1.0 / C) + EPSILON)
        standard = [c * inv_std for c in centred]
        normed = jnp.concatenate(
            [(standard[t] * gain[t] + shift[t]).astype(BF16) for t in range(2)], axis=1
        )
        upstream = up_ref[pl.ds(row, block_rows)].reshape(cells, CP)
        ups = [upstream[:, t * LANES : (t + 1) * LANES].astype(F32) for t in range(2)]
        grad_branch = [(scale[t] * ups[t]).astype(BF16) for t in range(2)]
        gbranch = jnp.concatenate(grad_branch, axis=1)
        for h in range(0, H, CHUNK):
            hidden = slice(h, h + CHUNK)
            pre = jnp.dot(normed, win_ref[:, hidden], preferred_element_type=F32)
            gact = lax.dot_general(gbranch, wout_ref[hidden, :], ALL, preferred_element_type=F32)
            square = pre * pre
            half = 0.5 + 0.5 * jnp.tanh(pre * (GELU_A + GELU_B * square))
            act = pre * half
            slope = half + act * (1.0 - half) * (2.0 * GELU_A + 6.0 * GELU_B * square)
            act_ref[:, hidden] = act.astype(BF16)
            gpre_ref[:, hidden] = (gact * slope).astype(BF16)
        act = act_ref[...]
        gpre = gpre_ref[...]
        branch = jnp.dot(act, wout_ref[...], preferred_element_type=F32)
        gnormed = lax.dot_general(gpre, win_ref[...], ALL, preferred_element_type=F32)
        gin_ref[...] += lax.dot_general(
            normed[:, :GIN_ROWS], gpre, OVER, preferred_element_type=F32
        )
        gout_ref[...] += lax.dot_general(
            gbranch[:, :C], act, OVER, preferred_element_type=F32
        )
        outs = []
        gs = []
        gn = []
        for t in range(2):
            lanes = slice(t * LANES, (t + 1) * LANES)
            branch_t = branch[:, lanes] + bias_out[t]
            feat = feat_ref[pl.ds(row, block_rows), :, lanes].reshape(cells, LANES).astype(F32)
            outs.append((feat + scale[t] * branch_t).astype(BF16))
            gn.append(gnormed[:, lanes])
            sums_ref[4, t] += partial(branch_t * ups[t])
            sums_ref[3, t] += partial(grad_branch[t].astype(F32))
            sums_ref[1, t] += partial(gn[t] * standard[t])
            sums_ref[2, t] += partial(gn[t])
            gs.append(gn[t] * gain[t])
        mean_g = jnp.sum(gs[0] + gs[1], axis=1, keepdims=True) * (1.0 / C)
        both = gs[0] * standard[0] + gs[1] * standard[1]
        mean_gs = jnp.sum(both, axis=1, keepdims=True) * (1.0 / C)
        gconv = []
        for t in range(2):
            grad = ((gs[t] - mean_g - standard[t] * mean_gs) * inv_std).astype(BF16)
            sums_ref[0, t] += partial(grad.astype(F32))
            gconv.append(grad)
        gconv_ref[pl.ds(row, block_rows)] = jnp.concatenate(gconv, axis=1).reshape(
            block_rows, lon_pad, CP
        )
        out = jnp.concatenate(outs, axis=1).reshape(block_rows, lon_pad, CP)
        out_ref[pl.ds(row, block_rows)] = out[:, : out_ref.shape[1], :C]
        return carry

    lax.fori_loop(0, rows // block_rows, body, 0)


def taps_kernel(order, starts, rows, lon_pad, block_rows, conv_rows, inner, outer,
                me_ref, gconv_ref, inner_ref, outer_ref, gin_ref, gout_ref, sums_ref, done_ref,
                g_ref, done_hbm, rows_ref, acc_ref, wo32_ref, small_ref, done_sem):
    done_copy = pltpu.make_async_copy(done_ref, done_hbm, done_sem)
    done_copy.start()
    acc_ref[...] = jnp.zeros_like(acc_ref)
    pairs, filters = points_for(conv_rows)
    count = len(filters)

    for v_ref, ranges in ((inner_ref, inner), (outer_ref, outer)):

        def step(place, block, v_ref=v_ref):
            def side(tile, carry):
                lanes = pl.ds(pl.multiple_of(tile * LANES, LANES), LANES)
                grads = grad_points(
                    pairs,
                    [
                        gconv_ref[block * conv_rows + r, :, lanes].astype(F32)
                        for r in range(conv_rows)
                    ],
                )
                for k in range(count):
                    for b in range(KS):
                        term = grads[k] * v_ref[tile, place * count + k, pl.ds(b, lon_pad), :]
                        acc_ref[tile, k, b] += term.reshape(lon_pad // 8, 8, LANES).sum(axis=0)
                return carry

            lax.fori_loop(0, 2, side, 0, unroll=True)

        over_blocks(ranges, step)

    rows_ref[...] = jnp.zeros_like(rows_ref)
    small_ref[...] = jnp.zeros_like(small_ref)
    for t in range(2):
        totals = [jnp.sum(acc_ref[t, k], axis=1) for k in range(count)]
        for a in range(KS):
            small_ref[t, pl.ds(a * KS, KS), :] = weighted([f[a] for f in filters], totals)
        for at, k in ((TAPS, 0), (TAPS + 1, 1), (TAPS + 2, 2), (TAPS + 7, 3), (TAPS + 8, 4)):
            small_ref[t, pl.ds(at, 1), :] = jnp.sum(sums_ref[k, t], axis=0, keepdims=True)
        width = min(C, (t + 1) * LANES) - t * LANES
        wo32_ref[t, :, 0:width] = gout_ref[pl.ds(t * LANES, width), :].T
    outs = join_quarters(
        [[wo32_ref[t, pl.ds(q, C, stride=4), :] for t in range(2)] for q in range(4)]
    )
    tails = join_quarters(
        [[small_ref[t, pl.ds(q, 16, stride=4), :] for t in range(2)] for q in range(4)]
    )
    put_rows(rows_ref, 0, [gin_ref[pl.ds(0, C), j * LANES : (j + 1) * LANES] for j in range(TILES)])
    put_rows(rows_ref, ROW_OUT, outs)
    put_rows(rows_ref, ROW_TAPS, tails)
    put_rows(
        rows_ref,
        ROW_BIAS_IN,
        [gin_ref[pl.ds(C, 1), j * LANES : (j + 1) * LANES] for j in range(TILES)],
    )
    me = me_ref[0]
    window = g_ref.shape[1]
    for position, start in zip(order, starts):
        share = [rows_ref[t, pl.ds(start, window), :] for t in range(2)]
        g_ref[position ^ me] = jnp.concatenate(share, axis=1).astype(BF16)
    done_copy.wait()


def field_kernel(ranges, rows, cols, lon_pad, conv_rows, lat_halos, before, last, begun,
                 u_ref, up_ref, main_ref, west_ref, east_ref, *rest):
    rest = list(rest)
    south_ref, north_ref = (rest.pop(0), rest.pop(0)) if lat_halos else (None, None)
    before_ref = rest.pop(0) if before else None
    if begun:
        rest.pop(0)
    out_hbm = rest.pop(0) if before or last else None
    out_ref = None if last else rest.pop(0)
    x_ref, v_ref, sum_ref, before_sem, out_sem, own_ref = rest
    out_ref = own_ref if last else out_ref
    if before:
        before_copy = pltpu.make_async_copy(before_ref, out_hbm.at[pl.ds(*before)], before_sem)
        before_copy.start()
    field_points(
        ranges, conv_rows, x_ref, v_ref, main_ref, west_ref, east_ref, south_ref, north_ref, rows,
        cols,
    )

    def step(place, block):
        row = block * conv_rows

        def store(tile, lon, chunk, sums):
            lanes = pl.ds(pl.multiple_of(tile * LANES, LANES), LANES)
            for r in range(conv_rows):
                total = sums[r] + up_ref[row + r, pl.ds(lon, chunk), lanes].astype(F32)
                sum_ref[r, pl.ds(lon, chunk), lanes] = total

        depthwise_block(v_ref, u_ref, place, conv_rows, lon_pad, store, True, True)
        out_ref[pl.ds(place * conv_rows, conv_rows)] = sum_ref[:, 0:cols, 0:C].astype(BF16)
        if last:
            out_copy(place, block).start()

    def out_copy(place, block):
        return pltpu.make_async_copy(
            out_ref.at[pl.ds(place * conv_rows, conv_rows)],
            out_hbm.at[pl.ds(block * conv_rows, conv_rows)],
            out_sem.at[place],
        )

    over_blocks(ranges, step)
    if last:
        over_blocks(ranges, lambda place, block: out_copy(place, block).wait())
    if before:
        before_copy.wait()


def shape(dims, kind):
    return jax.ShapeDtypeStruct(dims, kind)


def whole(count):
    return [pl.BlockSpec(memory_space=pltpu.VMEM)] * count


def cost(micros):
    return pl.CostEstimate(flops=int(micros * 1.1e9), bytes_accessed=0, transcendentals=0)


def body(features, params, langevin_noise, upstream):
    rows, cols = features.shape[:2]
    lon_pad = up(cols, 16)
    lon_wide = up(lon_pad + KS - 1, 8)
    conv_rows = max(r for r in (1, 3, 5) if rows % r == 0)
    points = conv_rows + KS - 1
    blocks = rows // conv_rows
    block_rows = max(r for r in range(1, 16) if rows % r == 0 and r % conv_rows == 0)
    groups, bits = exchange_groups()
    count = 1 << bits
    lat_size = lax.axis_size("lat")
    length = params.shape[0]
    number = lax.axis_index("lon") * lat_size + lax.axis_index("lat")
    place = jnp.int32(0)
    for k in range(bits):
        place = place | (((number >> k) & 1) << (bits - 1 - k))
    place = place.reshape(1).astype(jnp.int32)
    offset = (number * length) % SHARE_LANES
    order = [reversed_bits(s, bits) for s in range(count)]
    starts = [s * length // SHARE_LANES for s in range(count)]
    spill = SHARE_LANES - math.gcd(SHARE_LANES, length)
    window = up(-(-(length + spill) // SHARE_LANES), 8)
    flat_rows = up(max(starts[-1] + window, 3 * (ROWS + 1)), 8)

    share = jnp.pad(params, (SHARE_LANES, window * SHARE_LANES - length))
    share = lax.dynamic_slice(share, (SHARE_LANES - offset,), (window * SHARE_LANES,)).astype(BF16)
    gathered = share.reshape(1, window, SHARE_LANES)
    compiler_params = pltpu.CompilerParams(vmem_limit_bytes=VMEM)
    smem = [pl.BlockSpec(memory_space=pltpu.SMEM)]
    margin = -(-RAD // conv_rows)
    inner = [(margin, blocks - 2 * margin)]
    outer = [(0, margin), (blocks - margin, margin)]
    edges = pl.pallas_call(
        lambda *refs: edge_kernel(cols, *refs),
        out_shape=(shape((rows, RAD, C), BF16),) * 2,
        in_specs=[pl.BlockSpec(memory_space=pltpu.HBM)],
        out_specs=tuple(whole(2)),
        scratch_shapes=[pltpu.VMEM((rows, cols, C), BF16)],
        compiler_params=compiler_params,
        cost_estimate=cost(1),
        name="edges",
    )(features)
    for k, group in enumerate(groups):
        parts = [swap(gathered, mask) for mask in group]
        if k == min(1, len(groups) - 1):
            west, east = shift_both(*edges, "lon", True)
        if k == max(0, len(groups) - 2):
            west, east, _, upstream = lax.optimization_barrier((west, east, gathered, upstream))
            wides = pl.pallas_call(
                lambda *refs: wide_kernel(rows, cols, *refs),
                out_shape=(shape((RAD, cols + 2 * RAD, C), BF16),) * 2,
                in_specs=whole(3),
                out_specs=tuple(whole(2)),
                compiler_params=compiler_params,
                cost_estimate=cost(1),
                name="wides",
            )(features, west, east)
            south, north = shift_both(*wides, "lat", False)
            inner_data, feats, ups = pl.pallas_call(
                lambda *refs: inner_kernel(inner, rows, cols, conv_rows, *refs),
                out_shape=(
                    shape((2, block_count(inner) * points, lon_wide, LANES), F32),
                    shape((rows, lon_pad, CP), BF16),
                    shape((rows, lon_pad, CP), BF16),
                ),
                in_specs=whole(4),
                out_specs=tuple(whole(3)),
                scratch_shapes=[pltpu.VMEM((2, padded_rows(inner, conv_rows), lon_wide, LANES), F32)],
                compiler_params=compiler_params,
                cost_estimate=cost(2.5),
                name="inner",
            )(features, west, east, upstream)
        gathered = jnp.concatenate([gathered, *parts], axis=0)
        if k == 0:
            edges, _ = lax.optimization_barrier((edges, gathered))
        if k == max(0, len(groups) - 2):
            gathered, inner_data = lax.optimization_barrier((gathered, inner_data))

    outer_data = pl.pallas_call(
        lambda *refs: outer_kernel(outer, rows, cols, conv_rows, *refs),
        out_shape=shape((2, block_count(outer) * points, lon_wide, LANES), F32),
        in_specs=whole(5),
        out_specs=whole(1)[0],
        scratch_shapes=[pltpu.VMEM((2, padded_rows(outer, conv_rows), lon_wide, LANES), F32)],
        compiler_params=compiler_params,
        cost_estimate=cost(1),
        name="outer",
    )(features, west, east, south, north)

    static = (order, starts, rows, lon_pad, block_rows, conv_rows, inner, outer)
    output, gconv, gin, gout, sums, flipped = pl.pallas_call(
        lambda *refs: layer_kernel(*static, *refs),
        out_shape=(
            shape((rows, cols, C), BF16),
            shape((rows, lon_pad, CP), BF16),
            shape((GIN_ROWS, H), F32),
            shape((C, H), F32),
            shape((5, 2, 8, LANES), F32),
            shape((2, points, 8, LANES), F32),
        ),
        in_specs=smem + whole(5),
        out_specs=tuple(whole(6)),
        scratch_shapes=[
            pltpu.VMEM((2, points, 8, LANES), F32),
            pltpu.VMEM((2, 64, LANES), F32),
            pltpu.VMEM((2, flat_rows, LANES), F32),
            pltpu.VMEM((CP, H), BF16),
            pltpu.VMEM((H, CP), BF16),
            pltpu.VMEM((2, H, LANES), F32),
            pltpu.VMEM((2, rows, lon_pad, LANES), F32),
            pltpu.VMEM((block_rows * lon_pad, H), BF16),
            pltpu.VMEM((block_rows * lon_pad, H), BF16),
        ],
        compiler_params=compiler_params,
        cost_estimate=cost(22),
        name="layer",
    )(place, gathered, inner_data, outer_data, feats, ups)

    values, output = pl.pallas_call(
        lambda *refs: taps_kernel(*static, *refs),
        out_shape=(
            shape((count, window, SHARE_LANES), BF16),
            shape((rows, cols, C), BF16),
        ),
        in_specs=smem + whole(7),
        out_specs=(*whole(1), pl.BlockSpec(memory_space=pl.ANY)),
        scratch_shapes=[
            pltpu.VMEM((2, flat_rows, LANES), F32),
            pltpu.VMEM((2, points, KS, 8, LANES), F32),
            pltpu.VMEM((2, H, LANES), F32),
            pltpu.VMEM((2, 64, LANES), F32),
            pltpu.SemaphoreType.DMA(()),
        ],
        compiler_params=compiler_params,
        cost_estimate=cost(11),
        name="taps",
    )(place, gconv, inner_data, outer_data, gin, gout, sums, output)

    west, east = shift_both(gconv[:, :RAD, :C], gconv[:, cols - RAD : cols, :C], "lon", True)
    field = None

    def field_piece(ranges, lat_halos, before, field, last):
        count = block_count(ranges)
        own = shape((count * conv_rows, cols, C), BF16)
        operands = [flipped, ups, gconv, west, east, *lat_halos]
        in_specs = whole(len(operands))
        span = None
        if before is not None:
            span = (before[0], before[1].shape[0])
            operands.append(before[1])
            in_specs += whole(1)
        if field is not None:
            operands.append(field)
            in_specs.append(pl.BlockSpec(memory_space=pl.ANY))
        out_shape = []
        out_specs = []
        if before is not None or last:
            out_shape.append(shape((rows, cols, C), BF16))
            out_specs.append(pl.BlockSpec(memory_space=pl.ANY))
        if not last:
            out_shape.append(own)
            out_specs += whole(1)
        results = pl.pallas_call(
            lambda *refs: field_kernel(
                ranges, rows, cols, lon_pad, conv_rows, bool(lat_halos), span, last,
                field is not None, *refs
            ),
            out_shape=tuple(out_shape),
            in_specs=in_specs,
            out_specs=tuple(out_specs),
            scratch_shapes=[
                pltpu.VMEM((2, padded_rows(ranges, conv_rows), lon_wide, LANES), F32),
                pltpu.VMEM((2, count * points, lon_wide, LANES), F32),
                pltpu.VMEM((conv_rows, lon_pad, CP), F32),
                pltpu.SemaphoreType.DMA(()),
                pltpu.SemaphoreType.DMA((count,)),
                pltpu.VMEM(own.shape if last else (8, LANES), BF16),
            ],
            input_output_aliases={} if field is None else {len(operands) - 1: 0},
            compiler_params=compiler_params,
            cost_estimate=cost(1.1 * count),
            name="field",
        )(*operands)
        return (None if last else results[-1]), (results[0] if out_shape[0] is not own else None)

    early = (inner[0][1] + 1) // 2
    for k, group in enumerate(groups[::-1]):
        if k > 2:
            values, piece = lax.optimization_barrier((values, piece))
        if k == min(1, len(groups) - 1):
            values, west, east = lax.optimization_barrier((values, west, east))
        part = values.shape[0] // (len(group) + 1)
        sent = [values[(i + 1) * part : (i + 2) * part].astype(BF16) for i in range(len(group))]
        if k == min(1, len(groups) - 1):

            def wide(at):
                return jnp.concatenate([west[at], gconv[at, :cols, :C], east[at]], axis=1)

            wides = (wide(slice(0, RAD)), wide(slice(rows - RAD, rows)))
        received = [swap(one, mask) for one, mask in zip(sent, group)]
        if k == min(1, len(groups) - 1):
            piece, _ = field_piece([(margin, early)], (), None, None, False)
        if k == min(2, len(groups) - 1):
            lat_halos = shift_both(*wides, "lat", False)
            piece, _ = lax.optimization_barrier((piece, values))
            at = margin * conv_rows
            late = [(margin + early, inner[0][1] - early)]
            piece, field = field_piece(late, (), (at, piece), None, False)
        values = values[:part].astype(F32)
        for other in received:
            values = values + other.astype(F32)
        if k == 1 and len(groups) > 2:
            values, wides = lax.optimization_barrier((values, wides))
    at = (margin + early) * conv_rows
    _, field = field_piece(outer, lat_halos, (at, piece), field, True)
    summed = lax.dynamic_slice(values.reshape(-1), (offset,), (length,))
    new_params = params - STEP_SIZE * summed + NOISE_COEF * langevin_noise
    return (output, field, new_params)


def solution(mesh):
    return jax.shard_map(
        body,
        mesh=mesh,
        in_specs=(
            P("lat", "lon", None),
            P(("lon", "lat")),
            P(("lon", "lat")),
            P("lat", "lon", None),
        ),
        out_specs=(P("lat", "lon", None), P("lat", "lon", None), P(("lon", "lat"))),
        check_vma=False,
    )
```

```python
import math

import jax
import jax.numpy as jnp
from jax import lax
from jax.experimental import pallas as pl
from jax.experimental.pallas import tpu as pltpu
from jax.sharding import PartitionSpec as P

C = 192
H = 768
KS = 7
RAD = KS // 2
LANES = 128
CP = 256
TAPS = KS * KS
EPSILON = 1e-06
STEP_SIZE = 0.003
NOISE_COEF = 0.08
GELU_A = math.sqrt(2.0 / math.pi)
GELU_B = GELU_A * 0.044715
F32 = jnp.float32
BF16 = jnp.bfloat16
ROW_OUT = C
ROW_TAPS = 2 * C
ROW_NORM = ROW_TAPS + TAPS // 4
ROW_BIAS_IN = ROW_NORM + 1
ROW_LAST = ROW_NORM + 2
ROWS = ROW_LAST + 1
TILES = H // LANES
SHARE_LANES = 256
CHUNK = 256
UNROLL = True
GIN_ROWS = C + 8
ALL = ((1,), (1,)), ((), ())
OVER = ((0,), (0,)), ((), ())
VMEM = 28 << 20


def exchange_groups():
    lon, lat = lax.axis_size("lon"), lax.axis_size("lat")
    bits = [(lon >> k, 0) for k in range(1, lon.bit_length())]
    bits += [(0, lat >> k) for k in range(1, lat.bit_length())]
    groups = []
    k = 0
    while k < len(bits):
        if k + 1 < len(bits) and bits[k][0] == 1 and bits[k + 1][0] == 0:
            (lon_bit, _), (_, lat_bit) = bits[k : k + 2]
            groups.append([(lon_bit, 0), (0, lat_bit), (lon_bit, lat_bit)])
            k += 2
        else:
            groups.append([bits[k]])
            k += 1
    return groups, len(bits)


def swap(values, mask):
    lon, lat = lax.axis_size("lon"), lax.axis_size("lat")
    pairs = [
        (i * lat + j, (i ^ mask[0]) * lat + (j ^ mask[1])) for i in range(lon) for j in range(lat)
    ]
    return lax.ppermute(values, ("lon", "lat"), pairs)


def send_edges(low_edge, high_edge, axis, periodic):
    count = lax.axis_size(axis)
    even = lax.axis_index(axis) % 2 == 0
    near = [(i, i ^ 1) for i in range(count)]
    odds = [(i, (i + 1) % count) for i in range(1, count if periodic else count - 1, 2)]
    far = odds + [(target, source) for source, target in odds]
    near = lax.ppermute(jnp.where(even, high_edge, low_edge), axis, near)
    far = lax.ppermute(jnp.where(even, low_edge, high_edge), axis, far)
    return near, far


def edges_from(near, far, axis):
    even = lax.axis_index(axis) % 2 == 0
    return jnp.where(even, far, near), jnp.where(even, near, far)


def shift_both(low_edge, high_edge, axis, periodic):
    return edges_from(*send_edges(low_edge, high_edge, axis, periodic), axis)


def reversed_bits(number, count):
    result = 0
    for k in range(count):
        result |= ((number >> k) & 1) << (count - 1 - k)
    return result


def up(value, multiple):
    return -(-value // multiple) * multiple


def split_quarter(tiles, quarter):
    lane = lax.broadcasted_iota(jnp.int32, tiles[0].shape, 1)
    low = lane < LANES // 2
    first = 3 * quarter // 2
    if quarter % 2 == 0:
        return tiles[first], jnp.where(low, tiles[first + 1], 0.0)
    left = pltpu.roll(tiles[first], LANES // 2, 1)
    right = pltpu.roll(tiles[first + 1], LANES // 2, 1)
    return jnp.where(low, left, right), jnp.where(low, right, 0.0)


def join_quarters(quarters):
    lane = lax.broadcasted_iota(jnp.int32, quarters[0][0].shape, 1)
    low = lane < LANES // 2
    tiles = []
    for even in (0, 2):
        first, second = quarters[even]
        turned = pltpu.roll(quarters[even + 1][0], LANES // 2, 1)
        last = pltpu.roll(quarters[even + 1][1], LANES // 2, 1)
        tiles += [first, jnp.where(low, second, turned), jnp.where(low, turned, last)]
    return tiles


def get_rows(flat_ref, row, count):
    return [
        flat_ref[j % 2, pl.ds(3 * row + j // 2, count, stride=3), :] for j in range(TILES)
    ]


def put_rows(flat_ref, row, tiles):
    for j in range(TILES):
        flat_ref[j % 2, pl.ds(3 * row + j // 2, tiles[j].shape[0], stride=3), :] = tiles[j]


def assemble(x_ref, base, first, count, main, west, east, south, north, rows, cols):
    for t in range(2):
        lanes = slice(t * LANES, min(C, (t + 1) * LANES))
        width = slice(0, lanes.stop - lanes.start)
        low = max(0, first - RAD)
        high = min(rows, first + count - RAD)
        at = slice(base + low + RAD - first, base + high + RAD - first)
        if main.shape[2] == CP:
            span = slice(RAD, RAD + main.shape[1])
            x_ref[t, at, span, :] = main[low:high, :, t * LANES : (t + 1) * LANES].astype(F32)
        else:
            x_ref[t, at, RAD : RAD + cols, width] = main[low:high, 0:cols, lanes].astype(F32)
        x_ref[t, at, 0:RAD, width] = west[low:high, :, lanes].astype(F32)
        x_ref[t, at, RAD + cols : 2 * RAD + cols, width] = east[low:high, :, lanes].astype(F32)
        wide = slice(0, cols + 2 * RAD)
        if first < RAD:
            at = slice(base, base + RAD - first)
            x_ref[t, at] = jnp.zeros_like(x_ref[t, at])
            x_ref[t, at, wide, width] = south[first:, :, lanes].astype(F32)
        over = first + count - rows - RAD
        if over > 0:
            at = slice(base + count - over, base + count)
            x_ref[t, at] = jnp.zeros_like(x_ref[t, at])
            x_ref[t, at, wide, width] = north[0:over, :, lanes].astype(F32)


def field_points(ranges, conv_rows, x_ref, v_ref, main, west, east, south, north, rows, cols):
    if main.shape[1:] == (x_ref.shape[2] - 8, CP):
        for t in range(2):
            for lon in (0, x_ref.shape[2] - 8):
                x_ref[t, :, lon : lon + 8, :] = jnp.zeros_like(x_ref[t, :, lon : lon + 8, :])
    else:
        x_ref[...] = jnp.zeros_like(x_ref)
    base = done = 0
    for first, count in ranges:
        span = count * conv_rows + KS - 1
        assemble(
            x_ref, base, first * conv_rows, span, main, west, east, south, north, rows, cols
        )
        write_points(x_ref, base, v_ref, done, count, conv_rows)
        base += span
        done += count


def padded_rows(ranges, conv_rows):
    return sum(count * conv_rows + KS - 1 for _, count in ranges)


def block_count(ranges):
    return sum(count for _, count in ranges)


def over_blocks(ranges, step):
    done = 0
    for first, count in ranges:

        def body(i, carry, done=done, first=first):
            step(done + i, first + i)
            return carry

        lax.fori_loop(0, count, body, 0)
        done += count


def edge_kernel(cols, field_hbm, west_ref, east_ref, field_ref):
    pltpu.sync_copy(field_hbm, field_ref)
    west_ref[...] = field_ref[:, 0:RAD, :]
    east_ref[...] = field_ref[:, cols - RAD : cols, :]


def wide_kernel(rows, cols, field_ref, west_ref, east_ref, south_ref, north_ref):
    for out_ref, first in ((south_ref, 0), (north_ref, rows - RAD)):
        at = slice(first, first + RAD)
        out_ref[:, 0:RAD, :] = west_ref[at]
        out_ref[:, RAD : RAD + cols, :] = field_ref[at, 0:cols, :]
        out_ref[:, RAD + cols : 2 * RAD + cols, :] = east_ref[at]


def inner_kernel(ranges, rows, cols, conv_rows, feat_ref, west_ref, east_ref, up_ref,
                 v_ref, feats_ref, ups_ref, x_ref):
    field_points(
        ranges, conv_rows, x_ref, v_ref, feat_ref, west_ref, east_ref, None, None, rows, cols
    )
    feats_ref[...] = jnp.zeros_like(feats_ref)
    feats_ref[:, 0:cols, 0:C] = feat_ref[...]
    ups_ref[...] = jnp.zeros_like(ups_ref)
    ups_ref[:, 0:cols, 0:C] = up_ref[...]


def outer_kernel(ranges, rows, cols, conv_rows, feat_ref, west_ref, east_ref, south_ref, north_ref,
                 v_ref, x_ref):
    field_points(
        ranges, conv_rows, x_ref, v_ref, feat_ref, west_ref, east_ref, south_ref, north_ref, rows,
        cols,
    )


def points_for(out_rows):
    pairs = [1.0, 0.5, 2.0, 1.5, 0.75][: (out_rows + KS - 2) // 2]
    points = [0.0] + [sign * p for p in pairs for sign in (1.0, -1.0)]
    filters = []
    for k, point in enumerate(points):
        scale = math.prod(point - other for i, other in enumerate(points) if i != k)
        filters.append([point**a / scale for a in range(KS)])
    return pairs, filters


def polynomial(roots):
    coefs = [1.0]
    for root in roots:
        coefs = [
            (coefs[i - 1] if i else 0.0) - (root * coefs[i] if i < len(coefs) else 0.0)
            for i in range(len(coefs) + 1)
        ]
    return coefs


def weighted(coefs, values):
    total = None
    for coef, value in zip(coefs, values):
        if coef == 0.0:
            continue
        term = value if coef == 1.0 else value * coef
        total = term if total is None else total + term
    return total


def data_points(pairs, rows):
    squares = [p * p for p in pairs]
    values = [weighted(polynomial(squares), rows[0::2])]
    for p in pairs:
        coefs = polynomial([q for q in squares if q != p * p])
        even = weighted(coefs, rows[2::2])
        odd = weighted([p * c for c in coefs], rows[1::2])
        values += [even + odd, even - odd]
    return values


def grad_points(pairs, rows):
    values = [rows[0]]
    for p in pairs:
        even = weighted([p ** (2 * i) for i in range(len(rows[0::2]))], rows[0::2])
        odd = weighted([p ** (2 * i + 1) for i in range(len(rows[1::2]))], rows[1::2])
        values += [even + odd, even - odd] if odd is not None else [even, even]
    return values


def write_points(x_ref, base, v_ref, done, blocks, out_rows):
    pairs, filters = points_for(out_rows)
    count = len(filters)
    lon_regs = x_ref.shape[2] // 8

    def body(step, carry):
        tile = step // lon_regs
        lon = pl.ds(pl.multiple_of(step % lon_regs * 8, 8), 8)

        def block(k, carry):
            rows = [x_ref[tile, base + k * out_rows + r, lon, :] for r in range(count)]
            for i, value in enumerate(data_points(pairs, rows)):
                v_ref[tile, (done + k) * count + i, lon, :] = value
            return carry

        return lax.fori_loop(0, blocks, block, carry, unroll=True)

    lax.fori_loop(0, 2 * lon_regs, body, 0)


def filter_points(taps_ref, out_rows, u_ref, flip):
    for k, coefs in enumerate(points_for(out_rows)[1]):
        coefs = coefs[::-1] if flip else coefs
        for t in range(2):
            u_ref[t, k, 0:KS, :] = weighted(
                coefs, [taps_ref[t, pl.ds(a * KS, KS), :] for a in range(KS)]
            )


def depthwise_block(v_ref, u_ref, block, out_rows, lon_pad, store, flip, unroll):
    pairs, filters = points_for(out_rows)
    count = len(filters)
    chunk = lon_pad

    def body(step, carry):
        tile = step // (lon_pad // chunk)
        lon = pl.multiple_of(step % (lon_pad // chunk) * chunk, 8)

        def product(k):
            total = None
            for b in range(KS):
                tap = KS - 1 - b if flip else b
                term = v_ref[tile, block * count + k, pl.ds(lon + b, chunk), :]
                term = term * u_ref[tile, k, pl.ds(tap, 1), :]
                total = term if total is None else total + term
            return total

        sums = [None] * out_rows
        sums[0] = product(0)
        for i, p in enumerate(pairs):
            plus, minus = product(2 * i + 1), product(2 * i + 2)
            even, odd = plus + minus, plus - minus
            for r in range(out_rows):
                term = odd if r % 2 else even
                term = term if p**r == 1.0 else term * p**r
                sums[r] = term if sums[r] is None else sums[r] + term
        store(tile, lon, chunk, sums)
        return carry

    lax.fori_loop(0, 2 * (lon_pad // chunk), body, 0, unroll=unroll)


def conv_kernel(order, starts, rows, lon_pad, block_rows, conv_rows, inner, outer,
                me_ref, gathered_ref, inner_ref, outer_ref,
                conv_ref, win_ref, wout_ref, taps_ref, flipped_ref, u_ref, w_ref, wo32_ref, sum_ref):
    me = me_ref[0]
    window = gathered_ref.shape[1]
    w_ref[:, 0:8, :] = jnp.zeros_like(w_ref[:, 0:8, :])
    w_ref[:, starts[-1] :, :] = jnp.zeros_like(w_ref[:, starts[-1] :, :])
    for position, start in zip(order, starts):
        share = gathered_ref[position ^ me].astype(F32)
        for t in range(2):
            part = share[:, t * LANES : (t + 1) * LANES]
            first = w_ref[t, pl.ds(start, 1), :] + part[0:1]
            w_ref[t, pl.ds(start, window), :] = part
            w_ref[t, pl.ds(start, 1), :] = first
    rest = lax.broadcasted_iota(jnp.int32, (CP - C, LANES), 0)
    mains = get_rows(w_ref, 0, C)
    biases = get_rows(w_ref, ROW_BIAS_IN, 1)
    for j in range(TILES):
        bias = jnp.where(rest == 0, biases[j], 0.0)
        whole = jnp.concatenate([mains[j], bias], axis=0)
        win_ref[:, j * LANES : (j + 1) * LANES] = whole.astype(BF16)
    out_rows = get_rows(w_ref, ROW_OUT, C)
    tail_rows = get_rows(w_ref, ROW_TAPS, 16)
    for quarter in range(4):
        pair = split_quarter(out_rows, quarter)
        tail = split_quarter(tail_rows, quarter)
        for t in range(2):
            wo32_ref[t, pl.ds(quarter, C, stride=4), :] = pair[t]
            taps_ref[t, pl.ds(quarter, 16, stride=4), :] = tail[t]
    for t in range(2):
        wout_ref[:, t * LANES : (t + 1) * LANES] = wo32_ref[t].astype(BF16)

    filter_points(taps_ref, conv_rows, u_ref, False)
    filter_points(taps_ref, conv_rows, flipped_ref, True)
    for v_ref, ranges in ((inner_ref, inner), (outer_ref, outer)):

        def conv_step(place, block, v_ref=v_ref):
            def store(tile, lon, chunk, sums):
                for r in range(conv_rows):
                    sum_ref[tile, r, pl.ds(lon, chunk), :] = sums[r]

            depthwise_block(v_ref, u_ref, place, conv_rows, lon_pad, store, False, UNROLL)
            conv_ref[:, pl.ds(block * conv_rows, conv_rows)] = sum_ref[...]

        over_blocks(ranges, conv_step)


def layer_kernel(rows, lon_pad, block_rows, conv_ref, win_ref, wout_ref, taps_ref, feat_ref, up_ref,
                 out_ref, gconv_ref, gin_ref, gout_ref, sums_ref, *hidden_refs):
    act_refs, gpre_refs = hidden_refs[:2], hidden_refs[2:]
    def vector(row, quarter):
        at = (row - ROW_TAPS) * 4 + quarter
        return [taps_ref[t, pl.ds(at, 1), :] for t in range(2)]

    cbias = vector(ROW_NORM, 1)
    gain = vector(ROW_NORM, 2)
    shift = vector(ROW_NORM, 3)
    bias_out = vector(ROW_LAST, 0)
    scale = vector(ROW_LAST, 1)
    lane = lax.broadcasted_iota(jnp.int32, (1, LANES), 1)
    inside = (lane < C - LANES).astype(F32)
    shift[1] = shift[1] + (lane == C - LANES).astype(F32)

    gin_ref[...] = jnp.zeros_like(gin_ref)
    gout_ref[...] = jnp.zeros_like(gout_ref)
    sums_ref[...] = jnp.zeros_like(sums_ref)
    cells = block_rows * lon_pad

    def partial(values):
        return values.reshape(cells // 8, 8, LANES).sum(axis=0)

    def normalise(block):
        row = block * block_rows
        conv = [
            conv_ref[t, pl.ds(row, block_rows)].reshape(cells, LANES) + cbias[t] for t in range(2)
        ]
        mean = jnp.sum(conv[0] + conv[1], axis=1, keepdims=True) * (1.0 / C)
        centred = [conv[0] - mean, (conv[1] - mean) * inside]
        square = centred[0] * centred[0] + centred[1] * centred[1]
        inv_std = lax.rsqrt(jnp.sum(square, axis=1, keepdims=True) * (1.0 / C) + EPSILON)
        standard = [c * inv_std for c in centred]
        normed = jnp.concatenate(
            [(standard[t] * gain[t] + shift[t]).astype(BF16) for t in range(2)], axis=1
        )
        upstream = up_ref[pl.ds(row, block_rows)].reshape(cells, CP)
        ups = [upstream[:, t * LANES : (t + 1) * LANES].astype(F32) for t in range(2)]
        grad_branch = [(scale[t] * ups[t]).astype(BF16) for t in range(2)]
        gbranch = jnp.concatenate(grad_branch, axis=1)
        return standard, inv_std, normed, ups, grad_branch, gbranch

    def hidden_units(block, state):
        normed, gbranch = state[2], state[5]
        for h in range(0, H, CHUNK):
            hidden = slice(h, h + CHUNK)
            pre = jnp.dot(normed, win_ref[:, hidden], preferred_element_type=F32)
            gact = lax.dot_general(gbranch, wout_ref[hidden, :], ALL, preferred_element_type=F32)
            square = pre * pre
            half = 0.5 + 0.5 * jnp.tanh(pre * (GELU_A + GELU_B * square))
            act = pre * half
            slope = half + act * (1.0 - half) * (2.0 * GELU_A + 6.0 * GELU_B * square)
            act_refs[block % 2][:, hidden] = act.astype(BF16)
            gpre_refs[block % 2][:, hidden] = (gact * slope).astype(BF16)

    def finish(block, state):
        row = block * block_rows
        standard, inv_std, normed, ups, grad_branch, gbranch = state
        act = act_refs[block % 2][...]
        gpre = gpre_refs[block % 2][...]
        branch = jnp.dot(act, wout_ref[...], preferred_element_type=F32)
        gnormed = lax.dot_general(gpre, win_ref[...], ALL, preferred_element_type=F32)
        gin_ref[...] += lax.dot_general(
            normed[:, :GIN_ROWS], gpre, OVER, preferred_element_type=F32
        )
        gout_ref[...] += lax.dot_general(
            gbranch[:, :C], act, OVER, preferred_element_type=F32
        )
        outs = []
        gs = []
        gn = []
        for t in range(2):
            lanes = slice(t * LANES, (t + 1) * LANES)
            branch_t = branch[:, lanes] + bias_out[t]
            feat = feat_ref[pl.ds(row, block_rows), :, lanes].reshape(cells, LANES).astype(F32)
            outs.append((feat + scale[t] * branch_t).astype(BF16))
            gn.append(gnormed[:, lanes])
            sums_ref[4, t] += partial(branch_t * ups[t])
            sums_ref[3, t] += partial(grad_branch[t].astype(F32))
            sums_ref[1, t] += partial(gn[t] * standard[t])
            sums_ref[2, t] += partial(gn[t])
            gs.append(gn[t] * gain[t])
        mean_g = jnp.sum(gs[0] + gs[1], axis=1, keepdims=True) * (1.0 / C)
        both = gs[0] * standard[0] + gs[1] * standard[1]
        mean_gs = jnp.sum(both, axis=1, keepdims=True) * (1.0 / C)
        gconv = []
        for t in range(2):
            grad = ((gs[t] - mean_g - standard[t] * mean_gs) * inv_std).astype(BF16)
            sums_ref[0, t] += partial(grad.astype(F32))
            gconv.append(grad)
        gconv_ref[pl.ds(row, block_rows)] = jnp.concatenate(gconv, axis=1).reshape(
            block_rows, lon_pad, CP
        )
        out = jnp.concatenate(outs, axis=1).reshape(block_rows, lon_pad, CP)
        out_ref[pl.ds(row, block_rows)] = out[:, : out_ref.shape[1], :C]

    states = [normalise(0)]
    hidden_units(0, states[0])
    for block in range(rows // block_rows):
        if block + 1 < rows // block_rows:
            states.append(normalise(block + 1))
            hidden_units(block + 1, states[block + 1])
        finish(block, states[block])


def taps_kernel(order, starts, rows, lon_pad, block_rows, conv_rows, inner, outer,
                me_ref, gconv_ref, inner_ref, outer_ref, gin_ref, gout_ref, sums_ref, done_ref,
                g_ref, done_hbm, rows_ref, acc_ref, wo32_ref, small_ref, done_sem):
    done_copy = pltpu.make_async_copy(done_ref, done_hbm, done_sem)
    done_copy.start()
    acc_ref[...] = jnp.zeros_like(acc_ref)
    pairs, filters = points_for(conv_rows)
    count = len(filters)

    for v_ref, ranges in ((inner_ref, inner), (outer_ref, outer)):

        def step(place, block, v_ref=v_ref):
            def side(tile, carry):
                lanes = pl.ds(pl.multiple_of(tile * LANES, LANES), LANES)
                grads = grad_points(
                    pairs,
                    [
                        gconv_ref[block * conv_rows + r, :, lanes].astype(F32)
                        for r in range(conv_rows)
                    ],
                )
                for k in range(count):
                    for b in range(KS):
                        term = grads[k] * v_ref[tile, place * count + k, pl.ds(b, lon_pad), :]
                        acc_ref[tile, k, b] += term.reshape(lon_pad // 8, 8, LANES).sum(axis=0)
                return carry

            lax.fori_loop(0, 2, side, 0, unroll=True)

        over_blocks(ranges, step)

    rows_ref[...] = jnp.zeros_like(rows_ref)
    small_ref[...] = jnp.zeros_like(small_ref)
    for t in range(2):
        totals = [jnp.sum(acc_ref[t, k], axis=1) for k in range(count)]
        for a in range(KS):
            small_ref[t, pl.ds(a * KS, KS), :] = weighted([f[a] for f in filters], totals)
        for at, k in ((TAPS, 0), (TAPS + 1, 1), (TAPS + 2, 2), (TAPS + 7, 3), (TAPS + 8, 4)):
            small_ref[t, pl.ds(at, 1), :] = jnp.sum(sums_ref[k, t], axis=0, keepdims=True)
        width = min(C, (t + 1) * LANES) - t * LANES
        wo32_ref[t, :, 0:width] = gout_ref[pl.ds(t * LANES, width), :].T
    outs = join_quarters(
        [[wo32_ref[t, pl.ds(q, C, stride=4), :] for t in range(2)] for q in range(4)]
    )
    tails = join_quarters(
        [[small_ref[t, pl.ds(q, 16, stride=4), :] for t in range(2)] for q in range(4)]
    )
    put_rows(rows_ref, 0, [gin_ref[pl.ds(0, C), j * LANES : (j + 1) * LANES] for j in range(TILES)])
    put_rows(rows_ref, ROW_OUT, outs)
    put_rows(rows_ref, ROW_TAPS, tails)
    put_rows(
        rows_ref,
        ROW_BIAS_IN,
        [gin_ref[pl.ds(C, 1), j * LANES : (j + 1) * LANES] for j in range(TILES)],
    )
    me = me_ref[0]
    window = g_ref.shape[1]
    for position, start in zip(order, starts):
        share = [rows_ref[t, pl.ds(start, window), :] for t in range(2)]
        g_ref[position ^ me] = jnp.concatenate(share, axis=1).astype(BF16)
    done_copy.wait()


def field_kernel(ranges, rows, cols, lon_pad, conv_rows, lat_halos, before, last, begun,
                 u_ref, up_ref, main_ref, west_ref, east_ref, *rest):
    rest = list(rest)
    south_ref, north_ref = (rest.pop(0), rest.pop(0)) if lat_halos else (None, None)
    before_ref = rest.pop(0) if before else None
    if begun:
        rest.pop(0)
    out_hbm = rest.pop(0) if before or last else None
    out_ref = None if last else rest.pop(0)
    x_ref, v_ref, sum_ref, before_sem, out_sem, own_ref = rest
    out_ref = own_ref if last else out_ref
    if before:
        before_copy = pltpu.make_async_copy(before_ref, out_hbm.at[pl.ds(*before)], before_sem)
        before_copy.start()
    field_points(
        ranges, conv_rows, x_ref, v_ref, main_ref, west_ref, east_ref, south_ref, north_ref, rows,
        cols,
    )

    def step(place, block):
        row = block * conv_rows

        def store(tile, lon, chunk, sums):
            lanes = pl.ds(pl.multiple_of(tile * LANES, LANES), LANES)
            for r in range(conv_rows):
                total = sums[r] + up_ref[row + r, pl.ds(lon, chunk), lanes].astype(F32)
                sum_ref[r, pl.ds(lon, chunk), lanes] = total

        depthwise_block(v_ref, u_ref, place, conv_rows, lon_pad, store, True, True)
        out_ref[pl.ds(place * conv_rows, conv_rows)] = sum_ref[:, 0:cols, 0:C].astype(BF16)
        if last:
            out_copy(place, block).start()

    def out_copy(place, block):
        return pltpu.make_async_copy(
            out_ref.at[pl.ds(place * conv_rows, conv_rows)],
            out_hbm.at[pl.ds(block * conv_rows, conv_rows)],
            out_sem.at[place],
        )

    over_blocks(ranges, step)
    if last:
        over_blocks(ranges, lambda place, block: out_copy(place, block).wait())
    if before:
        before_copy.wait()


def shape(dims, kind):
    return jax.ShapeDtypeStruct(dims, kind)


def whole(count):
    return [pl.BlockSpec(memory_space=pltpu.VMEM)] * count


def cost(micros):
    return pl.CostEstimate(flops=int(micros * 1.1e9), bytes_accessed=0, transcendentals=0)


def body(features, params, langevin_noise, upstream):
    rows, cols = features.shape[:2]
    lon_pad = up(cols, 16)
    lon_wide = up(lon_pad + KS - 1, 8)
    conv_rows = max(r for r in (1, 3, 5) if rows % r == 0)
    points = conv_rows + KS - 1
    blocks = rows // conv_rows
    block_rows = max(r for r in range(1, 16) if rows % r == 0 and r % conv_rows == 0)
    groups, bits = exchange_groups()
    count = 1 << bits
    lat_size = lax.axis_size("lat")
    length = params.shape[0]
    number = lax.axis_index("lon") * lat_size + lax.axis_index("lat")
    place = jnp.int32(0)
    for k in range(bits):
        place = place | (((number >> k) & 1) << (bits - 1 - k))
    place = place.reshape(1).astype(jnp.int32)
    offset = (number * length) % SHARE_LANES
    order = [reversed_bits(s, bits) for s in range(count)]
    starts = [s * length // SHARE_LANES for s in range(count)]
    spill = SHARE_LANES - math.gcd(SHARE_LANES, length)
    window = up(-(-(length + spill) // SHARE_LANES), 8)
    flat_rows = up(max(starts[-1] + window, 3 * (ROWS + 1)), 8)

    share = jnp.pad(params, (SHARE_LANES, window * SHARE_LANES - length))
    share = lax.dynamic_slice(share, (SHARE_LANES - offset,), (window * SHARE_LANES,)).astype(BF16)
    gathered = share.reshape(1, window, SHARE_LANES)
    compiler_params = pltpu.CompilerParams(vmem_limit_bytes=VMEM)
    smem = [pl.BlockSpec(memory_space=pltpu.SMEM)]
    margin = -(-RAD // conv_rows)
    inner = [(margin, blocks - 2 * margin)]
    outer = [(0, margin), (blocks - margin, margin)]
    edges = pl.pallas_call(
        lambda *refs: edge_kernel(cols, *refs),
        out_shape=(shape((rows, RAD, C), BF16),) * 2,
        in_specs=[pl.BlockSpec(memory_space=pltpu.HBM)],
        out_specs=tuple(whole(2)),
        scratch_shapes=[pltpu.VMEM((rows, cols, C), BF16)],
        compiler_params=compiler_params,
        cost_estimate=cost(1),
        name="edges",
    )(features)
    for k, group in enumerate(groups):
        parts = [swap(gathered, mask) for mask in group]
        if k == min(1, len(groups) - 1):
            west, east = shift_both(*edges, "lon", True)
        if k == max(0, len(groups) - 2):
            west, east, _, upstream = lax.optimization_barrier((west, east, gathered, upstream))
            wides = pl.pallas_call(
                lambda *refs: wide_kernel(rows, cols, *refs),
                out_shape=(shape((RAD, cols + 2 * RAD, C), BF16),) * 2,
                in_specs=whole(3),
                out_specs=tuple(whole(2)),
                compiler_params=compiler_params,
                cost_estimate=cost(1),
                name="wides",
            )(features, west, east)
            south, north = shift_both(*wides, "lat", False)
            inner_data, feats, ups = pl.pallas_call(
                lambda *refs: inner_kernel(inner, rows, cols, conv_rows, *refs),
                out_shape=(
                    shape((2, block_count(inner) * points, lon_wide, LANES), F32),
                    shape((rows, lon_pad, CP), BF16),
                    shape((rows, lon_pad, CP), BF16),
                ),
                in_specs=whole(4),
                out_specs=tuple(whole(3)),
                scratch_shapes=[pltpu.VMEM((2, padded_rows(inner, conv_rows), lon_wide, LANES), F32)],
                compiler_params=compiler_params,
                cost_estimate=cost(2.5),
                name="inner",
            )(features, west, east, upstream)
        gathered = jnp.concatenate([gathered, *parts], axis=0)
        if k == 0:
            edges, _ = lax.optimization_barrier((edges, gathered))
        if k == max(0, len(groups) - 2):
            gathered, inner_data = lax.optimization_barrier((gathered, inner_data))

    outer_data = pl.pallas_call(
        lambda *refs: outer_kernel(outer, rows, cols, conv_rows, *refs),
        out_shape=shape((2, block_count(outer) * points, lon_wide, LANES), F32),
        in_specs=whole(5),
        out_specs=whole(1)[0],
        scratch_shapes=[pltpu.VMEM((2, padded_rows(outer, conv_rows), lon_wide, LANES), F32)],
        compiler_params=compiler_params,
        cost_estimate=cost(1),
        name="outer",
    )(features, west, east, south, north)

    static = (order, starts, rows, lon_pad, block_rows, conv_rows, inner, outer)
    *weights, flipped = pl.pallas_call(
        lambda *refs: conv_kernel(*static, *refs),
        out_shape=(
            shape((2, rows, lon_pad, LANES), F32),
            shape((CP, H), BF16),
            shape((H, CP), BF16),
            shape((2, 64, LANES), F32),
            shape((2, points, 8, LANES), F32),
        ),
        in_specs=smem + whole(3),
        out_specs=tuple(whole(5)),
        scratch_shapes=[
            pltpu.VMEM((2, points, 8, LANES), F32),
            pltpu.VMEM((2, flat_rows, LANES), F32),
            pltpu.VMEM((2, H, LANES), F32),
            pltpu.VMEM((2, conv_rows, lon_pad, LANES), F32),
        ],
        compiler_params=compiler_params,
        cost_estimate=cost(6),
        name="conv",
    )(place, gathered, inner_data, outer_data)
    output, gconv, gin, gout, sums = pl.pallas_call(
        lambda *refs: layer_kernel(rows, lon_pad, block_rows, *refs),
        out_shape=(
            shape((rows, cols, C), BF16),
            shape((rows, lon_pad, CP), BF16),
            shape((GIN_ROWS, H), F32),
            shape((C, H), F32),
            shape((5, 2, 8, LANES), F32),
        ),
        in_specs=whole(6),
        out_specs=tuple(whole(5)),
        scratch_shapes=[pltpu.VMEM((block_rows * lon_pad, H), BF16)] * 4,
        compiler_params=compiler_params,
        cost_estimate=cost(16),
        name="layer",
    )(*weights, feats, ups)

    values, output = pl.pallas_call(
        lambda *refs: taps_kernel(*static, *refs),
        out_shape=(
            shape((count, window, SHARE_LANES), BF16),
            shape((rows, cols, C), BF16),
        ),
        in_specs=smem + whole(7),
        out_specs=(*whole(1), pl.BlockSpec(memory_space=pl.ANY)),
        scratch_shapes=[
            pltpu.VMEM((2, flat_rows, LANES), F32),
            pltpu.VMEM((2, points, KS, 8, LANES), F32),
            pltpu.VMEM((2, H, LANES), F32),
            pltpu.VMEM((2, 64, LANES), F32),
            pltpu.SemaphoreType.DMA(()),
        ],
        compiler_params=compiler_params,
        cost_estimate=cost(11),
        name="taps",
    )(place, gconv, inner_data, outer_data, gin, gout, sums, output)

    west, east = shift_both(gconv[:, :RAD, :C], gconv[:, cols - RAD : cols, :C], "lon", True)
    field = None

    def field_piece(ranges, lat_halos, before, field, last):
        count = block_count(ranges)
        own = shape((count * conv_rows, cols, C), BF16)
        operands = [flipped, ups, gconv, west, east, *lat_halos]
        in_specs = whole(len(operands))
        span = None
        if before is not None:
            span = (before[0], before[1].shape[0])
            operands.append(before[1])
            in_specs += whole(1)
        if field is not None:
            operands.append(field)
            in_specs.append(pl.BlockSpec(memory_space=pl.ANY))
        out_shape = []
        out_specs = []
        if before is not None or last:
            out_shape.append(shape((rows, cols, C), BF16))
            out_specs.append(pl.BlockSpec(memory_space=pl.ANY))
        if not last:
            out_shape.append(own)
            out_specs += whole(1)
        results = pl.pallas_call(
            lambda *refs: field_kernel(
                ranges, rows, cols, lon_pad, conv_rows, bool(lat_halos), span, last,
                field is not None, *refs
            ),
            out_shape=tuple(out_shape),
            in_specs=in_specs,
            out_specs=tuple(out_specs),
            scratch_shapes=[
                pltpu.VMEM((2, padded_rows(ranges, conv_rows), lon_wide, LANES), F32),
                pltpu.VMEM((2, count * points, lon_wide, LANES), F32),
                pltpu.VMEM((conv_rows, lon_pad, CP), F32),
                pltpu.SemaphoreType.DMA(()),
                pltpu.SemaphoreType.DMA((count,)),
                pltpu.VMEM(own.shape if last else (8, LANES), BF16),
            ],
            input_output_aliases={} if field is None else {len(operands) - 1: 0},
            compiler_params=compiler_params,
            cost_estimate=cost(1.1 * count),
            name="field",
        )(*operands)
        return (None if last else results[-1]), (results[0] if out_shape[0] is not own else None)

    early = (inner[0][1] + 1) // 2
    for k, group in enumerate(groups[::-1]):
        if k > 2:
            values, piece = lax.optimization_barrier((values, piece))
        if k == min(1, len(groups) - 1):
            values, west, east = lax.optimization_barrier((values, west, east))
        part = values.shape[0] // (len(group) + 1)
        sent = [values[(i + 1) * part : (i + 2) * part].astype(BF16) for i in range(len(group))]
        if k == min(1, len(groups) - 1):

            def wide(at):
                return jnp.concatenate([west[at], gconv[at, :cols, :C], east[at]], axis=1)

            wides = (wide(slice(0, RAD)), wide(slice(rows - RAD, rows)))
        received = [swap(one, mask) for one, mask in zip(sent, group)]
        if k == min(1, len(groups) - 1):
            piece, _ = field_piece([(margin, early)], (), None, None, False)
        if k == min(2, len(groups) - 1):
            lat_halos = shift_both(*wides, "lat", False)
            piece, _ = lax.optimization_barrier((piece, values))
            at = margin * conv_rows
            late = [(margin + early, inner[0][1] - early)]
            piece, field = field_piece(late, (), (at, piece), None, False)
        values = values[:part].astype(F32)
        for other in received:
            values = values + other.astype(F32)
        if k == 1 and len(groups) > 2:
            values, wides = lax.optimization_barrier((values, wides))
    at = (margin + early) * conv_rows
    _, field = field_piece(outer, lat_halos, (at, piece), field, True)
    summed = lax.dynamic_slice(values.reshape(-1), (offset,), (length,))
    new_params = params - STEP_SIZE * summed + NOISE_COEF * langevin_noise
    return (output, field, new_params)


def solution(mesh):
    return jax.shard_map(
        body,
        mesh=mesh,
        in_specs=(
            P("lat", "lon", None),
            P(("lon", "lat")),
            P(("lon", "lat")),
            P("lat", "lon", None),
        ),
        out_specs=(P("lat", "lon", None), P("lat", "lon", None), P(("lon", "lat"))),
        check_vma=False,
    )
```

```python
import math

import jax
import jax.numpy as jnp
from jax import lax
from jax.experimental import pallas as pl
from jax.experimental.pallas import tpu as pltpu
from jax.sharding import PartitionSpec as P

C = 192
H = 768
KS = 7
RAD = KS // 2
LANES = 128
CP = 256
TAPS = KS * KS
EPSILON = 1e-06
STEP_SIZE = 0.003
NOISE_COEF = 0.08
GELU_A = math.sqrt(2.0 / math.pi)
GELU_B = GELU_A * 0.044715
F32 = jnp.float32
BF16 = jnp.bfloat16
ROW_OUT = C
ROW_TAPS = 2 * C
ROW_NORM = ROW_TAPS + TAPS // 4
ROW_BIAS_IN = ROW_NORM + 1
ROW_LAST = ROW_NORM + 2
ROWS = ROW_LAST + 1
TILES = H // LANES
SHARE_LANES = 256
CHUNK = 256
UNROLL = True
GIN_ROWS = C + 8
ALL = ((1,), (1,)), ((), ())
OVER = ((0,), (0,)), ((), ())
VMEM = 28 << 20


def exchange_groups():
    lon, lat = lax.axis_size("lon"), lax.axis_size("lat")
    bits = [(lon >> k, 0) for k in range(1, lon.bit_length())]
    bits += [(0, lat >> k) for k in range(1, lat.bit_length())]
    groups = []
    k = 0
    while k < len(bits):
        if k + 1 < len(bits) and bits[k][0] == 1 and bits[k + 1][0] == 0:
            (lon_bit, _), (_, lat_bit) = bits[k : k + 2]
            groups.append([(lon_bit, 0), (0, lat_bit), (lon_bit, lat_bit)])
            k += 2
        else:
            groups.append([bits[k]])
            k += 1
    return groups, len(bits)


def swap(values, mask):
    lon, lat = lax.axis_size("lon"), lax.axis_size("lat")
    pairs = [
        (i * lat + j, (i ^ mask[0]) * lat + (j ^ mask[1])) for i in range(lon) for j in range(lat)
    ]
    return lax.ppermute(values, ("lon", "lat"), pairs)


def send_edges(low_edge, high_edge, axis, periodic):
    count = lax.axis_size(axis)
    even = lax.axis_index(axis) % 2 == 0
    near = [(i, i ^ 1) for i in range(count)]
    odds = [(i, (i + 1) % count) for i in range(1, count if periodic else count - 1, 2)]
    far = odds + [(target, source) for source, target in odds]
    near = lax.ppermute(jnp.where(even, high_edge, low_edge), axis, near)
    far = lax.ppermute(jnp.where(even, low_edge, high_edge), axis, far)
    return near, far


def edges_from(near, far, axis):
    even = lax.axis_index(axis) % 2 == 0
    return jnp.where(even, far, near), jnp.where(even, near, far)


def shift_both(low_edge, high_edge, axis, periodic):
    return edges_from(*send_edges(low_edge, high_edge, axis, periodic), axis)


def reversed_bits(number, count):
    result = 0
    for k in range(count):
        result |= ((number >> k) & 1) << (count - 1 - k)
    return result


def up(value, multiple):
    return -(-value // multiple) * multiple


def split_quarter(tiles, quarter):
    lane = lax.broadcasted_iota(jnp.int32, tiles[0].shape, 1)
    low = lane < LANES // 2
    first = 3 * quarter // 2
    if quarter % 2 == 0:
        return tiles[first], jnp.where(low, tiles[first + 1], 0.0)
    left = pltpu.roll(tiles[first], LANES // 2, 1)
    right = pltpu.roll(tiles[first + 1], LANES // 2, 1)
    return jnp.where(low, left, right), jnp.where(low, right, 0.0)


def join_quarters(quarters):
    lane = lax.broadcasted_iota(jnp.int32, quarters[0][0].shape, 1)
    low = lane < LANES // 2
    tiles = []
    for even in (0, 2):
        first, second = quarters[even]
        turned = pltpu.roll(quarters[even + 1][0], LANES // 2, 1)
        last = pltpu.roll(quarters[even + 1][1], LANES // 2, 1)
        tiles += [first, jnp.where(low, second, turned), jnp.where(low, turned, last)]
    return tiles


def get_rows(flat_ref, row, count):
    return [
        flat_ref[j % 2, pl.ds(3 * row + j // 2, count, stride=3), :] for j in range(TILES)
    ]


def put_rows(flat_ref, row, tiles):
    for j in range(TILES):
        flat_ref[j % 2, pl.ds(3 * row + j // 2, tiles[j].shape[0], stride=3), :] = tiles[j]


def assemble(x_ref, base, first, count, main, west, east, south, north, rows, cols):
    for t in range(2):
        lanes = slice(t * LANES, min(C, (t + 1) * LANES))
        width = slice(0, lanes.stop - lanes.start)
        low = max(0, first - RAD)
        high = min(rows, first + count - RAD)
        at = slice(base + low + RAD - first, base + high + RAD - first)
        if main.shape[2] == CP:
            span = slice(RAD, RAD + main.shape[1])
            x_ref[t, at, span, :] = main[low:high, :, t * LANES : (t + 1) * LANES].astype(F32)
        else:
            x_ref[t, at, RAD : RAD + cols, width] = main[low:high, 0:cols, lanes].astype(F32)
        x_ref[t, at, 0:RAD, width] = west[low:high, :, lanes].astype(F32)
        x_ref[t, at, RAD + cols : 2 * RAD + cols, width] = east[low:high, :, lanes].astype(F32)
        wide = slice(0, cols + 2 * RAD)
        if first < RAD:
            at = slice(base, base + RAD - first)
            x_ref[t, at] = jnp.zeros_like(x_ref[t, at])
            x_ref[t, at, wide, width] = south[first:, :, lanes].astype(F32)
        over = first + count - rows - RAD
        if over > 0:
            at = slice(base + count - over, base + count)
            x_ref[t, at] = jnp.zeros_like(x_ref[t, at])
            x_ref[t, at, wide, width] = north[0:over, :, lanes].astype(F32)


def field_points(ranges, conv_rows, x_ref, v_ref, main, west, east, south, north, rows, cols):
    if main.shape[1:] == (x_ref.shape[2] - 8, CP):
        for t in range(2):
            for lon in (0, x_ref.shape[2] - 8):
                x_ref[t, :, lon : lon + 8, :] = jnp.zeros_like(x_ref[t, :, lon : lon + 8, :])
    else:
        x_ref[...] = jnp.zeros_like(x_ref)
    base = done = 0
    for first, count in ranges:
        span = count * conv_rows + KS - 1
        assemble(
            x_ref, base, first * conv_rows, span, main, west, east, south, north, rows, cols
        )
        write_points(x_ref, base, v_ref, done, count, conv_rows)
        base += span
        done += count


def padded_rows(ranges, conv_rows):
    return sum(count * conv_rows + KS - 1 for _, count in ranges)


def block_count(ranges):
    return sum(count for _, count in ranges)


def over_blocks(ranges, step):
    done = 0
    for first, count in ranges:

        def body(i, carry, done=done, first=first):
            step(done + i, first + i)
            return carry

        lax.fori_loop(0, count, body, 0)
        done += count


def edge_kernel(cols, field_hbm, west_ref, east_ref, field_ref):
    pltpu.sync_copy(field_hbm, field_ref)
    west_ref[...] = field_ref[:, 0:RAD, :]
    east_ref[...] = field_ref[:, cols - RAD : cols, :]


def wide_kernel(rows, cols, field_ref, west_ref, east_ref, south_ref, north_ref):
    for out_ref, first in ((south_ref, 0), (north_ref, rows - RAD)):
        at = slice(first, first + RAD)
        out_ref[:, 0:RAD, :] = west_ref[at]
        out_ref[:, RAD : RAD + cols, :] = field_ref[at, 0:cols, :]
        out_ref[:, RAD + cols : 2 * RAD + cols, :] = east_ref[at]


def inner_kernel(ranges, rows, cols, conv_rows, feat_ref, west_ref, east_ref, up_ref,
                 v_ref, feats_ref, ups_ref, x_ref):
    field_points(
        ranges, conv_rows, x_ref, v_ref, feat_ref, west_ref, east_ref, None, None, rows, cols
    )
    feats_ref[...] = jnp.zeros_like(feats_ref)
    feats_ref[:, 0:cols, 0:C] = feat_ref[...]
    ups_ref[...] = jnp.zeros_like(ups_ref)
    ups_ref[:, 0:cols, 0:C] = up_ref[...]


def outer_kernel(ranges, rows, cols, conv_rows, feat_ref, west_ref, east_ref, south_ref, north_ref,
                 v_ref, x_ref):
    field_points(
        ranges, conv_rows, x_ref, v_ref, feat_ref, west_ref, east_ref, south_ref, north_ref, rows,
        cols,
    )


def points_for(out_rows):
    pairs = [1.0, 0.5, 2.0, 1.5, 0.75][: (out_rows + KS - 2) // 2]
    points = [0.0] + [sign * p for p in pairs for sign in (1.0, -1.0)]
    filters = []
    for k, point in enumerate(points):
        scale = math.prod(point - other for i, other in enumerate(points) if i != k)
        filters.append([point**a / scale for a in range(KS)])
    return pairs, filters


def polynomial(roots):
    coefs = [1.0]
    for root in roots:
        coefs = [
            (coefs[i - 1] if i else 0.0) - (root * coefs[i] if i < len(coefs) else 0.0)
            for i in range(len(coefs) + 1)
        ]
    return coefs


def weighted(coefs, values):
    total = None
    for coef, value in zip(coefs, values):
        if coef == 0.0:
            continue
        term = value if coef == 1.0 else value * coef
        total = term if total is None else total + term
    return total


def data_points(pairs, rows):
    squares = [p * p for p in pairs]
    values = [weighted(polynomial(squares), rows[0::2])]
    for p in pairs:
        coefs = polynomial([q for q in squares if q != p * p])
        even = weighted(coefs, rows[2::2])
        odd = weighted([p * c for c in coefs], rows[1::2])
        values += [even + odd, even - odd]
    return values


def grad_points(pairs, rows):
    values = [rows[0]]
    for p in pairs:
        even = weighted([p ** (2 * i) for i in range(len(rows[0::2]))], rows[0::2])
        odd = weighted([p ** (2 * i + 1) for i in range(len(rows[1::2]))], rows[1::2])
        values += [even + odd, even - odd] if odd is not None else [even, even]
    return values


def write_points(x_ref, base, v_ref, done, blocks, out_rows):
    pairs, filters = points_for(out_rows)
    count = len(filters)
    lon_regs = x_ref.shape[2] // 8

    for step in range(2 * lon_regs):
        tile = step // lon_regs
        lon = pl.ds(step % lon_regs * 8, 8)
        for k in range(blocks):
            rows = [x_ref[tile, base + k * out_rows + r, lon, :] for r in range(count)]
            for i, value in enumerate(data_points(pairs, rows)):
                v_ref[tile, (done + k) * count + i, lon, :] = value


def filter_points(taps_ref, out_rows, u_ref, flip):
    for k, coefs in enumerate(points_for(out_rows)[1]):
        coefs = coefs[::-1] if flip else coefs
        for t in range(2):
            u_ref[t, k, 0:KS, :] = weighted(
                coefs, [taps_ref[t, pl.ds(a * KS, KS), :] for a in range(KS)]
            )


def depthwise_block(v_ref, u_ref, block, out_rows, lon_pad, store, flip, unroll):
    pairs, filters = points_for(out_rows)
    count = len(filters)
    chunk = lon_pad

    def body(step, carry):
        tile = step // (lon_pad // chunk)
        lon = pl.multiple_of(step % (lon_pad // chunk) * chunk, 8)

        def product(k):
            total = None
            for b in range(KS):
                tap = KS - 1 - b if flip else b
                term = v_ref[tile, block * count + k, pl.ds(lon + b, chunk), :]
                term = term * u_ref[tile, k, pl.ds(tap, 1), :]
                total = term if total is None else total + term
            return total

        sums = [None] * out_rows
        sums[0] = product(0)
        for i, p in enumerate(pairs):
            plus, minus = product(2 * i + 1), product(2 * i + 2)
            even, odd = plus + minus, plus - minus
            for r in range(out_rows):
                term = odd if r % 2 else even
                term = term if p**r == 1.0 else term * p**r
                sums[r] = term if sums[r] is None else sums[r] + term
        store(tile, lon, chunk, sums)
        return carry

    lax.fori_loop(0, 2 * (lon_pad // chunk), body, 0, unroll=unroll)


def conv_kernel(order, starts, rows, lon_pad, block_rows, conv_rows, inner, outer,
                me_ref, gathered_ref, inner_ref, outer_ref,
                conv_ref, win_ref, wout_ref, taps_ref, flipped_ref, u_ref, w_ref, wo32_ref, sum_ref):
    me = me_ref[0]
    window = gathered_ref.shape[1]
    w_ref[:, 0:8, :] = jnp.zeros_like(w_ref[:, 0:8, :])
    w_ref[:, starts[-1] :, :] = jnp.zeros_like(w_ref[:, starts[-1] :, :])
    for position, start in zip(order, starts):
        share = gathered_ref[position ^ me].astype(F32)
        for t in range(2):
            part = share[:, t * LANES : (t + 1) * LANES]
            first = w_ref[t, pl.ds(start, 1), :] + part[0:1]
            w_ref[t, pl.ds(start, window), :] = part
            w_ref[t, pl.ds(start, 1), :] = first
    rest = lax.broadcasted_iota(jnp.int32, (CP - C, LANES), 0)
    mains = get_rows(w_ref, 0, C)
    biases = get_rows(w_ref, ROW_BIAS_IN, 1)
    for j in range(TILES):
        bias = jnp.where(rest == 0, biases[j], 0.0)
        whole = jnp.concatenate([mains[j], bias], axis=0)
        win_ref[:, j * LANES : (j + 1) * LANES] = whole.astype(BF16)
    out_rows = get_rows(w_ref, ROW_OUT, C)
    tail_rows = get_rows(w_ref, ROW_TAPS, 16)
    for quarter in range(4):
        pair = split_quarter(out_rows, quarter)
        tail = split_quarter(tail_rows, quarter)
        for t in range(2):
            wo32_ref[t, pl.ds(quarter, C, stride=4), :] = pair[t]
            taps_ref[t, pl.ds(quarter, 16, stride=4), :] = tail[t]
    for t in range(2):
        wout_ref[:, t * LANES : (t + 1) * LANES] = wo32_ref[t].astype(BF16)

    filter_points(taps_ref, conv_rows, u_ref, False)
    filter_points(taps_ref, conv_rows, flipped_ref, True)
    for v_ref, ranges in ((inner_ref, inner), (outer_ref, outer)):

        def conv_step(place, block, v_ref=v_ref):
            def store(tile, lon, chunk, sums):
                for r in range(conv_rows):
                    sum_ref[tile, r, pl.ds(lon, chunk), :] = sums[r]

            depthwise_block(v_ref, u_ref, place, conv_rows, lon_pad, store, False, UNROLL)
            conv_ref[:, pl.ds(block * conv_rows, conv_rows)] = sum_ref[...]

        over_blocks(ranges, conv_step)


def layer_kernel(rows, lon_pad, block_rows, conv_ref, win_ref, wout_ref, taps_ref, feat_ref, up_ref,
                 out_ref, gconv_ref, gin_ref, gout_ref, sums_ref, *hidden_refs):
    act_refs, gpre_refs = hidden_refs[:2], hidden_refs[2:]
    def vector(row, quarter):
        at = (row - ROW_TAPS) * 4 + quarter
        return [taps_ref[t, pl.ds(at, 1), :] for t in range(2)]

    cbias = vector(ROW_NORM, 1)
    gain = vector(ROW_NORM, 2)
    shift = vector(ROW_NORM, 3)
    bias_out = vector(ROW_LAST, 0)
    scale = vector(ROW_LAST, 1)
    lane = lax.broadcasted_iota(jnp.int32, (1, LANES), 1)
    inside = (lane < C - LANES).astype(F32)
    shift[1] = shift[1] + (lane == C - LANES).astype(F32)

    gin_ref[...] = jnp.zeros_like(gin_ref)
    gout_ref[...] = jnp.zeros_like(gout_ref)
    sums_ref[...] = jnp.zeros_like(sums_ref)
    cells = block_rows * lon_pad

    def partial(values):
        return values.reshape(cells // 8, 8, LANES).sum(axis=0)

    def normalise(block):
        row = block * block_rows
        conv = [
            conv_ref[t, pl.ds(row, block_rows)].reshape(cells, LANES) + cbias[t] for t in range(2)
        ]
        mean = jnp.sum(conv[0] + conv[1], axis=1, keepdims=True) * (1.0 / C)
        centred = [conv[0] - mean, (conv[1] - mean) * inside]
        square = centred[0] * centred[0] + centred[1] * centred[1]
        inv_std = lax.rsqrt(jnp.sum(square, axis=1, keepdims=True) * (1.0 / C) + EPSILON)
        standard = [c * inv_std for c in centred]
        normed = jnp.concatenate(
            [(standard[t] * gain[t] + shift[t]).astype(BF16) for t in range(2)], axis=1
        )
        upstream = up_ref[pl.ds(row, block_rows)].reshape(cells, CP)
        ups = [upstream[:, t * LANES : (t + 1) * LANES].astype(F32) for t in range(2)]
        grad_branch = [(scale[t] * ups[t]).astype(BF16) for t in range(2)]
        gbranch = jnp.concatenate(grad_branch, axis=1)
        return standard, inv_std, normed, ups, grad_branch, gbranch

    def hidden_units(block, state):
        normed, gbranch = state[2], state[5]
        for h in range(0, H, CHUNK):
            hidden = slice(h, h + CHUNK)
            pre = jnp.dot(normed, win_ref[:, hidden], preferred_element_type=F32)
            gact = lax.dot_general(gbranch, wout_ref[hidden, :], ALL, preferred_element_type=F32)
            square = pre * pre
            half = 0.5 + 0.5 * jnp.tanh(pre * (GELU_A + GELU_B * square))
            act = pre * half
            slope = half + act * (1.0 - half) * (2.0 * GELU_A + 6.0 * GELU_B * square)
            act_refs[block % 2][:, hidden] = act.astype(BF16)
            gpre_refs[block % 2][:, hidden] = (gact * slope).astype(BF16)

    def finish(block, state):
        row = block * block_rows
        standard, inv_std, normed, ups, grad_branch, gbranch = state
        act = act_refs[block % 2][...]
        gpre = gpre_refs[block % 2][...]
        branch = jnp.dot(act, wout_ref[...], preferred_element_type=F32)
        gnormed = lax.dot_general(gpre, win_ref[...], ALL, preferred_element_type=F32)
        gin_ref[...] += lax.dot_general(
            normed[:, :GIN_ROWS], gpre, OVER, preferred_element_type=F32
        )
        gout_ref[...] += lax.dot_general(
            gbranch[:, :C], act, OVER, preferred_element_type=F32
        )
        outs = []
        gs = []
        gn = []
        for t in range(2):
            lanes = slice(t * LANES, (t + 1) * LANES)
            branch_t = branch[:, lanes] + bias_out[t]
            feat = feat_ref[pl.ds(row, block_rows), :, lanes].reshape(cells, LANES).astype(F32)
            outs.append((feat + scale[t] * branch_t).astype(BF16))
            gn.append(gnormed[:, lanes])
            sums_ref[4, t] += partial(branch_t * ups[t])
            sums_ref[3, t] += partial(grad_branch[t].astype(F32))
            sums_ref[1, t] += partial(gn[t] * standard[t])
            sums_ref[2, t] += partial(gn[t])
            gs.append(gn[t] * gain[t])
        mean_g = jnp.sum(gs[0] + gs[1], axis=1, keepdims=True) * (1.0 / C)
        both = gs[0] * standard[0] + gs[1] * standard[1]
        mean_gs = jnp.sum(both, axis=1, keepdims=True) * (1.0 / C)
        gconv = []
        for t in range(2):
            grad = ((gs[t] - mean_g - standard[t] * mean_gs) * inv_std).astype(BF16)
            sums_ref[0, t] += partial(grad.astype(F32))
            gconv.append(grad)
        gconv_ref[pl.ds(row, block_rows)] = jnp.concatenate(gconv, axis=1).reshape(
            block_rows, lon_pad, CP
        )
        out = jnp.concatenate(outs, axis=1).reshape(block_rows, lon_pad, CP)
        out_ref[pl.ds(row, block_rows)] = out[:, : out_ref.shape[1], :C]

    states = [normalise(0)]
    hidden_units(0, states[0])
    for block in range(rows // block_rows):
        if block + 1 < rows // block_rows:
            states.append(normalise(block + 1))
            hidden_units(block + 1, states[block + 1])
        finish(block, states[block])


def taps_kernel(order, starts, rows, lon_pad, block_rows, conv_rows, inner, outer,
                me_ref, gconv_ref, inner_ref, outer_ref, gin_ref, gout_ref, sums_ref, done_ref,
                g_ref, done_hbm, rows_ref, acc_ref, wo32_ref, small_ref, done_sem):
    done_copy = pltpu.make_async_copy(done_ref, done_hbm, done_sem)
    done_copy.start()
    acc_ref[...] = jnp.zeros_like(acc_ref)
    pairs, filters = points_for(conv_rows)
    count = len(filters)

    for v_ref, ranges in ((inner_ref, inner), (outer_ref, outer)):

        def step(place, block, v_ref=v_ref):
            def side(tile, carry):
                lanes = pl.ds(pl.multiple_of(tile * LANES, LANES), LANES)
                grads = grad_points(
                    pairs,
                    [
                        gconv_ref[block * conv_rows + r, :, lanes].astype(F32)
                        for r in range(conv_rows)
                    ],
                )
                for k in range(count):
                    for b in range(KS):
                        term = grads[k] * v_ref[tile, place * count + k, pl.ds(b, lon_pad), :]
                        acc_ref[tile, k, b] += term.reshape(lon_pad // 8, 8, LANES).sum(axis=0)
                return carry

            lax.fori_loop(0, 2, side, 0, unroll=True)

        over_blocks(ranges, step)

    rows_ref[...] = jnp.zeros_like(rows_ref)
    small_ref[...] = jnp.zeros_like(small_ref)
    for t in range(2):
        totals = [jnp.sum(acc_ref[t, k], axis=1) for k in range(count)]
        for a in range(KS):
            small_ref[t, pl.ds(a * KS, KS), :] = weighted([f[a] for f in filters], totals)
        for at, k in ((TAPS, 0), (TAPS + 1, 1), (TAPS + 2, 2), (TAPS + 7, 3), (TAPS + 8, 4)):
            small_ref[t, pl.ds(at, 1), :] = jnp.sum(sums_ref[k, t], axis=0, keepdims=True)
        width = min(C, (t + 1) * LANES) - t * LANES
        wo32_ref[t, :, 0:width] = gout_ref[pl.ds(t * LANES, width), :].T
    outs = join_quarters(
        [[wo32_ref[t, pl.ds(q, C, stride=4), :] for t in range(2)] for q in range(4)]
    )
    tails = join_quarters(
        [[small_ref[t, pl.ds(q, 16, stride=4), :] for t in range(2)] for q in range(4)]
    )
    put_rows(rows_ref, 0, [gin_ref[pl.ds(0, C), j * LANES : (j + 1) * LANES] for j in range(TILES)])
    put_rows(rows_ref, ROW_OUT, outs)
    put_rows(rows_ref, ROW_TAPS, tails)
    put_rows(
        rows_ref,
        ROW_BIAS_IN,
        [gin_ref[pl.ds(C, 1), j * LANES : (j + 1) * LANES] for j in range(TILES)],
    )
    me = me_ref[0]
    window = g_ref.shape[1]
    for position, start in zip(order, starts):
        share = [rows_ref[t, pl.ds(start, window), :] for t in range(2)]
        g_ref[position ^ me] = jnp.concatenate(share, axis=1).astype(BF16)
    done_copy.wait()


def field_kernel(ranges, rows, cols, lon_pad, conv_rows, lat_halos, before, last, begun,
                 u_ref, up_ref, main_ref, west_ref, east_ref, *rest):
    rest = list(rest)
    south_ref, north_ref = (rest.pop(0), rest.pop(0)) if lat_halos else (None, None)
    before_ref = rest.pop(0) if before else None
    if begun:
        rest.pop(0)
    out_hbm = rest.pop(0) if before or last else None
    out_ref = None if last else rest.pop(0)
    x_ref, v_ref, sum_ref, before_sem, out_sem, own_ref = rest
    out_ref = own_ref if last else out_ref
    if before:
        before_copy = pltpu.make_async_copy(before_ref, out_hbm.at[pl.ds(*before)], before_sem)
        before_copy.start()
    field_points(
        ranges, conv_rows, x_ref, v_ref, main_ref, west_ref, east_ref, south_ref, north_ref, rows,
        cols,
    )

    def step(place, block):
        row = block * conv_rows

        def store(tile, lon, chunk, sums):
            lanes = pl.ds(pl.multiple_of(tile * LANES, LANES), LANES)
            for r in range(conv_rows):
                total = sums[r] + up_ref[row + r, pl.ds(lon, chunk), lanes].astype(F32)
                sum_ref[r, pl.ds(lon, chunk), lanes] = total

        depthwise_block(v_ref, u_ref, place, conv_rows, lon_pad, store, True, True)
        out_ref[pl.ds(place * conv_rows, conv_rows)] = sum_ref[:, 0:cols, 0:C].astype(BF16)
        if last:
            out_copy(place, block).start()

    def out_copy(place, block):
        return pltpu.make_async_copy(
            out_ref.at[pl.ds(place * conv_rows, conv_rows)],
            out_hbm.at[pl.ds(block * conv_rows, conv_rows)],
            out_sem.at[place],
        )

    over_blocks(ranges, step)
    if last:
        over_blocks(ranges, lambda place, block: out_copy(place, block).wait())
    if before:
        before_copy.wait()


def shape(dims, kind):
    return jax.ShapeDtypeStruct(dims, kind)


def whole(count):
    return [pl.BlockSpec(memory_space=pltpu.VMEM)] * count


def cost(micros):
    return pl.CostEstimate(flops=int(micros * 1.1e9), bytes_accessed=0, transcendentals=0)


def body(features, params, langevin_noise, upstream):
    rows, cols = features.shape[:2]
    lon_pad = up(cols, 16)
    lon_wide = up(lon_pad + KS - 1, 8)
    conv_rows = max(r for r in (1, 3, 5) if rows % r == 0)
    points = conv_rows + KS - 1
    blocks = rows // conv_rows
    block_rows = max(r for r in range(1, 16) if rows % r == 0 and r % conv_rows == 0)
    groups, bits = exchange_groups()
    count = 1 << bits
    lat_size = lax.axis_size("lat")
    length = params.shape[0]
    number = lax.axis_index("lon") * lat_size + lax.axis_index("lat")
    place = jnp.int32(0)
    for k in range(bits):
        place = place | (((number >> k) & 1) << (bits - 1 - k))
    place = place.reshape(1).astype(jnp.int32)
    offset = (number * length) % SHARE_LANES
    order = [reversed_bits(s, bits) for s in range(count)]
    starts = [s * length // SHARE_LANES for s in range(count)]
    spill = SHARE_LANES - math.gcd(SHARE_LANES, length)
    window = up(-(-(length + spill) // SHARE_LANES), 8)
    flat_rows = up(max(starts[-1] + window, 3 * (ROWS + 1)), 8)

    share = jnp.pad(params, (SHARE_LANES, window * SHARE_LANES - length))
    share = lax.dynamic_slice(share, (SHARE_LANES - offset,), (window * SHARE_LANES,)).astype(BF16)
    gathered = share.reshape(1, window, SHARE_LANES)
    compiler_params = pltpu.CompilerParams(vmem_limit_bytes=VMEM)
    smem = [pl.BlockSpec(memory_space=pltpu.SMEM)]
    margin = -(-RAD // conv_rows)
    inner = [(margin, blocks - 2 * margin)]
    outer = [(0, margin), (blocks - margin, margin)]
    edges = pl.pallas_call(
        lambda *refs: edge_kernel(cols, *refs),
        out_shape=(shape((rows, RAD, C), BF16),) * 2,
        in_specs=[pl.BlockSpec(memory_space=pltpu.HBM)],
        out_specs=tuple(whole(2)),
        scratch_shapes=[pltpu.VMEM((rows, cols, C), BF16)],
        compiler_params=compiler_params,
        cost_estimate=cost(1),
        name="edges",
    )(features)
    for k, group in enumerate(groups):
        parts = [swap(gathered, mask) for mask in group]
        if k == min(1, len(groups) - 1):
            west, east = shift_both(*edges, "lon", True)
        if k == max(0, len(groups) - 2):
            west, east, _, upstream = lax.optimization_barrier((west, east, gathered, upstream))
            wides = pl.pallas_call(
                lambda *refs: wide_kernel(rows, cols, *refs),
                out_shape=(shape((RAD, cols + 2 * RAD, C), BF16),) * 2,
                in_specs=whole(3),
                out_specs=tuple(whole(2)),
                compiler_params=compiler_params,
                cost_estimate=cost(1),
                name="wides",
            )(features, west, east)
            south, north = shift_both(*wides, "lat", False)
            inner_data, feats, ups = pl.pallas_call(
                lambda *refs: inner_kernel(inner, rows, cols, conv_rows, *refs),
                out_shape=(
                    shape((2, block_count(inner) * points, lon_wide, LANES), F32),
                    shape((rows, lon_pad, CP), BF16),
                    shape((rows, lon_pad, CP), BF16),
                ),
                in_specs=whole(4),
                out_specs=tuple(whole(3)),
                scratch_shapes=[pltpu.VMEM((2, padded_rows(inner, conv_rows), lon_wide, LANES), F32)],
                compiler_params=compiler_params,
                cost_estimate=cost(2.5),
                name="inner",
            )(features, west, east, upstream)
        gathered = jnp.concatenate([gathered, *parts], axis=0)
        if k == 0:
            edges, _ = lax.optimization_barrier((edges, gathered))
        if k == max(0, len(groups) - 2):
            gathered, inner_data = lax.optimization_barrier((gathered, inner_data))

    outer_data = pl.pallas_call(
        lambda *refs: outer_kernel(outer, rows, cols, conv_rows, *refs),
        out_shape=shape((2, block_count(outer) * points, lon_wide, LANES), F32),
        in_specs=whole(5),
        out_specs=whole(1)[0],
        scratch_shapes=[pltpu.VMEM((2, padded_rows(outer, conv_rows), lon_wide, LANES), F32)],
        compiler_params=compiler_params,
        cost_estimate=cost(1),
        name="outer",
    )(features, west, east, south, north)

    static = (order, starts, rows, lon_pad, block_rows, conv_rows, inner, outer)
    *weights, flipped = pl.pallas_call(
        lambda *refs: conv_kernel(*static, *refs),
        out_shape=(
            shape((2, rows, lon_pad, LANES), F32),
            shape((CP, H), BF16),
            shape((H, CP), BF16),
            shape((2, 64, LANES), F32),
            shape((2, points, 8, LANES), F32),
        ),
        in_specs=smem + whole(3),
        out_specs=tuple(whole(5)),
        scratch_shapes=[
            pltpu.VMEM((2, points, 8, LANES), F32),
            pltpu.VMEM((2, flat_rows, LANES), F32),
            pltpu.VMEM((2, H, LANES), F32),
            pltpu.VMEM((2, conv_rows, lon_pad, LANES), F32),
        ],
        compiler_params=compiler_params,
        cost_estimate=cost(6),
        name="conv",
    )(place, gathered, inner_data, outer_data)
    output, gconv, gin, gout, sums = pl.pallas_call(
        lambda *refs: layer_kernel(rows, lon_pad, block_rows, *refs),
        out_shape=(
            shape((rows, cols, C), BF16),
            shape((rows, lon_pad, CP), BF16),
            shape((GIN_ROWS, H), F32),
            shape((C, H), F32),
            shape((5, 2, 8, LANES), F32),
        ),
        in_specs=whole(6),
        out_specs=tuple(whole(5)),
        scratch_shapes=[pltpu.VMEM((block_rows * lon_pad, H), BF16)] * 4,
        compiler_params=compiler_params,
        cost_estimate=cost(16),
        name="layer",
    )(*weights, feats, ups)

    values, output = pl.pallas_call(
        lambda *refs: taps_kernel(*static, *refs),
        out_shape=(
            shape((count, window, SHARE_LANES), BF16),
            shape((rows, cols, C), BF16),
        ),
        in_specs=smem + whole(7),
        out_specs=(*whole(1), pl.BlockSpec(memory_space=pl.ANY)),
        scratch_shapes=[
            pltpu.VMEM((2, flat_rows, LANES), F32),
            pltpu.VMEM((2, points, KS, 8, LANES), F32),
            pltpu.VMEM((2, H, LANES), F32),
            pltpu.VMEM((2, 64, LANES), F32),
            pltpu.SemaphoreType.DMA(()),
        ],
        compiler_params=compiler_params,
        cost_estimate=cost(11),
        name="taps",
    )(place, gconv, inner_data, outer_data, gin, gout, sums, output)

    west, east = shift_both(gconv[:, :RAD, :C], gconv[:, cols - RAD : cols, :C], "lon", True)
    field = None

    def field_piece(ranges, lat_halos, before, field, last):
        count = block_count(ranges)
        own = shape((count * conv_rows, cols, C), BF16)
        operands = [flipped, ups, gconv, west, east, *lat_halos]
        in_specs = whole(len(operands))
        span = None
        if before is not None:
            span = (before[0], before[1].shape[0])
            operands.append(before[1])
            in_specs += whole(1)
        if field is not None:
            operands.append(field)
            in_specs.append(pl.BlockSpec(memory_space=pl.ANY))
        out_shape = []
        out_specs = []
        if before is not None or last:
            out_shape.append(shape((rows, cols, C), BF16))
            out_specs.append(pl.BlockSpec(memory_space=pl.ANY))
        if not last:
            out_shape.append(own)
            out_specs += whole(1)
        results = pl.pallas_call(
            lambda *refs: field_kernel(
                ranges, rows, cols, lon_pad, conv_rows, bool(lat_halos), span, last,
                field is not None, *refs
            ),
            out_shape=tuple(out_shape),
            in_specs=in_specs,
            out_specs=tuple(out_specs),
            scratch_shapes=[
                pltpu.VMEM((2, padded_rows(ranges, conv_rows), lon_wide, LANES), F32),
                pltpu.VMEM((2, count * points, lon_wide, LANES), F32),
                pltpu.VMEM((conv_rows, lon_pad, CP), F32),
                pltpu.SemaphoreType.DMA(()),
                pltpu.SemaphoreType.DMA((count,)),
                pltpu.VMEM(own.shape if last else (8, LANES), BF16),
            ],
            input_output_aliases={} if field is None else {len(operands) - 1: 0},
            compiler_params=compiler_params,
            cost_estimate=cost(1.1 * count),
            name="field",
        )(*operands)
        return (None if last else results[-1]), (results[0] if out_shape[0] is not own else None)

    early = (inner[0][1] + 1) // 2
    for k, group in enumerate(groups[::-1]):
        if k > 2:
            values, piece = lax.optimization_barrier((values, piece))
        if k == min(1, len(groups) - 1):
            values, west, east = lax.optimization_barrier((values, west, east))
        part = values.shape[0] // (len(group) + 1)
        sent = [values[(i + 1) * part : (i + 2) * part].astype(BF16) for i in range(len(group))]
        if k == min(1, len(groups) - 1):

            def wide(at):
                return jnp.concatenate([west[at], gconv[at, :cols, :C], east[at]], axis=1)

            wides = (wide(slice(0, RAD)), wide(slice(rows - RAD, rows)))
        received = [swap(one, mask) for one, mask in zip(sent, group)]
        if k == min(1, len(groups) - 1):
            piece, _ = field_piece([(margin, early)], (), None, None, False)
        if k == min(2, len(groups) - 1):
            lat_halos = shift_both(*wides, "lat", False)
            piece, _ = lax.optimization_barrier((piece, values))
            at = margin * conv_rows
            late = [(margin + early, inner[0][1] - early)]
            piece, field = field_piece(late, (), (at, piece), None, False)
        values = values[:part].astype(F32)
        for other in received:
            values = values + other.astype(F32)
        if k == 1 and len(groups) > 2:
            values, wides = lax.optimization_barrier((values, wides))
    at = (margin + early) * conv_rows
    _, field = field_piece(outer, lat_halos, (at, piece), field, True)
    summed = lax.dynamic_slice(values.reshape(-1), (offset,), (length,))
    new_params = params - STEP_SIZE * summed + NOISE_COEF * langevin_noise
    return (output, field, new_params)


def solution(mesh):
    return jax.shard_map(
        body,
        mesh=mesh,
        in_specs=(
            P("lat", "lon", None),
            P(("lon", "lat")),
            P(("lon", "lat")),
            P("lat", "lon", None),
        ),
        out_specs=(P("lat", "lon", None), P("lat", "lon", None), P(("lon", "lat"))),
        check_vma=False,
    )
```

```python
import math

import jax
import jax.numpy as jnp
from jax import lax
from jax.experimental import pallas as pl
from jax.experimental.pallas import tpu as pltpu
from jax.sharding import PartitionSpec as P

C = 192
H = 768
KS = 7
RAD = KS // 2
LANES = 128
CP = 256
TAPS = KS * KS
EPSILON = 1e-06
STEP_SIZE = 0.003
NOISE_COEF = 0.08
GELU_A = math.sqrt(2.0 / math.pi)
GELU_B = GELU_A * 0.044715
F32 = jnp.float32
BF16 = jnp.bfloat16
ROW_OUT = C
ROW_TAPS = 2 * C
ROW_NORM = ROW_TAPS + TAPS // 4
ROW_BIAS_IN = ROW_NORM + 1
ROW_LAST = ROW_NORM + 2
ROWS = ROW_LAST + 1
TILES = H // LANES
SHARE_LANES = 256
CHUNK = 256
UNROLL = True
GIN_ROWS = C + 8
ALL = ((1,), (1,)), ((), ())
OVER = ((0,), (0,)), ((), ())
VMEM = 28 << 20


def exchange_groups():
    lon, lat = lax.axis_size("lon"), lax.axis_size("lat")
    bits = [(lon >> k, 0) for k in range(1, lon.bit_length())]
    bits += [(0, lat >> k) for k in range(1, lat.bit_length())]
    groups = []
    k = 0
    while k < len(bits):
        if k + 1 < len(bits) and bits[k][0] == 1 and bits[k + 1][0] == 0:
            (lon_bit, _), (_, lat_bit) = bits[k : k + 2]
            groups.append([(lon_bit, 0), (0, lat_bit), (lon_bit, lat_bit)])
            k += 2
        else:
            groups.append([bits[k]])
            k += 1
    return groups, len(bits)


def swap(values, mask):
    lon, lat = lax.axis_size("lon"), lax.axis_size("lat")
    pairs = [
        (i * lat + j, (i ^ mask[0]) * lat + (j ^ mask[1])) for i in range(lon) for j in range(lat)
    ]
    return lax.ppermute(values, ("lon", "lat"), pairs)


def send_edges(low_edge, high_edge, axis, periodic):
    count = lax.axis_size(axis)
    even = lax.axis_index(axis) % 2 == 0
    near = [(i, i ^ 1) for i in range(count)]
    odds = [(i, (i + 1) % count) for i in range(1, count if periodic else count - 1, 2)]
    far = odds + [(target, source) for source, target in odds]
    near = lax.ppermute(jnp.where(even, high_edge, low_edge), axis, near)
    far = lax.ppermute(jnp.where(even, low_edge, high_edge), axis, far)
    return near, far


def edges_from(near, far, axis):
    even = lax.axis_index(axis) % 2 == 0
    return jnp.where(even, far, near), jnp.where(even, near, far)


def shift_both(low_edge, high_edge, axis, periodic):
    return edges_from(*send_edges(low_edge, high_edge, axis, periodic), axis)


def reversed_bits(number, count):
    result = 0
    for k in range(count):
        result |= ((number >> k) & 1) << (count - 1 - k)
    return result


def up(value, multiple):
    return -(-value // multiple) * multiple


def split_quarter(tiles, quarter):
    lane = lax.broadcasted_iota(jnp.int32, tiles[0].shape, 1)
    low = lane < LANES // 2
    first = 3 * quarter // 2
    if quarter % 2 == 0:
        return tiles[first], jnp.where(low, tiles[first + 1], 0.0)
    left = pltpu.roll(tiles[first], LANES // 2, 1)
    right = pltpu.roll(tiles[first + 1], LANES // 2, 1)
    return jnp.where(low, left, right), jnp.where(low, right, 0.0)


def join_quarters(quarters):
    lane = lax.broadcasted_iota(jnp.int32, quarters[0][0].shape, 1)
    low = lane < LANES // 2
    tiles = []
    for even in (0, 2):
        first, second = quarters[even]
        turned = pltpu.roll(quarters[even + 1][0], LANES // 2, 1)
        last = pltpu.roll(quarters[even + 1][1], LANES // 2, 1)
        tiles += [first, jnp.where(low, second, turned), jnp.where(low, turned, last)]
    return tiles


def get_rows(flat_ref, row, count):
    return [
        flat_ref[j % 2, pl.ds(3 * row + j // 2, count, stride=3), :] for j in range(TILES)
    ]


def put_rows(flat_ref, row, tiles):
    for j in range(TILES):
        flat_ref[j % 2, pl.ds(3 * row + j // 2, tiles[j].shape[0], stride=3), :] = tiles[j]


def assemble(x_ref, base, first, count, main, west, east, south, north, rows, cols):
    for t in range(2):
        lanes = slice(t * LANES, min(C, (t + 1) * LANES))
        width = slice(0, lanes.stop - lanes.start)
        low = max(0, first - RAD)
        high = min(rows, first + count - RAD)
        at = slice(base + low + RAD - first, base + high + RAD - first)
        if main.shape[2] == CP:
            span = slice(RAD, RAD + main.shape[1])
            x_ref[t, at, span, :] = main[low:high, :, t * LANES : (t + 1) * LANES].astype(F32)
        else:
            x_ref[t, at, RAD : RAD + cols, width] = main[low:high, 0:cols, lanes].astype(F32)
        x_ref[t, at, 0:RAD, width] = west[low:high, :, lanes].astype(F32)
        x_ref[t, at, RAD + cols : 2 * RAD + cols, width] = east[low:high, :, lanes].astype(F32)
        wide = slice(0, cols + 2 * RAD)
        if first < RAD:
            at = slice(base, base + RAD - first)
            x_ref[t, at] = jnp.zeros_like(x_ref[t, at])
            x_ref[t, at, wide, width] = south[first:, :, lanes].astype(F32)
        over = first + count - rows - RAD
        if over > 0:
            at = slice(base + count - over, base + count)
            x_ref[t, at] = jnp.zeros_like(x_ref[t, at])
            x_ref[t, at, wide, width] = north[0:over, :, lanes].astype(F32)


def field_points(ranges, conv_rows, x_ref, v_ref, main, west, east, south, north, rows, cols):
    if main.shape[1:] == (x_ref.shape[2] - 8, CP):
        for t in range(2):
            for lon in (0, x_ref.shape[2] - 8):
                x_ref[t, :, lon : lon + 8, :] = jnp.zeros_like(x_ref[t, :, lon : lon + 8, :])
    else:
        x_ref[...] = jnp.zeros_like(x_ref)
    base = done = 0
    for first, count in ranges:
        span = count * conv_rows + KS - 1
        assemble(
            x_ref, base, first * conv_rows, span, main, west, east, south, north, rows, cols
        )
        write_points(x_ref, base, v_ref, done, count, conv_rows)
        base += span
        done += count


def padded_rows(ranges, conv_rows):
    return sum(count * conv_rows + KS - 1 for _, count in ranges)


def block_count(ranges):
    return sum(count for _, count in ranges)


def over_blocks(ranges, step):
    done = 0
    for first, count in ranges:

        def body(i, carry, done=done, first=first):
            step(done + i, first + i)
            return carry

        lax.fori_loop(0, count, body, 0)
        done += count


def edge_kernel(cols, field_hbm, west_ref, east_ref, field_ref):
    pltpu.sync_copy(field_hbm, field_ref)
    west_ref[...] = field_ref[:, 0:RAD, :]
    east_ref[...] = field_ref[:, cols - RAD : cols, :]


def wide_kernel(rows, cols, field_ref, west_ref, east_ref, south_ref, north_ref):
    for out_ref, first in ((south_ref, 0), (north_ref, rows - RAD)):
        at = slice(first, first + RAD)
        out_ref[:, 0:RAD, :] = west_ref[at]
        out_ref[:, RAD : RAD + cols, :] = field_ref[at, 0:cols, :]
        out_ref[:, RAD + cols : 2 * RAD + cols, :] = east_ref[at]


def inner_kernel(ranges, rows, cols, conv_rows, feat_ref, west_ref, east_ref, up_ref,
                 v_ref, feats_ref, ups_ref, x_ref):
    field_points(
        ranges, conv_rows, x_ref, v_ref, feat_ref, west_ref, east_ref, None, None, rows, cols
    )
    feats_ref[...] = jnp.zeros_like(feats_ref)
    feats_ref[:, 0:cols, 0:C] = feat_ref[...]
    ups_ref[...] = jnp.zeros_like(ups_ref)
    ups_ref[:, 0:cols, 0:C] = up_ref[...]


def outer_kernel(ranges, rows, cols, conv_rows, feat_ref, west_ref, east_ref, south_ref, north_ref,
                 v_ref, x_ref):
    field_points(
        ranges, conv_rows, x_ref, v_ref, feat_ref, west_ref, east_ref, south_ref, north_ref, rows,
        cols,
    )


def points_for(out_rows):
    pairs = [1.0, 0.5, 2.0, 1.5, 0.75][: (out_rows + KS - 2) // 2]
    points = [0.0] + [sign * p for p in pairs for sign in (1.0, -1.0)]
    filters = []
    for k, point in enumerate(points):
        scale = math.prod(point - other for i, other in enumerate(points) if i != k)
        filters.append([point**a / scale for a in range(KS)])
    return pairs, filters


def polynomial(roots):
    coefs = [1.0]
    for root in roots:
        coefs = [
            (coefs[i - 1] if i else 0.0) - (root * coefs[i] if i < len(coefs) else 0.0)
            for i in range(len(coefs) + 1)
        ]
    return coefs


def weighted(coefs, values):
    total = None
    for coef, value in zip(coefs, values):
        if coef == 0.0:
            continue
        term = value if coef == 1.0 else value * coef
        total = term if total is None else total + term
    return total


def data_points(pairs, rows):
    squares = [p * p for p in pairs]
    values = [weighted(polynomial(squares), rows[0::2])]
    for p in pairs:
        coefs = polynomial([q for q in squares if q != p * p])
        even = weighted(coefs, rows[2::2])
        odd = weighted([p * c for c in coefs], rows[1::2])
        values += [even + odd, even - odd]
    return values


def grad_points(pairs, rows):
    values = [rows[0]]
    for p in pairs:
        even = weighted([p ** (2 * i) for i in range(len(rows[0::2]))], rows[0::2])
        odd = weighted([p ** (2 * i + 1) for i in range(len(rows[1::2]))], rows[1::2])
        values += [even + odd, even - odd] if odd is not None else [even, even]
    return values


def write_points(x_ref, base, v_ref, done, blocks, out_rows):
    pairs, filters = points_for(out_rows)
    count = len(filters)
    lon_regs = x_ref.shape[2] // 8

    for step in range(2 * lon_regs):
        tile = step // lon_regs
        lon = pl.ds(step % lon_regs * 8, 8)
        for k in range(blocks):
            rows = [x_ref[tile, base + k * out_rows + r, lon, :] for r in range(count)]
            for i, value in enumerate(data_points(pairs, rows)):
                v_ref[tile, (done + k) * count + i, lon, :] = value


def filter_points(taps_ref, out_rows, u_ref, flip):
    for k, coefs in enumerate(points_for(out_rows)[1]):
        coefs = coefs[::-1] if flip else coefs
        for t in range(2):
            u_ref[t, k, 0:KS, :] = weighted(
                coefs, [taps_ref[t, pl.ds(a * KS, KS), :] for a in range(KS)]
            )


def depthwise_block(v_ref, u_ref, block, out_rows, lon_pad, store, flip, unroll):
    pairs, filters = points_for(out_rows)
    count = len(filters)
    chunk = lon_pad

    def body(step, carry):
        tile = step // (lon_pad // chunk)
        lon = pl.multiple_of(step % (lon_pad // chunk) * chunk, 8)

        def product(k):
            total = None
            for b in range(KS):
                tap = KS - 1 - b if flip else b
                term = v_ref[tile, block * count + k, pl.ds(lon + b, chunk), :]
                term = term * u_ref[tile, k, pl.ds(tap, 1), :]
                total = term if total is None else total + term
            return total

        sums = [None] * out_rows
        sums[0] = product(0)
        for i, p in enumerate(pairs):
            plus, minus = product(2 * i + 1), product(2 * i + 2)
            even, odd = plus + minus, plus - minus
            for r in range(out_rows):
                term = odd if r % 2 else even
                term = term if p**r == 1.0 else term * p**r
                sums[r] = term if sums[r] is None else sums[r] + term
        store(tile, lon, chunk, sums)
        return carry

    lax.fori_loop(0, 2 * (lon_pad // chunk), body, 0, unroll=unroll)


def conv_kernel(order, starts, rows, lon_pad, block_rows, conv_rows, inner, outer,
                me_ref, gathered_ref, inner_ref, outer_ref,
                conv_ref, win_ref, wout_ref, taps_ref, flipped_ref, u_ref, w_ref, wo32_ref, sum_ref):
    me = me_ref[0]
    window = gathered_ref.shape[1]
    w_ref[:, 0:8, :] = jnp.zeros_like(w_ref[:, 0:8, :])
    w_ref[:, starts[-1] :, :] = jnp.zeros_like(w_ref[:, starts[-1] :, :])
    for position, start in zip(order, starts):
        share = gathered_ref[position ^ me].astype(F32)
        for t in range(2):
            part = share[:, t * LANES : (t + 1) * LANES]
            first = w_ref[t, pl.ds(start, 1), :] + part[0:1]
            w_ref[t, pl.ds(start, window), :] = part
            w_ref[t, pl.ds(start, 1), :] = first
    rest = lax.broadcasted_iota(jnp.int32, (CP - C, LANES), 0)
    mains = get_rows(w_ref, 0, C)
    biases = get_rows(w_ref, ROW_BIAS_IN, 1)
    for j in range(TILES):
        bias = jnp.where(rest == 0, biases[j], 0.0)
        whole = jnp.concatenate([mains[j], bias], axis=0)
        win_ref[:, j * LANES : (j + 1) * LANES] = whole.astype(BF16)
    out_rows = get_rows(w_ref, ROW_OUT, C)
    tail_rows = get_rows(w_ref, ROW_TAPS, 16)
    for quarter in range(4):
        pair = split_quarter(out_rows, quarter)
        tail = split_quarter(tail_rows, quarter)
        for t in range(2):
            wo32_ref[t, pl.ds(quarter, C, stride=4), :] = pair[t]
            taps_ref[t, pl.ds(quarter, 16, stride=4), :] = tail[t]
    for t in range(2):
        wout_ref[:, t * LANES : (t + 1) * LANES] = wo32_ref[t].astype(BF16)

    filter_points(taps_ref, conv_rows, u_ref, False)
    filter_points(taps_ref, conv_rows, flipped_ref, True)
    for v_ref, ranges in ((inner_ref, inner), (outer_ref, outer)):

        def conv_step(place, block, v_ref=v_ref):
            def store(tile, lon, chunk, sums):
                for r in range(conv_rows):
                    sum_ref[tile, r, pl.ds(lon, chunk), :] = sums[r]

            depthwise_block(v_ref, u_ref, place, conv_rows, lon_pad, store, False, UNROLL)
            conv_ref[:, pl.ds(block * conv_rows, conv_rows)] = sum_ref[...]

        over_blocks(ranges, conv_step)


def layer_kernel(rows, lon_pad, block_rows, conv_ref, win_ref, wout_ref, taps_ref, feat_ref, up_ref,
                 out_ref, gconv_ref, gin_ref, gout_ref, sums_ref, *hidden_refs):
    act_refs, gpre_refs = hidden_refs[:2], hidden_refs[2:]
    def vector(row, quarter):
        at = (row - ROW_TAPS) * 4 + quarter
        return [taps_ref[t, pl.ds(at, 1), :] for t in range(2)]

    cbias = vector(ROW_NORM, 1)
    gain = vector(ROW_NORM, 2)
    shift = vector(ROW_NORM, 3)
    bias_out = vector(ROW_LAST, 0)
    scale = vector(ROW_LAST, 1)
    lane = lax.broadcasted_iota(jnp.int32, (1, LANES), 1)
    inside = (lane < C - LANES).astype(F32)
    shift[1] = shift[1] + (lane == C - LANES).astype(F32)

    gin_ref[...] = jnp.zeros_like(gin_ref)
    gout_ref[...] = jnp.zeros_like(gout_ref)
    sums_ref[...] = jnp.zeros_like(sums_ref)
    cells = block_rows * lon_pad

    def partial(values):
        return values.reshape(cells // 8, 8, LANES).sum(axis=0)

    def normalise(block):
        row = block * block_rows
        conv = [
            conv_ref[t, pl.ds(row, block_rows)].reshape(cells, LANES) + cbias[t] for t in range(2)
        ]
        mean = jnp.sum(conv[0] + conv[1], axis=1, keepdims=True) * (1.0 / C)
        centred = [conv[0] - mean, (conv[1] - mean) * inside]
        square = centred[0] * centred[0] + centred[1] * centred[1]
        inv_std = lax.rsqrt(jnp.sum(square, axis=1, keepdims=True) * (1.0 / C) + EPSILON)
        standard = [c * inv_std for c in centred]
        normed = jnp.concatenate(
            [(standard[t] * gain[t] + shift[t]).astype(BF16) for t in range(2)], axis=1
        )
        upstream = up_ref[pl.ds(row, block_rows)].reshape(cells, CP)
        ups = [upstream[:, t * LANES : (t + 1) * LANES].astype(F32) for t in range(2)]
        grad_branch = [(scale[t] * ups[t]).astype(BF16) for t in range(2)]
        gbranch = jnp.concatenate(grad_branch, axis=1)
        return standard, inv_std, normed, ups, grad_branch, gbranch

    def hidden_units(block, state):
        normed, gbranch = state[2], state[5]
        for h in range(0, H, CHUNK):
            hidden = slice(h, h + CHUNK)
            pre = jnp.dot(normed, win_ref[:, hidden], preferred_element_type=F32)
            gact = lax.dot_general(gbranch, wout_ref[hidden, :], ALL, preferred_element_type=F32)
            square = pre * pre
            half = 0.5 + 0.5 * jnp.tanh(pre * (GELU_A + GELU_B * square))
            act = pre * half
            slope = half + act * (1.0 - half) * (2.0 * GELU_A + 6.0 * GELU_B * square)
            act_refs[block % 2][:, hidden] = act.astype(BF16)
            gpre_refs[block % 2][:, hidden] = (gact * slope).astype(BF16)

    def finish(block, state):
        row = block * block_rows
        standard, inv_std, normed, ups, grad_branch, gbranch = state
        act = act_refs[block % 2][...]
        gpre = gpre_refs[block % 2][...]
        branch = jnp.dot(act, wout_ref[...], preferred_element_type=F32)
        gnormed = lax.dot_general(gpre, win_ref[...], ALL, preferred_element_type=F32)
        gin_ref[...] += lax.dot_general(
            normed[:, :GIN_ROWS], gpre, OVER, preferred_element_type=F32
        )
        gout_ref[...] += lax.dot_general(
            gbranch[:, :C], act, OVER, preferred_element_type=F32
        )
        outs = []
        gs = []
        gn = []
        for t in range(2):
            lanes = slice(t * LANES, (t + 1) * LANES)
            branch_t = branch[:, lanes] + bias_out[t]
            feat = feat_ref[pl.ds(row, block_rows), :, lanes].reshape(cells, LANES).astype(F32)
            outs.append((feat + scale[t] * branch_t).astype(BF16))
            gn.append(gnormed[:, lanes])
            sums_ref[4, t] += partial(branch_t * ups[t])
            sums_ref[3, t] += partial(grad_branch[t].astype(F32))
            sums_ref[1, t] += partial(gn[t] * standard[t])
            sums_ref[2, t] += partial(gn[t])
            gs.append(gn[t] * gain[t])
        mean_g = jnp.sum(gs[0] + gs[1], axis=1, keepdims=True) * (1.0 / C)
        both = gs[0] * standard[0] + gs[1] * standard[1]
        mean_gs = jnp.sum(both, axis=1, keepdims=True) * (1.0 / C)
        gconv = []
        for t in range(2):
            grad = ((gs[t] - mean_g - standard[t] * mean_gs) * inv_std).astype(BF16)
            sums_ref[0, t] += partial(grad.astype(F32))
            gconv.append(grad)
        gconv_ref[pl.ds(row, block_rows)] = jnp.concatenate(gconv, axis=1).reshape(
            block_rows, lon_pad, CP
        )
        out = jnp.concatenate(outs, axis=1).reshape(block_rows, lon_pad, CP)
        out_ref[pl.ds(row, block_rows)] = out[:, : out_ref.shape[1], :C]

    states = [normalise(0)]
    hidden_units(0, states[0])
    for block in range(rows // block_rows):
        if block + 1 < rows // block_rows:
            states.append(normalise(block + 1))
            hidden_units(block + 1, states[block + 1])
        finish(block, states[block])


def taps_kernel(order, starts, rows, lon_pad, block_rows, conv_rows, inner, outer,
                me_ref, gconv_ref, inner_ref, outer_ref, gin_ref, gout_ref, sums_ref, done_ref,
                g_ref, done_hbm, rows_ref, acc_ref, wo32_ref, small_ref, done_sem):
    done_copy = pltpu.make_async_copy(done_ref, done_hbm, done_sem)
    done_copy.start()
    acc_ref[...] = jnp.zeros_like(acc_ref)
    pairs, filters = points_for(conv_rows)
    count = len(filters)

    for v_ref, ranges in ((inner_ref, inner), (outer_ref, outer)):

        def step(place, block, v_ref=v_ref):
            def side(tile, carry):
                lanes = pl.ds(pl.multiple_of(tile * LANES, LANES), LANES)
                grads = grad_points(
                    pairs,
                    [
                        gconv_ref[block * conv_rows + r, :, lanes].astype(F32)
                        for r in range(conv_rows)
                    ],
                )
                for k in range(count):
                    for b in range(KS):
                        term = grads[k] * v_ref[tile, place * count + k, pl.ds(b, lon_pad), :]
                        acc_ref[tile, k, b] += term.reshape(lon_pad // 8, 8, LANES).sum(axis=0)
                return carry

            lax.fori_loop(0, 2, side, 0, unroll=True)

        over_blocks(ranges, step)

    rows_ref[...] = jnp.zeros_like(rows_ref)
    small_ref[...] = jnp.zeros_like(small_ref)
    for t in range(2):
        totals = [jnp.sum(acc_ref[t, k], axis=1) for k in range(count)]
        for a in range(KS):
            small_ref[t, pl.ds(a * KS, KS), :] = weighted([f[a] for f in filters], totals)
        for at, k in ((TAPS, 0), (TAPS + 1, 1), (TAPS + 2, 2), (TAPS + 7, 3), (TAPS + 8, 4)):
            small_ref[t, pl.ds(at, 1), :] = jnp.sum(sums_ref[k, t], axis=0, keepdims=True)
        width = min(C, (t + 1) * LANES) - t * LANES
        wo32_ref[t, :, 0:width] = gout_ref[pl.ds(t * LANES, width), :].T
    outs = join_quarters(
        [[wo32_ref[t, pl.ds(q, C, stride=4), :] for t in range(2)] for q in range(4)]
    )
    tails = join_quarters(
        [[small_ref[t, pl.ds(q, 16, stride=4), :] for t in range(2)] for q in range(4)]
    )
    put_rows(rows_ref, 0, [gin_ref[pl.ds(0, C), j * LANES : (j + 1) * LANES] for j in range(TILES)])
    put_rows(rows_ref, ROW_OUT, outs)
    put_rows(rows_ref, ROW_TAPS, tails)
    put_rows(
        rows_ref,
        ROW_BIAS_IN,
        [gin_ref[pl.ds(C, 1), j * LANES : (j + 1) * LANES] for j in range(TILES)],
    )
    me = me_ref[0]
    window = g_ref.shape[1]
    for position, start in zip(order, starts):
        share = [rows_ref[t, pl.ds(start, window), :] for t in range(2)]
        g_ref[position ^ me] = jnp.concatenate(share, axis=1).astype(BF16)
    done_copy.wait()


def field_kernel(ranges, rows, cols, lon_pad, conv_rows, lat_halos, before, last, begun,
                 u_ref, up_ref, main_ref, west_ref, east_ref, *rest):
    rest = list(rest)
    south_ref, north_ref = (rest.pop(0), rest.pop(0)) if lat_halos else (None, None)
    before_ref = rest.pop(0) if before else None
    if begun:
        rest.pop(0)
    out_hbm = rest.pop(0) if before or last else None
    out_ref = None if last else rest.pop(0)
    x_ref, v_ref, sum_ref, before_sem, out_sem, own_ref = rest
    out_ref = own_ref if last else out_ref
    if before:
        before_copy = pltpu.make_async_copy(before_ref, out_hbm.at[pl.ds(*before)], before_sem)
        before_copy.start()
    field_points(
        ranges, conv_rows, x_ref, v_ref, main_ref, west_ref, east_ref, south_ref, north_ref, rows,
        cols,
    )

    def step(place, block):
        row = block * conv_rows

        def store(tile, lon, chunk, sums):
            lanes = pl.ds(pl.multiple_of(tile * LANES, LANES), LANES)
            for r in range(conv_rows):
                total = sums[r] + up_ref[row + r, pl.ds(lon, chunk), lanes].astype(F32)
                sum_ref[r, pl.ds(lon, chunk), lanes] = total

        depthwise_block(v_ref, u_ref, place, conv_rows, lon_pad, store, True, True)
        out_ref[pl.ds(place * conv_rows, conv_rows)] = sum_ref[:, 0:cols, 0:C].astype(BF16)
        if last:
            out_copy(place, block).start()

    def out_copy(place, block):
        return pltpu.make_async_copy(
            out_ref.at[pl.ds(place * conv_rows, conv_rows)],
            out_hbm.at[pl.ds(block * conv_rows, conv_rows)],
            out_sem.at[place],
        )

    over_blocks(ranges, step)
    if last:
        over_blocks(ranges, lambda place, block: out_copy(place, block).wait())
    if before:
        before_copy.wait()


def shape(dims, kind):
    return jax.ShapeDtypeStruct(dims, kind)


def whole(count):
    return [pl.BlockSpec(memory_space=pltpu.VMEM)] * count


def cost(micros):
    return pl.CostEstimate(flops=int(micros * 1.1e9), bytes_accessed=0, transcendentals=0)


def body(features, params, langevin_noise, upstream):
    rows, cols = features.shape[:2]
    lon_pad = up(cols, 16)
    lon_wide = up(lon_pad + KS - 1, 8)
    conv_rows = max(r for r in (1, 3, 5) if rows % r == 0)
    points = conv_rows + KS - 1
    blocks = rows // conv_rows
    block_rows = max(r for r in range(1, 16) if rows % r == 0 and r % conv_rows == 0)
    groups, bits = exchange_groups()
    count = 1 << bits
    lat_size = lax.axis_size("lat")
    length = params.shape[0]
    number = lax.axis_index("lon") * lat_size + lax.axis_index("lat")
    place = jnp.int32(0)
    for k in range(bits):
        place = place | (((number >> k) & 1) << (bits - 1 - k))
    place = place.reshape(1).astype(jnp.int32)
    offset = (number * length) % SHARE_LANES
    order = [reversed_bits(s, bits) for s in range(count)]
    starts = [s * length // SHARE_LANES for s in range(count)]
    spill = SHARE_LANES - math.gcd(SHARE_LANES, length)
    window = up(-(-(length + spill) // SHARE_LANES), 8)
    flat_rows = up(max(starts[-1] + window, 3 * (ROWS + 1)), 8)

    share = jnp.pad(params, (SHARE_LANES, window * SHARE_LANES - length))
    share = lax.dynamic_slice(share, (SHARE_LANES - offset,), (window * SHARE_LANES,)).astype(BF16)
    gathered = share.reshape(1, window, SHARE_LANES)
    compiler_params = pltpu.CompilerParams(vmem_limit_bytes=VMEM)
    smem = [pl.BlockSpec(memory_space=pltpu.SMEM)]
    margin = -(-RAD // conv_rows)
    inner = [(margin, blocks - 2 * margin)]
    outer = [(0, margin), (blocks - margin, margin)]
    edges = pl.pallas_call(
        lambda *refs: edge_kernel(cols, *refs),
        out_shape=(shape((rows, RAD, C), BF16),) * 2,
        in_specs=[pl.BlockSpec(memory_space=pltpu.HBM)],
        out_specs=tuple(whole(2)),
        scratch_shapes=[pltpu.VMEM((rows, cols, C), BF16)],
        compiler_params=compiler_params,
        cost_estimate=cost(1),
        name="edges",
    )(features)
    for k, group in enumerate(groups):
        parts = [swap(gathered, mask) for mask in group]
        if k == min(1, len(groups) - 1):
            west, east = shift_both(*edges, "lon", True)
        if k == max(0, len(groups) - 2):
            west, east, _, upstream = lax.optimization_barrier((west, east, gathered, upstream))
            wides = pl.pallas_call(
                lambda *refs: wide_kernel(rows, cols, *refs),
                out_shape=(shape((RAD, cols + 2 * RAD, C), BF16),) * 2,
                in_specs=whole(3),
                out_specs=tuple(whole(2)),
                compiler_params=compiler_params,
                cost_estimate=cost(1),
                name="wides",
            )(features, west, east)
            south, north = shift_both(*wides, "lat", False)
            inner_data, feats, ups = pl.pallas_call(
                lambda *refs: inner_kernel(inner, rows, cols, conv_rows, *refs),
                out_shape=(
                    shape((2, block_count(inner) * points, lon_wide, LANES), F32),
                    shape((rows, lon_pad, CP), BF16),
                    shape((rows, lon_pad, CP), BF16),
                ),
                in_specs=whole(4),
                out_specs=tuple(whole(3)),
                scratch_shapes=[pltpu.VMEM((2, padded_rows(inner, conv_rows), lon_wide, LANES), F32)],
                compiler_params=compiler_params,
                cost_estimate=cost(2.5),
                name="inner",
            )(features, west, east, upstream)
        gathered = jnp.concatenate([gathered, *parts], axis=0)
        if k == 0:
            edges, _ = lax.optimization_barrier((edges, gathered))
        if k == max(0, len(groups) - 2):
            gathered, inner_data = lax.optimization_barrier((gathered, inner_data))

    outer_data = pl.pallas_call(
        lambda *refs: outer_kernel(outer, rows, cols, conv_rows, *refs),
        out_shape=shape((2, block_count(outer) * points, lon_wide, LANES), F32),
        in_specs=whole(5),
        out_specs=whole(1)[0],
        scratch_shapes=[pltpu.VMEM((2, padded_rows(outer, conv_rows), lon_wide, LANES), F32)],
        compiler_params=compiler_params,
        cost_estimate=cost(1),
        name="outer",
    )(features, west, east, south, north)

    static = (order, starts, rows, lon_pad, block_rows, conv_rows, inner, outer)
    *weights, flipped = pl.pallas_call(
        lambda *refs: conv_kernel(*static, *refs),
        out_shape=(
            shape((2, rows, lon_pad, LANES), F32),
            shape((CP, H), BF16),
            shape((H, CP), BF16),
            shape((2, 64, LANES), F32),
            shape((2, points, 8, LANES), F32),
        ),
        in_specs=smem + whole(3),
        out_specs=tuple(whole(5)),
        scratch_shapes=[
            pltpu.VMEM((2, points, 8, LANES), F32),
            pltpu.VMEM((2, flat_rows, LANES), F32),
            pltpu.VMEM((2, H, LANES), F32),
            pltpu.VMEM((2, conv_rows, lon_pad, LANES), F32),
        ],
        compiler_params=compiler_params,
        cost_estimate=cost(6),
        name="conv",
    )(place, gathered, inner_data, outer_data)
    output, gconv, gin, gout, sums = pl.pallas_call(
        lambda *refs: layer_kernel(rows, lon_pad, block_rows, *refs),
        out_shape=(
            shape((rows, cols, C), BF16),
            shape((rows, lon_pad, CP), BF16),
            shape((GIN_ROWS, H), F32),
            shape((C, H), F32),
            shape((5, 2, 8, LANES), F32),
        ),
        in_specs=whole(6),
        out_specs=tuple(whole(5)),
        scratch_shapes=[pltpu.VMEM((block_rows * lon_pad, H), BF16)] * 4,
        compiler_params=compiler_params,
        cost_estimate=cost(16),
        name="layer",
    )(*weights, feats, ups)

    values, output = pl.pallas_call(
        lambda *refs: taps_kernel(*static, *refs),
        out_shape=(
            shape((count, window, SHARE_LANES), BF16),
            shape((rows, cols, C), BF16),
        ),
        in_specs=smem + whole(7),
        out_specs=(*whole(1), pl.BlockSpec(memory_space=pl.ANY)),
        scratch_shapes=[
            pltpu.VMEM((2, flat_rows, LANES), F32),
            pltpu.VMEM((2, points, KS, 8, LANES), F32),
            pltpu.VMEM((2, H, LANES), F32),
            pltpu.VMEM((2, 64, LANES), F32),
            pltpu.SemaphoreType.DMA(()),
        ],
        compiler_params=compiler_params,
        cost_estimate=cost(11),
        name="taps",
    )(place, gconv, inner_data, outer_data, gin, gout, sums, output)

    west, east = shift_both(gconv[:, :RAD, :C], gconv[:, cols - RAD : cols, :C], "lon", True)
    field = None

    def field_piece(ranges, lat_halos, before, field, last):
        count = block_count(ranges)
        own = shape((count * conv_rows, cols, C), BF16)
        operands = [flipped, ups, gconv, west, east, *lat_halos]
        in_specs = whole(len(operands))
        span = None
        if before is not None:
            span = (before[0], before[1].shape[0])
            operands.append(before[1])
            in_specs += whole(1)
        if field is not None:
            operands.append(field)
            in_specs.append(pl.BlockSpec(memory_space=pl.ANY))
        out_shape = []
        out_specs = []
        if before is not None or last:
            out_shape.append(shape((rows, cols, C), BF16))
            out_specs.append(pl.BlockSpec(memory_space=pl.ANY))
        if not last:
            out_shape.append(own)
            out_specs += whole(1)
        results = pl.pallas_call(
            lambda *refs: field_kernel(
                ranges, rows, cols, lon_pad, conv_rows, bool(lat_halos), span, last,
                field is not None, *refs
            ),
            out_shape=tuple(out_shape),
            in_specs=in_specs,
            out_specs=tuple(out_specs),
            scratch_shapes=[
                pltpu.VMEM((2, padded_rows(ranges, conv_rows), lon_wide, LANES), F32),
                pltpu.VMEM((2, count * points, lon_wide, LANES), F32),
                pltpu.VMEM((conv_rows, lon_pad, CP), F32),
                pltpu.SemaphoreType.DMA(()),
                pltpu.SemaphoreType.DMA((count,)),
                pltpu.VMEM(own.shape if last else (8, LANES), BF16),
            ],
            input_output_aliases={} if field is None else {len(operands) - 1: 0},
            compiler_params=compiler_params,
            cost_estimate=cost(1.1 * count),
            name="field",
        )(*operands)
        return (None if last else results[-1]), (results[0] if out_shape[0] is not own else None)

    early = (2 * inner[0][1] + 2) // 3
    for k, group in enumerate(groups[::-1]):
        if k > 2:
            values, piece = lax.optimization_barrier((values, piece))
        if k == min(1, len(groups) - 1):
            values, west, east = lax.optimization_barrier((values, west, east))
        part = values.shape[0] // (len(group) + 1)
        sent = [values[(i + 1) * part : (i + 2) * part].astype(BF16) for i in range(len(group))]
        if k == min(1, len(groups) - 1):

            def wide(at):
                return jnp.concatenate([west[at], gconv[at, :cols, :C], east[at]], axis=1)

            wides = (wide(slice(0, RAD)), wide(slice(rows - RAD, rows)))
        received = [swap(one, mask) for one, mask in zip(sent, group)]
        if k == min(1, len(groups) - 1):
            piece, _ = field_piece([(margin, early)], (), None, None, False)
        if k == min(2, len(groups) - 1):
            lat_halos = shift_both(*wides, "lat", False)
            piece, _ = lax.optimization_barrier((piece, values))
            at = margin * conv_rows
            late = [(margin + early, inner[0][1] - early)]
            piece, field = field_piece(late, (), (at, piece), None, False)
        values = values[:part].astype(F32)
        for other in received:
            values = values + other.astype(F32)
        if k == 1 and len(groups) > 2:
            values, wides = lax.optimization_barrier((values, wides))
    at = (margin + early) * conv_rows
    _, field = field_piece(outer, lat_halos, (at, piece), field, True)
    summed = lax.dynamic_slice(values.reshape(-1), (offset,), (length,))
    new_params = params - STEP_SIZE * summed + NOISE_COEF * langevin_noise
    return (output, field, new_params)


def solution(mesh):
    return jax.shard_map(
        body,
        mesh=mesh,
        in_specs=(
            P("lat", "lon", None),
            P(("lon", "lat")),
            P(("lon", "lat")),
            P("lat", "lon", None),
        ),
        out_specs=(P("lat", "lon", None), P("lat", "lon", None), P(("lon", "lat"))),
        check_vma=False,
    )
```
